256 devices in a mesh: tmpl: 32 (over z, x), chan: 8 (over y, core).
Axes of the slice: x: 4, y: 4, z: 8, core: 2. Of those that a mesh axis runs over, the one named last changes fastest.
Arguments:
- records: bfloat16 [1024, 98304], P('chan', 'tmpl'), may hold values from -60 to 60
- waveforms: bfloat16 [1024, 32, 512], P('tmpl'), may hold values from -1 to 1
- slot_channels: int32 [1024, 32], P('tmpl'), may hold values from 0 to 1023, as said below
- slot_counts: int32 [1024], P('tmpl'), may hold values from 8 to 32, as said below
- slot_lags: int32 [1024, 32], P('tmpl'), may hold values from 0 to 511
Outputs:
- detections: float32 [1024, 98304], P('tmpl', 'chan')
The draws below stay inside these ranges and needn't reach their ends.
Inputs may be any that keep to these rules, and one draw needn't show every extreme that they name: `slot_channels`: the 32 channels of one template are distinct. `slot_counts`: some template uses all 32 slots.
All inputs are finite; a program needn't handle non-finite values.
Results may differ from the reference program's by a relative error of at most 0.013.
Values may be sent and summed in bfloat16 or wider, within the bound.
No kernel may reach another device: no remote copies, remote signals or barrier semaphores. Data moves between devices by JAX's collectives and lax.ppermute only.
A program may use at most 128 MiB of HBM per device.

```python
import math
import jax
import jax.numpy as jnp
from jax import lax

CHANNELS = 1024
NFFT = 4096
BAND = 1024
TLEN = 512
LAG_MAX = 512
K_MAX = 32
TMPL_DEV = 32
HOP = 3072
TIME = 98304
TEMPLATES = 1024


def draw_records(key, part):
    key = jax.random.fold_in(key, 11)
    key_samples, key_scale = jax.random.split(key)
    samples = jnp.clip(jax.random.normal(key_samples, (CHANNELS, TIME), jnp.float32), -6.0, 6.0)
    growth = 0.5
    position = jnp.arange(TIME, dtype=jnp.float32) / TIME
    envelope = jnp.power(10.0, growth * position)
    channel_scale = jnp.power(10.0, 0.5 * jax.random.uniform(key_scale, (CHANNELS, 1), jnp.float32))
    return (samples * envelope[None, :] * channel_scale).astype(jnp.bfloat16)


def draw_waveforms(key, part):
    key = jax.random.fold_in(key, 17)
    key_shape, key_scale = jax.random.split(key)
    samples = jnp.clip(jax.random.normal(key_shape, (TEMPLATES, K_MAX, TLEN), jnp.float32), -6.0, 6.0)
    slot_scale = jnp.power(10.0, jax.random.uniform(key_scale, (TEMPLATES, K_MAX, 1), jnp.float32))
    return jnp.clip(0.02 * samples * slot_scale, -1.0, 1.0).astype(jnp.bfloat16)


def draw_slot_channels(key, part):
    key = jax.random.fold_in(key, 23)
    template_keys = jax.random.split(key, TEMPLATES)

    def choose_channels(single_key):
        return jax.random.permutation(single_key, CHANNELS)[:K_MAX]
    return jax.vmap(choose_channels)(template_keys).astype(jnp.int32)


def draw_slot_counts(key, part):
    key = jax.random.fold_in(key, 37)
    key_top, key_each, key_full = jax.random.split(key, 3)
    group_total = TEMPLATES // TMPL_DEV
    group_top = jax.random.randint(key_top, (group_total,), K_MAX // 2, K_MAX + 1)
    upper_bound = jnp.repeat(group_top, TMPL_DEV) + 1
    counts_drawn = jax.random.randint(key_each, (TEMPLATES,), K_MAX // 4, upper_bound)
    full_index = jax.random.randint(key_full, (), 0, TEMPLATES)
    positions = jnp.arange(TEMPLATES, dtype=jnp.int32)
    return jnp.where(positions == full_index, K_MAX, counts_drawn).astype(jnp.int32)


def plant(values, key, low, largest):
    spot = [jax.random.randint(jax.random.fold_in(key, axis), (), 0, length) for axis, length in enumerate(values.shape)]
    main_axis = values.shape.index(max(values.shape))
    beside = spot[:main_axis] + [(spot[main_axis] + 1) % values.shape[main_axis]] + spot[main_axis + 1:]
    return values.at[tuple(spot)].set(low).at[tuple(beside)].set(largest)


def setup_inputs(seed: int = 0) -> dict:
    streams_of = jax.random.split(jax.random.key(seed), 6)
    return {
        "records": draw_records(jax.random.fold_in(streams_of[5], 71), 0),
        "waveforms": draw_waveforms(jax.random.fold_in(streams_of[5], 71), 0),
        "slot_channels": draw_slot_channels(jax.random.fold_in(streams_of[5], 71), 0),
        "slot_counts": draw_slot_counts(jax.random.fold_in(streams_of[5], 71), 0),
        "slot_lags": plant(jax.random.randint(streams_of[4], (TEMPLATES, K_MAX), 0, LAG_MAX), jax.random.fold_in(streams_of[4], 1), 0, LAG_MAX - 1).astype(jnp.int32),
    }


def rounded(values):
    narrow = lax.optimization_barrier(values.astype(jnp.bfloat16))
    return narrow.astype(jnp.float32)

def reference(records, waveforms, slot_channels, slot_counts, slot_lags):
    channel_count = records.shape[0]
    block_count = records.shape[1] // HOP
    bin_index = jnp.arange(BAND, dtype=jnp.int32)
    spectrum = jnp.fft.rfft(waveforms.astype(jnp.float32), n=NFFT, axis=-1)[..., :BAND]
    phase_angle = jnp.mod(slot_lags[:, :, None] * bin_index[None, None, :], NFFT).astype(jnp.float32) * (2.0 * math.pi / NFFT)
    phase_cos = jnp.cos(phase_angle)
    phase_sin = jnp.sin(phase_angle)
    base_real = jnp.real(spectrum)
    base_imag = -jnp.imag(spectrum)
    live_slots = (jnp.arange(K_MAX, dtype=jnp.int32)[None, :] < slot_counts[:, None]).astype(jnp.float32)[:, :, None]
    bank_real = rounded(base_real * phase_cos - base_imag * phase_sin) * live_slots
    bank_imag = rounded(base_real * phase_sin + base_imag * phase_cos) * live_slots
    padded = jnp.concatenate([records.astype(jnp.float32), jnp.zeros((channel_count, NFFT - HOP), jnp.float32)], axis=1)
    pad_width = NFFT // 2 + 1 - BAND

    def one_block(block_index):
        window_data = lax.dynamic_slice_in_dim(padded, block_index * HOP, NFFT, 1)
        data_spectrum = jnp.fft.rfft(window_data, axis=-1)[:, :BAND]
        data_real = rounded(jnp.real(data_spectrum))
        data_imag = rounded(jnp.imag(data_spectrum))
        picked_real = data_real[slot_channels]
        picked_imag = data_imag[slot_channels]
        total_real = lax.optimization_barrier(jnp.sum(bank_real * picked_real - bank_imag * picked_imag, axis=1))
        total_imag = lax.optimization_barrier(jnp.sum(bank_real * picked_imag + bank_imag * picked_real, axis=1))
        full_real = jnp.pad(total_real, ((0, 0), (0, pad_width)))
        full_imag = jnp.pad(total_imag, ((0, 0), (0, pad_width)))
        return jnp.fft.irfft(lax.complex(full_real, full_imag), n=NFFT, axis=-1)[:, :HOP]
    traces = lax.map(one_block, jnp.arange(block_count, dtype=jnp.int32))
    template_count = traces.shape[1]
    traces = jnp.transpose(traces, (1, 0, 2)).reshape(template_count, block_count * HOP)
    energy = lax.optimization_barrier(jnp.mean(traces * traces, axis=1, keepdims=True))
    return traces * lax.rsqrt(energy + 1e-06)
```

```python
import math

import jax
import jax.numpy as jnp
import numpy as np
from jax import lax
from jax.experimental import pallas as pl
from jax.experimental.pallas import tpu as pltpu
from jax.sharding import Mesh
from jax.sharding import PartitionSpec as P

NFFT = 4096
BAND = 1024
HOP = 3072
SLOTS = 32
EPS = 1e-06
RADIX = 64
BINS = 8
SHARES = BAND // BINS
BF = jnp.bfloat16
F32 = jnp.float32


def halves(matrix):
    upper = matrix.astype(BF)
    lower = (matrix - upper.astype(np.float64)).astype(BF)
    return upper, lower


def share_bins():
    share = np.arange(SHARES)
    return 512 * (share % 2)[:, None] + 64 * np.arange(BINS)[None, :] + (share // 2)[:, None]


def forward_tables():
    a = np.arange(RADIX)
    angle = 2.0 * np.pi * ((a[:, None] * a[None, :]) % RADIX) / RADIX
    first = np.stack([np.cos(angle), -np.sin(angle)], axis=1).reshape(2 * RADIX, RADIX)
    bins = share_bins().reshape(RADIX, 2, BINS)
    angle = 2.0 * np.pi * ((bins[..., None] * a) % NFFT) / NFFT
    cosine, sine = np.cos(angle), np.sin(angle)
    real = np.stack([cosine, sine], axis=3)
    imag = np.stack([-sine, cosine], axis=3)
    second = np.stack([real, imag], axis=2).reshape(RADIX, 4 * BINS, 2 * RADIX)
    return first, second


def bank_table(samples):
    angle = 2.0 * np.pi * ((share_bins()[..., None] * np.arange(samples)) % NFFT) / NFFT
    return np.stack([np.cos(angle), np.sin(angle)], axis=1).reshape(2 * BAND, samples)


def inverse_table():
    bins = share_bins()
    angle = 2.0 * np.pi * ((bins[..., None] * np.arange(HOP)) % NFFT) / NFFT
    weight = np.where(bins == 0, 1.0, 2.0)[..., None] / NFFT
    table = np.stack([np.cos(angle) * weight, -np.sin(angle) * weight], axis=1)
    return table.reshape(2 * BAND, HOP)


def forward_spectra(framed):
    channels = framed.shape[0]
    first, second = forward_tables()
    first_both = np.concatenate(halves(first), axis=0)
    signal = framed.T.reshape(RADIX, RADIX * channels)
    mixed = jnp.dot(first_both, signal, preferred_element_type=F32)
    mixed = mixed[: 2 * RADIX] + mixed[2 * RADIX :]
    mixed = mixed.reshape(RADIX, 2 * RADIX, channels)
    mixed_upper = mixed.astype(BF)
    mixed_lower = (mixed - mixed_upper.astype(F32)).astype(BF)
    second_upper, second_lower = halves(second)
    left = np.concatenate([second_upper, second_lower, second_upper], axis=2)
    right = jnp.concatenate([mixed_upper, mixed_upper, mixed_lower], axis=1)
    spectra = jnp.einsum("kmq,kqc->kmc", left, right, preferred_element_type=F32)
    return spectra.astype(BF).reshape(SHARES, 2 * BINS, channels)


def bank_spectra(waveforms, lags, live):
    rows, samples = waveforms.shape
    table = np.concatenate(halves(bank_table(samples)), axis=1)
    both = jnp.concatenate([waveforms, waveforms], axis=1)
    base = jnp.einsum("km,rm->kr", table, both, preferred_element_type=F32)
    base = base.reshape(RADIX, 2, 2, BINS, rows)
    turn = 2.0 * math.pi / NFFT
    fine = jnp.mod(jnp.arange(RADIX, dtype=jnp.int32)[:, None] * lags[None], NFFT)
    fine = fine.astype(F32) * turn
    step = jnp.mod(RADIX * jnp.arange(2 * BINS, dtype=jnp.int32)[:, None] * lags[None], NFFT)
    step = step.astype(F32) * turn
    fine_cos, fine_sin = (f(fine)[:, None, None, :] for f in (jnp.cos, jnp.sin))
    step_cos, step_sin = (f(step).reshape(1, 2, BINS, rows) for f in (jnp.cos, jnp.sin))
    cosine = fine_cos * step_cos - fine_sin * step_sin
    sine = fine_sin * step_cos + fine_cos * step_sin
    base_real, base_imag = base[:, :, 0], base[:, :, 1]
    real = base_real * cosine - base_imag * sine
    imag = base_real * sine + base_imag * cosine
    bank = jnp.stack([real, imag], axis=2)
    bank = jnp.where(live, bank, 0.0).astype(BF)
    return bank.reshape(SHARES, 2 * BINS, rows)


def swap_blocks(parts, lane):
    count = len(parts)
    size = 128 // count
    step = count // 2
    while step:
        low = (lane // (size * step)) % 2 == 0
        fresh = list(parts)
        for i in range(count):
            if i & step:
                continue
            j = i + step
            fresh[i] = jnp.where(low, parts[i], pltpu.roll(parts[j], size * step, 1))
            fresh[j] = jnp.where(low, pltpu.roll(parts[i], 128 - size * step, 1), parts[j])
        parts = fresh
        step //= 2
    return parts


def correlate_kernel(place, chunks, own, other, spread, out, table, weights, sums):
    blocks = 32
    for half, source in enumerate((own, other)):
        for y in range(4):
            for s in range(4):
                tiles = [source[(8 * s + i) * 4 + y, 0:16, :] for i in range(8)]
                block = jnp.concatenate(tiles, axis=0).astype(F32)
                start = half * 512 + y * 128
                table[start : start + 128, s, :] = block.T

    def expand(q, carry):
        tile = own[q, 16:32, :].astype(F32).T.astype(BF)
        weights[pl.ds(q * 128, 128), :] = jnp.dot(tile, spread[...], preferred_element_type=F32)
        return carry

    lax.fori_loop(0, SHARES, expand, 0, unroll=4)

    def one_template(t, carry):
        zero = jnp.zeros((4, 128), F32)

        def one_chunk(step, totals):
            first, second = totals
            base = t * SLOTS + step * 8
            for u in range(8):
                row = table[place[base + u]]
                both = weights[pl.ds(base + u, 1), :]
                first = first + row * both[:, :128]
                second = second + row * both[:, 128:]
            return first, second

        first, second = lax.fori_loop(0, chunks[t], one_chunk, (zero, zero))
        sums[t, 0:4, :] = first
        sums[t, 4:8, :] = second
        return carry

    lax.fori_loop(0, 512, one_template, 0)

    lane = lax.broadcasted_iota(jnp.int32, (128, 128), 1)
    is_real = (lane // BINS) % 2 == 0
    for g in range(blocks // 8):
        for y in range(4):
            first = sums[g * 128 : (g + 1) * 128, y, :]
            second = sums[g * 128 : (g + 1) * 128, 4 + y, :]
            crossed = jnp.where(
                is_real, -pltpu.roll(second, 128 - BINS, 1), pltpu.roll(second, BINS, 1)
            )
            turned = (first + crossed).T
            parts = [turned[16 * i : 16 * (i + 1)] for i in range(8)]
            for i, part in enumerate(swap_blocks(parts, lane[:16])):
                out[(8 * g + i) * 4 + y] = part.astype(BF)


def spread_table():
    lane = np.arange(128)
    table = np.zeros((2, BINS, 2, 128))
    for part in range(2):
        table[part, lane % BINS, part, lane] = 1.0
    return table.reshape(2 * BINS, 256).astype(BF)


def correlate(place, chunks, own, other):
    vmem = pl.BlockSpec(memory_space=pltpu.VMEM)
    smem = pl.BlockSpec(memory_space=pltpu.SMEM)
    return pl.pallas_call(
        correlate_kernel,
        out_shape=jax.ShapeDtypeStruct((SHARES, 16, 128), BF),
        in_specs=[smem, smem, vmem, vmem, vmem],
        out_specs=vmem,
        scratch_shapes=[
            pltpu.VMEM((1024, 4, 128), F32),
            pltpu.VMEM((512 * SLOTS, 256), F32),
            pltpu.VMEM((512, 8, 128), F32),
        ],
        compiler_params=pltpu.CompilerParams(vmem_limit_bytes=50 * 2**20),
    )(place, chunks, own, other, jnp.asarray(spread_table()))


def on_device(records, waveforms, slot_channels, slot_counts, slot_lags):
    core = lax.axis_index("c")
    quarter = lax.axis_index("y")
    following = lax.ppermute(records[:, : NFFT - HOP], ("z", "x"), [(i, i - 1) for i in range(1, 32)])

    half_channels = lax.dynamic_slice_in_dim(slot_channels, core * 16, 16, 0)
    half_counts = lax.dynamic_slice_in_dim(slot_counts, core * 16, 16, 0)
    home = half_channels // 128
    place = ((home % 2) ^ core) * 512 + (home // 2) * 128 + half_channels % 128
    slots = jnp.concatenate([place.reshape(4, 128), jnp.pad((half_counts + 7) // 8, (0, 112))[None]])
    slots = lax.all_gather(slots, ("z", "x"), axis=0)
    places = slots[:, :4].reshape(512 * SLOTS)
    chunks = slots[:, 4, :16].reshape(512)

    first = core * 16 + quarter * 4
    waves = lax.dynamic_slice_in_dim(waveforms, first, 4, 0).reshape(128, -1)
    lags = lax.dynamic_slice_in_dim(slot_lags, first, 4, 0).reshape(128)
    counts = lax.dynamic_slice_in_dim(slot_counts, first, 4, 0)
    live = (jnp.arange(SLOTS, dtype=jnp.int32)[None] < counts[:, None]).reshape(128)
    bank = bank_spectra(waves, lags, live)

    spectra = forward_spectra(jnp.concatenate([records, following], axis=1))
    shares = jnp.concatenate([spectra, bank], axis=1)
    own = lax.all_to_all(shares, ("z", "x", "y"), split_axis=0, concat_axis=0, tiled=True)
    other = lax.ppermute(own[:, :16], "c", [(0, 1), (1, 0)])
    correlated = correlate(places, chunks, own, other)
    here = lax.all_to_all(correlated, ("z", "x", "y"), split_axis=0, concat_axis=0, tiled=True)
    here = here.reshape(2 * BAND, 128)
    mine = lax.dynamic_slice_in_dim(here, core * 64, 64, 1)
    given = lax.dynamic_slice_in_dim(here, (1 - core) * 64, 64, 1)
    taken = lax.ppermute(given, "c", [(0, 1), (1, 0)])
    spectral = jnp.concatenate([mine, taken], axis=1)
    traces = jnp.einsum(
        "kr,kn->rn", spectral, inverse_table().astype(BF), preferred_element_type=F32
    )
    traces = traces.reshape(2, 4, 16, HOP)
    energy = jnp.sum(traces * traces, axis=(1, 3))
    energy = jnp.where(core == 0, energy, energy[::-1])
    energy = lax.psum(energy, ("y", "c"))
    scale = lax.rsqrt(energy / (32 * HOP) + EPS)
    traces = jnp.where(core == 0, traces, traces[::-1])
    detections = jnp.transpose(traces, (0, 2, 1, 3)).reshape(32, 4 * HOP)
    return detections * scale.reshape(32, 1)


def solution(mesh):
    fine = Mesh(mesh.devices.reshape(8, 4, 4, 2), ("z", "x", "y", "c"))
    tmpl, chan = ("z", "x"), ("y", "c")
    in_specs = (P(chan, tmpl), P(tmpl, None, None), P(tmpl, None), P(tmpl), P(tmpl, None))
    return jax.shard_map(
        on_device, mesh=fine, in_specs=in_specs, out_specs=P(tmpl, chan), check_vma=False
    )
```

```python
import math

import jax
import jax.numpy as jnp
import numpy as np
from jax import lax
from jax.experimental import pallas as pl
from jax.experimental.pallas import tpu as pltpu
from jax.sharding import Mesh
from jax.sharding import PartitionSpec as P

NFFT = 4096
BAND = 1024
HOP = 3072
SLOTS = 32
EPS = 1e-06
RADIX = 64
BINS = 8
SHARES = BAND // BINS
UNROLL = 8
BF = jnp.bfloat16
F32 = jnp.float32


def halves(matrix):
    upper = matrix.astype(BF)
    lower = (matrix - upper.astype(np.float64)).astype(BF)
    return upper, lower


def share_bins():
    share = np.arange(SHARES)
    return 512 * (share % 2)[:, None] + 64 * np.arange(BINS)[None, :] + (share // 2)[:, None]


def forward_tables():
    a = np.arange(RADIX)
    angle = 2.0 * np.pi * ((a[:, None] * a[None, :]) % RADIX) / RADIX
    first = np.stack([np.cos(angle), -np.sin(angle)], axis=1).reshape(2 * RADIX, RADIX)
    bins = share_bins().reshape(RADIX, 2, BINS)
    angle = 2.0 * np.pi * ((bins[..., None] * a) % NFFT) / NFFT
    cosine, sine = np.cos(angle), np.sin(angle)
    real = np.stack([cosine, sine], axis=3)
    imag = np.stack([-sine, cosine], axis=3)
    second = np.stack([real, imag], axis=2).reshape(RADIX, 4 * BINS, 2 * RADIX)
    return first, second


def bank_table(samples):
    angle = 2.0 * np.pi * ((share_bins()[..., None] * np.arange(samples)) % NFFT) / NFFT
    return np.stack([np.cos(angle), np.sin(angle)], axis=1).reshape(2 * BAND, samples)


def inverse_table():
    bins = share_bins()
    angle = 2.0 * np.pi * ((bins[..., None] * np.arange(HOP)) % NFFT) / NFFT
    weight = np.where(bins == 0, 1.0, 2.0)[..., None] / NFFT
    table = np.stack([np.cos(angle) * weight, -np.sin(angle) * weight], axis=1)
    return table.reshape(2 * BAND, HOP)


def forward_spectra(framed):
    channels = framed.shape[0]
    first, second = forward_tables()
    first_both = np.concatenate(halves(first), axis=0)
    signal = framed.T.reshape(RADIX, RADIX * channels)
    mixed = jnp.dot(first_both, signal, preferred_element_type=F32)
    mixed = mixed[: 2 * RADIX] + mixed[2 * RADIX :]
    mixed = mixed.reshape(RADIX, 2 * RADIX, channels)
    mixed_upper = mixed.astype(BF)
    mixed_lower = (mixed - mixed_upper.astype(F32)).astype(BF)
    second_upper, second_lower = halves(second)
    left = np.concatenate([second_upper, second_lower, second_upper], axis=2)
    right = jnp.concatenate([mixed_upper, mixed_upper, mixed_lower], axis=1)
    spectra = jnp.einsum("kmq,kqc->kmc", left, right, preferred_element_type=F32)
    return spectra.astype(BF).reshape(SHARES, 2 * BINS, channels)


def bank_spectra(waveforms, lags, live):
    rows, samples = waveforms.shape
    table = np.concatenate(halves(bank_table(samples)), axis=1)
    both = jnp.concatenate([waveforms, waveforms], axis=1)
    base = jnp.einsum("km,rm->kr", table, both, preferred_element_type=F32)
    base = base.reshape(RADIX, 2, 2, BINS, rows)
    turn = 2.0 * math.pi / NFFT
    fine = jnp.mod(jnp.arange(RADIX, dtype=jnp.int32)[:, None] * lags[None], NFFT)
    fine = fine.astype(F32) * turn
    step = jnp.mod(RADIX * jnp.arange(2 * BINS, dtype=jnp.int32)[:, None] * lags[None], NFFT)
    step = step.astype(F32) * turn
    fine_cos, fine_sin = (f(fine)[:, None, None, :] for f in (jnp.cos, jnp.sin))
    step_cos, step_sin = (f(step).reshape(1, 2, BINS, rows) for f in (jnp.cos, jnp.sin))
    cosine = fine_cos * step_cos - fine_sin * step_sin
    sine = fine_sin * step_cos + fine_cos * step_sin
    base_real, base_imag = base[:, :, 0], base[:, :, 1]
    real = base_real * cosine - base_imag * sine
    imag = base_real * sine + base_imag * cosine
    bank = jnp.stack([real, imag], axis=2)
    bank = jnp.where(live, bank, 0.0).astype(BF)
    return bank.reshape(SHARES, 2 * BINS, rows)


def swap_blocks(parts, lane):
    count = len(parts)
    size = 128 // count
    step = count // 2
    while step:
        low = (lane // (size * step)) % 2 == 0
        fresh = list(parts)
        for i in range(count):
            if i & step:
                continue
            j = i + step
            fresh[i] = jnp.where(low, parts[i], pltpu.roll(parts[j], size * step, 1))
            fresh[j] = jnp.where(low, pltpu.roll(parts[i], 128 - size * step, 1), parts[j])
        parts = fresh
        step //= 2
    return parts


def correlate_kernel(place, chunks, own, other, bank, spread, unit, out, table, weights, sums, live):
    rotated = (((1,), (1,)), ((), ()))
    eye = unit[...]

    def turned(block):
        return lax.dot_general(eye, block, rotated, preferred_element_type=F32)

    for half, source in enumerate((own, other)):
        for y in range(4):
            start = half * 512 + y * 128
            for s in range(4):
                tiles = [source[(8 * s + i) * 4 + y] for i in range(8)]
                table[start : start + 128, s, :] = turned(jnp.concatenate(tiles, axis=0))
                wide = [tile.astype(F32) for tile in tiles]
                swapped = [part for tile in wide for part in (tile[8:], tile[:8])]
                block = jnp.concatenate(swapped, axis=0).astype(BF)
                table[start : start + 128, 4 + s, :] = turned(block)

    def expand(g, position):
        block = jnp.concatenate([bank[g * 8 + i, 0:16, :] for i in range(8)], axis=0)
        compact = turned(block).astype(BF)
        for i in range(4):
            wide = jnp.dot(compact, spread[i], preferred_element_type=F32)
            for j in range(2):
                first = (g * 8 + 2 * i + j) * 16
                part = wide[:, 128 * j : 128 * (j + 1)]
                weights[pl.ds(first, 16)] = part.reshape(16, 8, 128)
        for i in range(32):
            t = g * 32 + i
            for s in range(4):
                live[position + s] = t * 4 + s
            position = position + chunks[t]
        return position

    count = lax.fori_loop(0, 16, expand, 0)
    for s in range(UNROLL):
        live[count + s] = 2048
    weights[2048] = jnp.zeros((8, 128), F32)
    sums[...] = jnp.zeros_like(sums)

    def some_chunks(step, carry):
        for i in range(UNROLL):
            chunk = live[step * UNROLL + i]
            tile = weights[chunk]
            totals = [None, None]
            for u in range(8):
                row = table_rows(table, place[chunk * 8 + u])
                term = row * tile[u : u + 1]
                totals[u % 2] = term if u < 2 else totals[u % 2] + term
            t = lax.shift_right_logical(chunk, 2)
            sums[t] = sums[t] + (totals[0] + totals[1])
        return carry

    lax.fori_loop(0, lax.div(count + UNROLL - 1, UNROLL), some_chunks, 0)

    lane = lax.broadcasted_iota(jnp.int32, (128, 128), 1)
    is_real = (lane // BINS) % 2 == 0
    for g in range(4):
        for y in range(4):
            first = sums[g * 128 : (g + 1) * 128, y, :]
            second = sums[g * 128 : (g + 1) * 128, 4 + y, :]
            real = first - pltpu.roll(first, 128 - BINS, 1)
            imag = second + pltpu.roll(second, BINS, 1)
            total = turned(jnp.where(is_real, real, imag).astype(BF))
            parts = [total[16 * i : 16 * (i + 1)] for i in range(8)]
            for i, part in enumerate(swap_blocks(parts, lane[:16])):
                out[(8 * g + i) * 4 + y] = part.astype(BF)


def table_rows(table, first):
    rows = table.reshape(8192, 128)
    return rows[pl.ds(pl.multiple_of(first, 8), 8)]


def spread_table():
    lane = np.arange(128)
    one = np.zeros((2, BINS, 128))
    for part in range(2):
        one[part, lane % BINS, lane] = (lane // BINS) % 2 == part
    one = one.reshape(2 * BINS, 128)
    table = np.zeros((4, 8, 2 * BINS, 2, 128))
    for share in range(8):
        table[share // 2, share, :, share % 2] = one
    return table.reshape(4, 128, 256).astype(BF)


def correlate(place, chunks, own, other, bank):
    vmem = pl.BlockSpec(memory_space=pltpu.VMEM)
    smem = pl.BlockSpec(memory_space=pltpu.SMEM)
    return pl.pallas_call(
        correlate_kernel,
        out_shape=jax.ShapeDtypeStruct((SHARES, 16, 128), BF),
        in_specs=[smem, smem, vmem, vmem, vmem, vmem, vmem],
        out_specs=vmem,
        scratch_shapes=[
            pltpu.VMEM((1024, 8, 128), F32),
            pltpu.VMEM((2049, 8, 128), F32),
            pltpu.VMEM((513, 8, 128), F32),
            pltpu.SMEM((2048 + 2 * UNROLL,), jnp.int32),
        ],
        compiler_params=pltpu.CompilerParams(vmem_limit_bytes=40 * 2**20),
    )(place, chunks, own, other, bank, jnp.asarray(spread_table()), jnp.eye(128, dtype=BF))


def on_device(records, waveforms, slot_channels, slot_counts, slot_lags):
    core = lax.axis_index("c")
    quarter = lax.axis_index("y")
    following = lax.ppermute(records[:, : NFFT - HOP], ("z", "x"), [(i, i - 1) for i in range(1, 32)])

    first = core * 16 + quarter * 4
    waves = lax.dynamic_slice_in_dim(waveforms, first, 4, 0).reshape(128, -1)
    lags = lax.dynamic_slice_in_dim(slot_lags, first, 4, 0).reshape(128)
    counts = lax.dynamic_slice_in_dim(slot_counts, first, 4, 0)
    channels = lax.dynamic_slice_in_dim(slot_channels, first, 4, 0).reshape(128)
    live = (jnp.arange(SLOTS, dtype=jnp.int32)[None] < counts[:, None]).reshape(128)
    bank = bank_spectra(waves, lags, live)
    digits = jnp.stack([channels // 32, channels % 32, jnp.repeat(counts, SLOTS)])
    digits = jnp.pad(digits, ((0, 5), (0, 0))).astype(BF)
    bank = jnp.concatenate([bank, jnp.broadcast_to(digits, (SHARES, 8, 128))], axis=1)
    bank = lax.all_to_all(bank, ("z", "x", "y"), split_axis=0, concat_axis=0, tiled=True)
    channels = bank[:, 16].astype(jnp.int32) * 32 + bank[:, 17].astype(jnp.int32)
    home = channels // 128
    place = ((home % 2) ^ core) * 512 + (home // 2) * 128 + channels % 128
    place = jnp.pad(8 * place.reshape(512 * SLOTS), (0, 128))
    chunks = (bank[:, 18].astype(jnp.int32).reshape(512, SLOTS)[:, 0] + 7) // 8

    spectra = forward_spectra(jnp.concatenate([records, following], axis=1))
    own = lax.all_to_all(spectra, ("z", "x", "y"), split_axis=0, concat_axis=0, tiled=True)
    other = lax.ppermute(own, "c", [(0, 1), (1, 0)])
    correlated = correlate(place, chunks, own, other, bank)
    here = lax.all_to_all(correlated, ("z", "x", "y"), split_axis=0, concat_axis=0, tiled=True)
    here = here.reshape(2 * BAND, 128)
    mine = lax.dynamic_slice_in_dim(here, core * 64, 64, 1)
    given = lax.dynamic_slice_in_dim(here, (1 - core) * 64, 64, 1)
    taken = lax.ppermute(given, "c", [(0, 1), (1, 0)])
    spectral = jnp.concatenate([mine, taken], axis=1)
    traces = jnp.einsum(
        "kr,kn->rn", spectral, inverse_table().astype(BF), preferred_element_type=F32
    )
    traces = traces.reshape(2, 4, 16, HOP)
    energy = jnp.sum(traces * traces, axis=(1, 3))
    energy = jnp.where(core == 0, energy, energy[::-1])
    energy = energy + lax.ppermute(energy, "c", [(0, 1), (1, 0)])
    shifts = [[(i, (i + d) % 4) for i in range(4)] for d in range(1, 4)]
    energy = sum((lax.ppermute(energy, "y", shift) for shift in shifts), energy)
    scale = lax.rsqrt(energy / (32 * HOP) + EPS)
    traces = jnp.where(core == 0, traces, traces[::-1])
    detections = jnp.transpose(traces, (0, 2, 1, 3)).reshape(32, 4 * HOP)
    return detections * scale.reshape(32, 1)


def solution(mesh):
    fine = Mesh(mesh.devices.reshape(8, 4, 4, 2), ("z", "x", "y", "c"))
    tmpl, chan = ("z", "x"), ("y", "c")
    in_specs = (P(chan, tmpl), P(tmpl, None, None), P(tmpl, None), P(tmpl), P(tmpl, None))
    return jax.shard_map(
        on_device, mesh=fine, in_specs=in_specs, out_specs=P(tmpl, chan), check_vma=False
    )
```

```python
import functools
import math

import jax
import jax.numpy as jnp
import numpy as np
from jax import lax
from jax.experimental import pallas as pl
from jax.experimental.pallas import tpu as pltpu
from jax.sharding import Mesh
from jax.sharding import PartitionSpec as P

NFFT = 4096
BAND = 1024
HOP = 3072
SLOTS = 32
EPS = 1e-06
RADIX = 64
BINS = 8
SHARES = BAND // BINS
UNROLL = 8
BF = jnp.bfloat16
F32 = jnp.float32


def halves(matrix):
    upper = matrix.astype(BF)
    lower = (matrix - upper.astype(np.float64)).astype(BF)
    return upper, lower


def residues():
    place = np.arange(RADIX)
    return 4 * (place % 16) + place // 16


def share_bins():
    share = np.arange(SHARES)
    low = residues()[share // 2]
    return 512 * (share % 2)[:, None] + 64 * np.arange(BINS)[None, :] + low[:, None]


def forward_tables():
    a = np.arange(RADIX)
    angle = 2.0 * np.pi * ((residues()[:, None] * a[None, :]) % RADIX) / RADIX
    first = np.stack([np.cos(angle), -np.sin(angle)], axis=1).reshape(2 * RADIX, RADIX)
    bins = share_bins().reshape(RADIX, 2, BINS)
    angle = 2.0 * np.pi * ((bins[..., None] * a) % NFFT) / NFFT
    cosine, sine = np.cos(angle), np.sin(angle)
    real = np.stack([cosine, sine], axis=3)
    imag = np.stack([-sine, cosine], axis=3)
    second = np.stack([real, imag], axis=2).reshape(RADIX, 4 * BINS, 2 * RADIX)
    return first, second


def bank_table(samples):
    angle = 2.0 * np.pi * ((share_bins()[..., None] * np.arange(samples)) % NFFT) / NFFT
    return np.stack([np.cos(angle), np.sin(angle)], axis=1).reshape(2 * BAND, samples)


def inverse_tables():
    bins = share_bins()
    angle = 2.0 * np.pi * ((bins[..., None] * np.arange(HOP // 3)) % NFFT) / NFFT
    weight = np.where(bins == 0, 1.0, 2.0)[..., None] / NFFT
    real = np.stack([np.cos(angle) * weight, -np.sin(angle) * weight], axis=1)
    imag = np.stack([np.sin(angle) * weight, np.cos(angle) * weight], axis=1)
    real, imag = (table.reshape(4, 512, HOP // 3) for table in (real, imag))
    even = np.stack([real[0], real[2]])
    odd = np.stack([np.concatenate([real[1], real[3]]), np.concatenate([-imag[1], imag[3]])])
    return even.astype(BF), odd.astype(BF)


def inverse_kernel(mine, other, choice, even, odd, traces, energy, left):
    pick = choice[...]
    for i in range(16):
        rows = slice(8 * i, 8 * i + 8)
        block = jnp.concatenate([q[rows].reshape(128, 128) for q in (mine, other)], axis=1)
        chosen = lax.dot_general(pick, block, ROTATED, preferred_element_type=F32)
        left[:, 128 * i : 128 * i + 128] = chosen.astype(BF)
    width = 256
    squares = jnp.zeros((128, width), F32)
    for start in range(0, HOP // 3, width):
        columns = slice(start, start + width)
        dot = functools.partial(jnp.dot, preferred_element_type=F32)
        first = dot(left[:, 0:512], even[0, :, columns])
        second = dot(left[:, 1024:1536], even[1, :, columns])
        turn = []
        for part in range(2):
            low = dot(left[:, 512:1024], odd[part, 0:512, columns])
            turn.append(low + dot(left[:, 1536:2048], odd[part, 512:1024, columns]))
        both = first + second
        for quarter, value in enumerate((both + turn[0], first - second + turn[1], both - turn[0])):
            squares = squares + value * value
            for block in range(4):
                begin = block * HOP + quarter * (HOP // 3) + start
                traces[:, begin : begin + width] = value[32 * block : 32 * block + 32]
    total = squares[:, :128] + squares[:, 128:]
    energy[...] = total[0:32] + total[32:64] + total[64:96] + total[96:128]


def inverse_traces(mine, other, core):
    row = jnp.arange(128)[:, None]
    lane = jnp.arange(256)[None, :]
    block, half, template = row // 32, (row // 16) % 2, row % 16
    choice = lane == 128 * (half ^ core) + 64 * core + 16 * block + template
    even, odd = inverse_tables()
    vmem = pl.BlockSpec(memory_space=pltpu.VMEM)
    return pl.pallas_call(
        inverse_kernel,
        out_shape=(
            jax.ShapeDtypeStruct((32, 4 * HOP), F32),
            jax.ShapeDtypeStruct((32, 128), F32),
        ),
        in_specs=[vmem] * 5,
        out_specs=(vmem, vmem),
        scratch_shapes=[pltpu.VMEM((128, 2 * BAND), BF)],
        compiler_params=pltpu.CompilerParams(vmem_limit_bytes=24 * 2**20),
    )(mine, other, choice.astype(BF), jnp.asarray(even), jnp.asarray(odd))


ROTATED = (((1,), (1,)), ((), ()))


def forward_kernel(records, following, first, second, unit, out, samples, mixed):
    eye = unit[...]
    for i in range(NFFT // 128):
        source = records if i < HOP // 128 else following
        start = 128 * i if i < HOP // 128 else 128 * i - HOP
        block = source[:, start : start + 128]
        turned = lax.dot_general(eye, block, ROTATED, preferred_element_type=F32)
        samples[2 * i : 2 * i + 2] = turned.reshape(2, RADIX, 128)

    def mix(b, carry):
        signal = samples[:, b, :].astype(BF)
        both = jnp.concatenate([signal, signal], axis=0)
        mixed[:, b, :] = jnp.dot(first[...], both, preferred_element_type=F32)
        return carry

    lax.fori_loop(0, RADIX, mix, 0, unroll=8)

    def finish(i, carry):
        values = mixed[pl.ds(2 * i, 2)].reshape(2 * RADIX, 128)
        upper = values.astype(BF)
        lower = (values - upper.astype(F32)).astype(BF)
        right = jnp.concatenate([upper, upper, lower], axis=0)
        total = jnp.dot(second[i], right, preferred_element_type=F32).astype(BF)
        out[pl.ds(2 * i, 2)] = total.reshape(2, 2 * BINS, 128)
        return carry

    lax.fori_loop(0, RADIX, finish, 0, unroll=8)


def forward_spectra(records, following):
    first, second = forward_tables()
    first = np.concatenate(halves(first), axis=1)
    upper, lower = halves(second)
    second = np.concatenate([upper, lower, upper], axis=2)
    vmem = pl.BlockSpec(memory_space=pltpu.VMEM)
    return pl.pallas_call(
        forward_kernel,
        out_shape=jax.ShapeDtypeStruct((SHARES, 2 * BINS, 128), BF),
        in_specs=[vmem] * 5,
        out_specs=vmem,
        scratch_shapes=[
            pltpu.VMEM((RADIX, RADIX, 128), F32),
            pltpu.VMEM((2 * RADIX, RADIX, 128), F32),
        ],
        compiler_params=pltpu.CompilerParams(vmem_limit_bytes=24 * 2**20),
    )(records, following, jnp.asarray(first), jnp.asarray(second), jnp.eye(128, dtype=BF))


def bank_spectra(waveforms, lags, live):
    rows, samples = waveforms.shape
    table = np.concatenate(halves(bank_table(samples)), axis=1)
    both = jnp.concatenate([waveforms, waveforms], axis=1)
    base = jnp.einsum("km,rm->kr", table, both, preferred_element_type=F32)
    base = base.reshape(RADIX, 2, 2, BINS, rows)
    turn = 2.0 * math.pi / NFFT
    fine = jnp.mod(residues().astype(np.int32)[:, None] * lags[None], NFFT)
    fine = fine.astype(F32) * turn
    step = jnp.mod(RADIX * jnp.arange(2 * BINS, dtype=jnp.int32)[:, None] * lags[None], NFFT)
    step = step.astype(F32) * turn
    fine_cos, fine_sin = (f(fine)[:, None, None, :] for f in (jnp.cos, jnp.sin))
    step_cos, step_sin = (f(step).reshape(1, 2, BINS, rows) for f in (jnp.cos, jnp.sin))
    cosine = fine_cos * step_cos - fine_sin * step_sin
    sine = fine_sin * step_cos + fine_cos * step_sin
    base_real, base_imag = base[:, :, 0], base[:, :, 1]
    real = base_real * cosine - base_imag * sine
    imag = base_real * sine + base_imag * cosine
    bank = jnp.stack([real, imag], axis=2)
    bank = jnp.where(live, bank, 0.0).astype(BF)
    return bank.reshape(SHARES, 2 * BINS, rows)


def swap_blocks(parts, lane):
    count = len(parts)
    size = 128 // count
    step = count // 2
    while step:
        low = (lane // (size * step)) % 2 == 0
        fresh = list(parts)
        for i in range(count):
            if i & step:
                continue
            j = i + step
            fresh[i] = jnp.where(low, parts[i], pltpu.roll(parts[j], size * step, 1))
            fresh[j] = jnp.where(low, pltpu.roll(parts[i], 128 - size * step, 1), parts[j])
        parts = fresh
        step //= 2
    return parts


def correlate_kernel(place, chunks, own, other, spread, unit, out, table, weights, sums, live):
    eye = unit[...]

    def turned(block):
        return lax.dot_general(eye, block, ROTATED, preferred_element_type=F32)

    for half, source in enumerate((own, other)):
        for y in range(4):
            start = half * 512 + y * 128
            for s in range(4):
                tiles = [source[(8 * s + i) * 4 + y, 0:16, :] for i in range(8)]
                table[start : start + 128, s, :] = turned(jnp.concatenate(tiles, axis=0))
                wide = [tile.astype(F32) for tile in tiles]
                swapped = [part for tile in wide for part in (tile[8:], tile[:8])]
                block = jnp.concatenate(swapped, axis=0).astype(BF)
                table[start : start + 128, 4 + s, :] = turned(block)

    def expand(g, position):
        block = jnp.concatenate([own[g * 8 + i, 16:32, :] for i in range(8)], axis=0)
        compact = turned(block).astype(BF)
        for i in range(4):
            wide = jnp.dot(compact, spread[i], preferred_element_type=F32)
            for j in range(2):
                first = (g * 8 + 2 * i + j) * 16
                part = wide[:, 128 * j : 128 * (j + 1)]
                weights[pl.ds(first, 16)] = part.reshape(16, 8, 128)
        for i in range(32):
            t = g * 32 + i
            for s in range(4):
                live[position + s] = t * 4 + s
            position = position + chunks[t]
        return position

    count = lax.fori_loop(0, 16, expand, 0)
    for s in range(UNROLL):
        live[count + s] = 2048
    weights[2048] = jnp.zeros((8, 128), F32)
    sums[...] = jnp.zeros_like(sums)

    def some_chunks(step, carry):
        for i in range(UNROLL):
            chunk = live[step * UNROLL + i]
            tile = weights[chunk]
            totals = [None, None]
            for u in range(8):
                row = table_rows(table, place[chunk * 8 + u])
                term = row * tile[u : u + 1]
                totals[u % 2] = term if u < 2 else totals[u % 2] + term
            t = lax.shift_right_logical(chunk, 2)
            sums[t] = sums[t] + (totals[0] + totals[1])
        return carry

    lax.fori_loop(0, lax.div(count + UNROLL - 1, UNROLL), some_chunks, 0)

    lane = lax.broadcasted_iota(jnp.int32, (128, 128), 1)
    is_real = (lane // BINS) % 2 == 0
    for g in range(4):
        for y in range(4):
            first = sums[g * 128 : (g + 1) * 128, y, :]
            second = sums[g * 128 : (g + 1) * 128, 4 + y, :]
            real = first - pltpu.roll(first, 128 - BINS, 1)
            imag = second + pltpu.roll(second, BINS, 1)
            total = turned(jnp.where(is_real, real, imag).astype(BF))
            parts = [total[16 * i : 16 * (i + 1)] for i in range(8)]
            for i, part in enumerate(swap_blocks(parts, lane[:16])):
                out[(8 * g + i) * 4 + y] = part.astype(BF)


def table_rows(table, first):
    rows = table.reshape(8192, 128)
    return rows[pl.ds(pl.multiple_of(first, 8), 8)]


def spread_table():
    lane = np.arange(128)
    one = np.zeros((2, BINS, 128))
    for part in range(2):
        one[part, lane % BINS, lane] = (lane // BINS) % 2 == part
    one = one.reshape(2 * BINS, 128)
    table = np.zeros((4, 8, 2 * BINS, 2, 128))
    for share in range(8):
        table[share // 2, share, :, share % 2] = one
    return table.reshape(4, 128, 256).astype(BF)


def correlate(place, chunks, own, other):
    vmem = pl.BlockSpec(memory_space=pltpu.VMEM)
    smem = pl.BlockSpec(memory_space=pltpu.SMEM)
    return pl.pallas_call(
        correlate_kernel,
        out_shape=jax.ShapeDtypeStruct((SHARES, 16, 128), BF),
        in_specs=[smem, smem, vmem, vmem, vmem, vmem],
        out_specs=vmem,
        scratch_shapes=[
            pltpu.VMEM((1024, 8, 128), F32),
            pltpu.VMEM((2049, 8, 128), F32),
            pltpu.VMEM((513, 8, 128), F32),
            pltpu.SMEM((2048 + 2 * UNROLL,), jnp.int32),
        ],
        compiler_params=pltpu.CompilerParams(vmem_limit_bytes=40 * 2**20),
    )(place, chunks, own, other, jnp.asarray(spread_table()), jnp.eye(128, dtype=BF))


def on_device(records, waveforms, slot_channels, slot_counts, slot_lags):
    core = lax.axis_index("c")
    quarter = lax.axis_index("y")
    following = lax.ppermute(records[:, : NFFT - HOP], ("z", "x"), [(i, i - 1) for i in range(1, 32)])

    first = core * 16 + quarter * 4
    waves = lax.dynamic_slice_in_dim(waveforms, first, 4, 0).reshape(128, -1)
    lags = lax.dynamic_slice_in_dim(slot_lags, first, 4, 0).reshape(128)
    counts = lax.dynamic_slice_in_dim(slot_counts, first, 4, 0)
    channels = lax.dynamic_slice_in_dim(slot_channels, first, 4, 0).reshape(128)
    live = (jnp.arange(SLOTS, dtype=jnp.int32)[None] < counts[:, None]).reshape(128)
    bank = bank_spectra(waves, lags, live)
    digits = jnp.stack([channels // 32, channels % 32, jnp.repeat(counts, SLOTS)])
    digits = jnp.pad(digits, ((0, 5), (0, 0))).astype(BF)
    digits = jnp.broadcast_to(digits, (SHARES, 8, 128))

    spectra = forward_spectra(records, following)
    shares = jnp.concatenate([spectra, bank, digits], axis=1)
    own = lax.all_to_all(shares, ("z", "x", "y"), split_axis=0, concat_axis=0, tiled=True)
    other = lax.ppermute(own[:, : 2 * BINS], "c", [(0, 1), (1, 0)])
    channels = own[:, 32].astype(jnp.int32) * 32 + own[:, 33].astype(jnp.int32)
    home = channels // 128
    place = ((home % 2) ^ core) * 512 + (home // 2) * 128 + channels % 128
    place = jnp.pad(8 * place.reshape(512 * SLOTS), (0, 128))
    chunks = (own[:, 34].astype(jnp.int32).reshape(512, SLOTS)[:, 0] + 7) // 8
    correlated = correlate(place, chunks, own, other)
    here = lax.all_to_all(correlated, ("z", "x", "y"), split_axis=0, concat_axis=0, tiled=True)
    there = lax.ppermute(here, "c", [(0, 1), (1, 0)])
    traces, energy = inverse_traces(here, there, core)
    energy = jnp.sum(energy, axis=1)
    energy = energy + lax.ppermute(energy, "c", [(0, 1), (1, 0)])
    shifts = [[(i, (i + d) % 4) for i in range(4)] for d in range(1, 4)]
    energy = sum((lax.ppermute(energy, "y", shift) for shift in shifts), energy)
    return traces * lax.rsqrt(energy / (32 * HOP) + EPS)[:, None]


def solution(mesh):
    fine = Mesh(mesh.devices.reshape(8, 4, 4, 2), ("z", "x", "y", "c"))
    tmpl, chan = ("z", "x"), ("y", "c")
    in_specs = (P(chan, tmpl), P(tmpl, None, None), P(tmpl, None), P(tmpl), P(tmpl, None))
    return jax.shard_map(
        on_device, mesh=fine, in_specs=in_specs, out_specs=P(tmpl, chan), check_vma=False
    )
```

```python
import functools
import math

import jax
import jax.numpy as jnp
import numpy as np
from jax import lax
from jax.experimental import pallas as pl
from jax.experimental.pallas import tpu as pltpu
from jax.sharding import Mesh
from jax.sharding import PartitionSpec as P

NFFT = 4096
BAND = 1024
HOP = 3072
SLOTS = 32
EPS = 1e-06
POINTS = 16
SPAN = NFFT // POINTS
ROTATED = (((1,), (1,)), ((), ()))
BINS = 8
SHARES = BAND // BINS
UNROLL = 8
COLUMNS = 256
BF = jnp.bfloat16
F32 = jnp.float32


def halves(matrix):
    upper = matrix.astype(BF)
    lower = (matrix - upper.astype(np.float64)).astype(BF)
    return upper, lower


def residues():
    place = np.arange(POINTS)
    return 4 * (place % 4) + place // 4


def share_bins():
    share = np.arange(SHARES)
    fine = BINS * (share % BINS)[:, None] + np.arange(BINS)[None, :]
    return POINTS * fine + residues()[share // BINS][:, None]


def sources():
    return [(0,), (8,)] + [(low, POINTS - low) for low in range(1, POINTS // 2)]


def band_table():
    samples = np.arange(SPAN)
    tables = []
    for group in sources():
        for residue in group:
            bins = POINTS * np.arange(BINS * BINS).reshape(BINS, BINS) + residue
            angle = 2.0 * np.pi * ((bins[..., None] * samples) % NFFT) / NFFT
            cosine, sine = np.cos(angle), np.sin(angle)
            sign = 1.0 if residue == group[0] else -1.0
            real = np.concatenate([cosine, sign * sine], axis=2)
            imag = np.concatenate([-sine, sign * cosine], axis=2)
            tables.append(np.stack([real, imag], axis=1).reshape(2 * BINS * BINS, 2 * SPAN))
    return np.stack(halves(np.stack(tables)))


def band_products(table, upper, lower, sink):
    order = list(residues())
    begin = 0
    for source, group in enumerate(sources()):
        depth = SPAN if len(group) == 1 else 2 * SPAN
        count = len(group)
        coarse, fine = (
            table[part, begin : begin + count, :, :depth].reshape(count * 128, depth)
            for part in range(2)
        )
        dot = functools.partial(
            lax.dot_general, dimension_numbers=ROTATED, preferred_element_type=F32
        )
        high, low = upper[source, :, :depth], lower[source, :, :depth]
        total = dot(coarse, high) + (dot(fine, high) + dot(coarse, low))
        for i, residue in enumerate(group):
            sink(BINS * order.index(residue), residue, total[128 * i : 128 * i + 128])
        begin += count


def inverse_table():
    bins = share_bins()
    angle = 2.0 * np.pi * ((bins[..., None] * np.arange(HOP // 3)) % NFFT) / NFFT
    weight = np.where(bins == 0, 1.0, 2.0)[..., None] / NFFT
    real = np.stack([np.cos(angle) * weight, -np.sin(angle) * weight], axis=1)
    imag = np.stack([np.sin(angle) * weight, np.cos(angle) * weight], axis=1)
    real, imag = (table.reshape(4, 512, HOP // 3) for table in (real, imag))
    table = np.concatenate([real[0], real[2], real[1], real[3], -imag[1], imag[3]])
    return table.reshape(-1, HOP // 3 // COLUMNS, COLUMNS).swapaxes(0, 1).astype(BF)


def inverse_kernel(mine, other, choice, table, traces, energy, left, held, arrived):
    steps = table.shape[0]
    copies = [
        pltpu.make_async_copy(table.at[step], held.at[step], arrived.at[step])
        for step in range(steps)
    ]
    for copy in copies:
        copy.start()
    pick = choice[...]
    for i in range(16):
        rows = slice(8 * i, 8 * i + 8)
        block = jnp.concatenate([q[rows].reshape(128, 128) for q in (mine, other)], axis=1)
        chosen = lax.dot_general(pick, block, ROTATED, preferred_element_type=F32)
        left[:, 128 * i : 128 * i + 128] = chosen.astype(BF)
    dot = functools.partial(jnp.dot, preferred_element_type=F32)
    squares = jnp.zeros((32, 128), F32)
    for step, copy in enumerate(copies):
        copy.wait()
        first = dot(left[:, 0:512], held[step, 0:512])
        second = dot(left[:, 1024:1536], held[step, 512:1024])
        turn = []
        for part in (1024, 2048):
            low = dot(left[:, 512:1024], held[step, part : part + 512])
            turn.append(low + dot(left[:, 1536:2048], held[step, part + 512 : part + 1024]))
        both = first + second
        values = both + turn[0], first - second + turn[1], both - turn[0]
        for quarter, value in enumerate(values):
            for block in range(4):
                part = value[32 * block : 32 * block + 32]
                begin = block * HOP + quarter * (HOP // 3) + step * COLUMNS
                traces[:, begin : begin + COLUMNS] = part
                part = part * part
                for lane in range(0, COLUMNS, 128):
                    squares = squares + part[:, lane : lane + 128]
    energy[...] = squares


def inverse_traces(mine, other, core):
    row = jnp.arange(128)[:, None]
    lane = jnp.arange(256)[None, :]
    block, half, template = row // 32, (row // 16) % 2, row % 16
    choice = lane == 128 * (half ^ core) + 64 * core + 16 * block + template
    table = inverse_table()
    vmem = pl.BlockSpec(memory_space=pltpu.VMEM)
    return pl.pallas_call(
        inverse_kernel,
        out_shape=(
            jax.ShapeDtypeStruct((32, 4 * HOP), F32),
            jax.ShapeDtypeStruct((32, 128), F32),
        ),
        in_specs=[vmem, vmem, vmem, pl.BlockSpec(memory_space=pl.ANY)],
        out_specs=(vmem, vmem),
        scratch_shapes=[
            pltpu.VMEM((128, 2 * BAND), BF),
            pltpu.VMEM(table.shape, BF),
            pltpu.SemaphoreType.DMA((table.shape[0],)),
        ],
        compiler_params=pltpu.CompilerParams(vmem_limit_bytes=56 * 2**20),
    )(mine, other, choice.astype(BF), jnp.asarray(table))


def split_store(upper, lower, source, rows, columns, value):
    high = value.astype(BF)
    upper[source, rows, columns] = high
    lower[source, rows, columns] = (value - high.astype(F32)).astype(BF)


def times(value, turns):
    real, imag = value
    cosine = math.cos(2.0 * math.pi * turns / POINTS)
    sine = math.sin(2.0 * math.pi * turns / POINTS)
    if turns == 0:
        return value
    if imag is None:
        return real * cosine, real * -sine
    return real * cosine + imag * sine, imag * cosine - real * sine


def sixteen_point(values):
    inner = []
    for a in range(4):
        x = values[a::4]
        even, odd = x[0] + x[2], x[1] + x[3]
        step = (x[0] - x[2], x[3] - x[1])
        inner.append([(even + odd, None), step, (even - odd, None), (step[0], -step[1])])
    sums = [None] * 9
    for low in range(4):
        v = [times(inner[a][low], (low * a) % POINTS) for a in range(4)]
        real = [part[0] for part in v]
        if low == 0:
            even, odd = real[0] + real[2], real[1] + real[3]
            sums[0], sums[8] = (even + odd, None), (even - odd, None)
            sums[4] = (real[0] - real[2], real[3] - real[1])
            continue
        imag = [jnp.zeros_like(real[0]) if part[1] is None else part[1] for part in v]
        even = (real[0] + real[2], imag[0] + imag[2])
        odd = (real[1] + real[3], imag[1] + imag[3])
        sums[low] = (even[0] + odd[0], even[1] + odd[1])
        even = (real[0] - real[2], imag[0] - imag[2])
        odd = (real[1] - real[3], imag[1] - imag[3])
        sums[low + 4] = (even[0] + odd[1], even[1] - odd[0])
    return sums


def source_places():
    return {group[0]: source for source, group in enumerate(sources())}


def forward_kernel(records, following, table, out, upper, lower):
    def mix(i, carry):
        rows = pl.ds(pl.multiple_of(16 * i, 16), 16)
        for start in range(0, SPAN, 128):
            values = []
            for a in range(POINTS):
                begin = SPAN * a + start
                part = records if begin < HOP else following
                begin = begin % HOP
                values.append(part[rows, begin : begin + 128].astype(F32))
            for residue, value in enumerate(sixteen_point(values)):
                source = source_places()[residue]
                for part in range(2):
                    if value[part] is not None:
                        columns = slice(SPAN * part + start, SPAN * part + start + 128)
                        split_store(upper, lower, source, rows, columns, value[part])
        return carry

    lax.fori_loop(0, 8, mix, 0)

    def sink(first, residue, total):
        out[first : first + BINS] = total.astype(BF).reshape(BINS, 2 * BINS, 128)

    band_products(table, upper, lower, sink)


def bank_kernel(first, waveforms, lags, live, table, out, upper, lower):
    for i in range(4):
        rows = slice(SLOTS * i, SLOTS * i + SLOTS)
        wave = waveforms[first[0] + i].astype(F32)
        begin, end = wave[:, :SPAN], wave[:, SPAN:]
        for group in sources():
            source = source_places()[group[0]]
            cosine = math.cos(2.0 * math.pi * group[0] / POINTS)
            sine = math.sin(2.0 * math.pi * group[0] / POINTS)
            split_store(upper, lower, source, rows, slice(0, SPAN), begin + end * cosine)
            if len(group) == 2:
                split_store(upper, lower, source, rows, slice(SPAN, 2 * SPAN), end * -sine)
    turn = 2.0 * math.pi / NFFT
    lag = lags[...]
    fine = lax.broadcasted_iota(jnp.int32, (BINS * BINS, 128), 0) * POINTS
    fine = jnp.bitwise_and(fine * lag, NFFT - 1).astype(F32) * turn
    fine_cos, fine_sin = jnp.cos(fine), jnp.sin(fine)
    step = lax.broadcasted_iota(jnp.int32, (POINTS, 128), 0)
    step = jnp.bitwise_and(step * lag, NFFT - 1).astype(F32) * turn
    step_cos, step_sin = jnp.cos(step) * live[...], jnp.sin(step) * live[...]

    def sink(place, residue, total):
        total = total.reshape(BINS, 2, BINS, 128)
        base_real = total[:, 0].reshape(BINS * BINS, 128)
        base_imag = -total[:, 1].reshape(BINS * BINS, 128)
        low_cos, low_sin = (v[residue : residue + 1] for v in (step_cos, step_sin))
        cosine = fine_cos * low_cos - fine_sin * low_sin
        sine = fine_sin * low_cos + fine_cos * low_sin
        real = base_real * cosine - base_imag * sine
        imag = base_real * sine + base_imag * cosine
        both = [part.reshape(BINS, 1, BINS, 128) for part in (real, imag)]
        both = jnp.concatenate(both, axis=1).reshape(BINS, 2 * BINS, 128)
        out[place : place + BINS] = both.astype(BF)

    band_products(table, upper, lower, sink)


def spectra_call(kernel, smem_count, operands):
    vmem = pl.BlockSpec(memory_space=pltpu.VMEM)
    smem = pl.BlockSpec(memory_space=pltpu.SMEM)
    return pl.pallas_call(
        kernel,
        out_shape=jax.ShapeDtypeStruct((SHARES, 2 * BINS, 128), BF),
        in_specs=[smem] * smem_count + [vmem] * (len(operands) - smem_count),
        out_specs=vmem,
        scratch_shapes=[pltpu.VMEM((9, 128, 2 * SPAN), BF)] * 2,
        compiler_params=pltpu.CompilerParams(vmem_limit_bytes=24 * 2**20),
    )(*operands)


def forward_spectra(records, following):
    return spectra_call(forward_kernel, 0, (records, following, jnp.asarray(band_table())))


def bank_spectra(first, waveforms, lags, live):
    operands = (first.reshape(1), waveforms, lags, live, jnp.asarray(band_table()))
    return spectra_call(bank_kernel, 1, operands)


def swap_blocks(parts, lane):
    count = len(parts)
    size = 128 // count
    step = count // 2
    while step:
        low = (lane // (size * step)) % 2 == 0
        fresh = list(parts)
        for i in range(count):
            if i & step:
                continue
            j = i + step
            fresh[i] = jnp.where(low, parts[i], pltpu.roll(parts[j], size * step, 1))
            fresh[j] = jnp.where(low, pltpu.roll(parts[i], 128 - size * step, 1), parts[j])
        parts = fresh
        step //= 2
    return parts


def correlate_kernel(place, chunks, own, other, spread, unit, out, table, weights, sums, live):
    eye = unit[...]

    def turned(block):
        return lax.dot_general(eye, block, ROTATED, preferred_element_type=F32)

    for half, source in enumerate((own, other)):
        for y in range(4):
            start = half * 512 + y * 128
            for s in range(4):
                tiles = [source[(8 * s + i) * 4 + y, 0:16, :] for i in range(8)]
                table[start : start + 128, s, :] = turned(jnp.concatenate(tiles, axis=0))
                wide = [tile.astype(F32) for tile in tiles]
                swapped = [part for tile in wide for part in (tile[8:], tile[:8])]
                block = jnp.concatenate(swapped, axis=0).astype(BF)
                table[start : start + 128, 4 + s, :] = turned(block)

    def expand(g, position):
        block = jnp.concatenate([own[g * 8 + i, 16:32, :] for i in range(8)], axis=0)
        compact = turned(block).astype(BF)
        for i in range(4):
            wide = jnp.dot(compact, spread[i], preferred_element_type=F32)
            for j in range(2):
                first = (g * 8 + 2 * i + j) * 16
                part = wide[:, 128 * j : 128 * (j + 1)]
                weights[pl.ds(first, 16)] = part.reshape(16, 8, 128)
        for i in range(32):
            t = g * 32 + i
            for s in range(4):
                live[position + s] = t * 4 + s
            position = position + chunks[t]
        return position

    count = lax.fori_loop(0, 16, expand, 0)
    for s in range(UNROLL):
        live[count + s] = 2048
    weights[2048] = jnp.zeros((8, 128), F32)
    sums[...] = jnp.zeros_like(sums)

    def some_chunks(step, carry):
        for i in range(UNROLL):
            chunk = live[step * UNROLL + i]
            tile = weights[chunk]
            totals = [None, None]
            for u in range(8):
                row = table_rows(table, place[chunk * 8 + u])
                term = row * tile[u : u + 1]
                totals[u % 2] = term if u < 2 else totals[u % 2] + term
            t = lax.shift_right_logical(chunk, 2)
            sums[t] = sums[t] + (totals[0] + totals[1])
        return carry

    lax.fori_loop(0, lax.div(count + UNROLL - 1, UNROLL), some_chunks, 0)

    lane = lax.broadcasted_iota(jnp.int32, (128, 128), 1)
    is_real = (lane // BINS) % 2 == 0
    for g in range(4):
        for y in range(4):
            first = sums[g * 128 : (g + 1) * 128, y, :]
            second = sums[g * 128 : (g + 1) * 128, 4 + y, :]
            real = first - pltpu.roll(first, 128 - BINS, 1)
            imag = second + pltpu.roll(second, BINS, 1)
            total = turned(jnp.where(is_real, real, imag).astype(BF))
            parts = [total[16 * i : 16 * (i + 1)] for i in range(8)]
            for i, part in enumerate(swap_blocks(parts, lane[:16])):
                out[(8 * g + i) * 4 + y] = part.astype(BF)


def table_rows(table, first):
    rows = table.reshape(8192, 128)
    return rows[pl.ds(pl.multiple_of(first, 8), 8)]


def spread_table():
    lane = np.arange(128)
    one = np.zeros((2, BINS, 128))
    for part in range(2):
        one[part, lane % BINS, lane] = (lane // BINS) % 2 == part
    one = one.reshape(2 * BINS, 128)
    table = np.zeros((4, 8, 2 * BINS, 2, 128))
    for share in range(8):
        table[share // 2, share, :, share % 2] = one
    return table.reshape(4, 128, 256).astype(BF)


def correlate(place, chunks, own, other):
    vmem = pl.BlockSpec(memory_space=pltpu.VMEM)
    smem = pl.BlockSpec(memory_space=pltpu.SMEM)
    return pl.pallas_call(
        correlate_kernel,
        out_shape=jax.ShapeDtypeStruct((SHARES, 16, 128), BF),
        in_specs=[smem, smem, vmem, vmem, vmem, vmem],
        out_specs=vmem,
        scratch_shapes=[
            pltpu.VMEM((1024, 8, 128), F32),
            pltpu.VMEM((2049, 8, 128), F32),
            pltpu.VMEM((513, 8, 128), F32),
            pltpu.SMEM((2048 + 2 * UNROLL,), jnp.int32),
        ],
        compiler_params=pltpu.CompilerParams(vmem_limit_bytes=40 * 2**20),
    )(place, chunks, own, other, jnp.asarray(spread_table()), jnp.eye(128, dtype=BF))


def on_device(records, waveforms, slot_channels, slot_counts, slot_lags):
    core = lax.axis_index("c")
    quarter = lax.axis_index("y")
    following = lax.ppermute(records[:, : NFFT - HOP], ("z", "x"), [(i, i - 1) for i in range(1, 32)])

    first = core * 16 + quarter * 4
    lags = lax.dynamic_slice_in_dim(slot_lags, first, 4, 0).reshape(1, 128)
    counts = lax.dynamic_slice_in_dim(slot_counts, first, 4, 0)
    channels = lax.dynamic_slice_in_dim(slot_channels, first, 4, 0).reshape(128)
    live = (jnp.arange(SLOTS, dtype=jnp.int32)[None] < counts[:, None]).reshape(1, 128)
    bank = bank_spectra(first, waveforms, lags, live.astype(F32))
    digits = jnp.stack([channels // 32, channels % 32, jnp.repeat(counts, SLOTS)])
    digits = jnp.pad(digits, ((0, 5), (0, 0))).astype(BF)
    digits = jnp.broadcast_to(digits, (SHARES, 8, 128))

    spectra = forward_spectra(records, following)
    shares = jnp.concatenate([spectra, bank, digits], axis=1)
    own = lax.all_to_all(shares, ("z", "x", "y"), split_axis=0, concat_axis=0, tiled=True)
    other = lax.ppermute(own[:, : 2 * BINS], "c", [(0, 1), (1, 0)])
    channels = own[:, 32].astype(jnp.int32) * 32 + own[:, 33].astype(jnp.int32)
    home = channels // 128
    place = ((home % 2) ^ core) * 512 + (home // 2) * 128 + channels % 128
    place = jnp.pad(8 * place.reshape(512 * SLOTS), (0, 128))
    chunks = (own[:, 34].astype(jnp.int32).reshape(512, SLOTS)[:, 0] + 7) // 8
    correlated = correlate(place, chunks, own, other)
    here = lax.all_to_all(correlated, ("z", "x", "y"), split_axis=0, concat_axis=0, tiled=True)
    there = lax.ppermute(here, "c", [(0, 1), (1, 0)])
    traces, energy = inverse_traces(here, there, core)
    energy = jnp.sum(energy, axis=1)
    energy = energy + lax.ppermute(energy, "c", [(0, 1), (1, 0)])
    shifts = [[(i, (i + d) % 4) for i in range(4)] for d in range(1, 4)]
    energy = sum((lax.ppermute(energy, "y", shift) for shift in shifts), energy)
    return traces * lax.rsqrt(energy / (32 * HOP) + EPS)[:, None]


def solution(mesh):
    fine = Mesh(mesh.devices.reshape(8, 4, 4, 2), ("z", "x", "y", "c"))
    tmpl, chan = ("z", "x"), ("y", "c")
    in_specs = (P(chan, tmpl), P(tmpl, None, None), P(tmpl, None), P(tmpl), P(tmpl, None))
    return jax.shard_map(
        on_device, mesh=fine, in_specs=in_specs, out_specs=P(tmpl, chan), check_vma=False
    )
```

```python
import functools
import math

import jax
import jax.numpy as jnp
import numpy as np
from jax import lax
from jax.experimental import pallas as pl
from jax.experimental.pallas import tpu as pltpu
from jax.sharding import Mesh
from jax.sharding import PartitionSpec as P

NFFT = 4096
BAND = 1024
HOP = 3072
SLOTS = 32
EPS = 1e-06
POINTS = 16
SPAN = NFFT // POINTS
ROTATED = (((1,), (1,)), ((), ()))
BINS = 8
SHARES = BAND // BINS
UNROLL = 8
COLUMNS = 256
BF = jnp.bfloat16
F32 = jnp.float32


def halves(matrix):
    upper = matrix.astype(BF)
    lower = (matrix - upper.astype(np.float64)).astype(BF)
    return upper, lower


def residues():
    place = np.arange(POINTS)
    return 4 * (place % 4) + place // 4


def share_bins():
    share = np.arange(SHARES)
    fine = BINS * (share % BINS)[:, None] + np.arange(BINS)[None, :]
    return POINTS * fine + residues()[share // BINS][:, None]


def sources():
    return [(0,), (8,)] + [(low, POINTS - low) for low in range(1, POINTS // 2)]


def band_table():
    samples = np.arange(SPAN)
    tables = []
    for group in sources():
        for residue in group:
            bins = POINTS * np.arange(BINS * BINS).reshape(BINS, BINS) + residue
            angle = 2.0 * np.pi * ((bins[..., None] * samples) % NFFT) / NFFT
            cosine, sine = np.cos(angle), np.sin(angle)
            sign = 1.0 if residue == group[0] else -1.0
            real = np.concatenate([cosine, sign * sine], axis=2)
            imag = np.concatenate([-sine, sign * cosine], axis=2)
            tables.append(np.stack([real, imag], axis=1).reshape(2 * BINS * BINS, 2 * SPAN))
    return np.stack(halves(np.stack(tables)))


def band_products(table, upper, lower, sink):
    order = list(residues())
    begin = 0
    for source, group in enumerate(sources()):
        depth = SPAN if len(group) == 1 else 2 * SPAN
        count = len(group)
        coarse, fine = (
            table[part, begin : begin + count, :, :depth].reshape(count * 128, depth)
            for part in range(2)
        )
        dot = functools.partial(
            lax.dot_general, dimension_numbers=ROTATED, preferred_element_type=F32
        )
        high, low = upper[source, :, :depth], lower[source, :, :depth]
        total = dot(coarse, high) + (dot(fine, high) + dot(coarse, low))
        for i, residue in enumerate(group):
            sink(BINS * order.index(residue), residue, total[128 * i : 128 * i + 128])
        begin += count


def inverse_table():
    bins = share_bins()
    angle = 2.0 * np.pi * ((bins[..., None] * np.arange(HOP // 3)) % NFFT) / NFFT
    weight = np.where(bins == 0, 1.0, 2.0)[..., None] / NFFT
    real = np.stack([np.cos(angle) * weight, -np.sin(angle) * weight], axis=1)
    imag = np.stack([np.sin(angle) * weight, np.cos(angle) * weight], axis=1)
    real, imag = (table.reshape(4, 512, HOP // 3) for table in (real, imag))
    table = np.concatenate([real[0], real[2], real[1], real[3], -imag[1], imag[3]])
    return table.reshape(-1, HOP // 3 // COLUMNS, COLUMNS).swapaxes(0, 1).astype(BF)


def inverse_kernel(core, mine, other, table, traces, energy, left, held, arrived):
    steps = table.shape[0]
    copies = [
        pltpu.make_async_copy(table.at[step], held.at[step], arrived.at[step])
        for step in range(steps)
    ]
    for copy in copies:
        copy.start()
    row = lax.broadcasted_iota(jnp.int32, (128, 256), 0)
    lane = lax.broadcasted_iota(jnp.int32, (128, 256), 1)
    half = lax.shift_right_logical(row, 4) & 1
    wanted = 128 * (half ^ core[0]) + 64 * core[0]
    wanted = wanted + 16 * lax.shift_right_logical(row, 5) + (row & 15)
    pick = jnp.where(lane == wanted, 1.0, 0.0).astype(BF)
    for i in range(16):
        rows = slice(8 * i, 8 * i + 8)
        block = jnp.concatenate([q[rows].reshape(128, 128) for q in (mine, other)], axis=1)
        chosen = lax.dot_general(pick, block, ROTATED, preferred_element_type=F32)
        left[:, 128 * i : 128 * i + 128] = chosen.astype(BF)
    dot = functools.partial(jnp.dot, preferred_element_type=F32)
    squares = jnp.zeros((32, 128), F32)
    for step, copy in enumerate(copies):
        copy.wait()
        first = dot(left[:, 0:512], held[step, 0:512])
        second = dot(left[:, 1024:1536], held[step, 512:1024])
        turn = []
        for part in (1024, 2048):
            low = dot(left[:, 512:1024], held[step, part : part + 512])
            turn.append(low + dot(left[:, 1536:2048], held[step, part + 512 : part + 1024]))
        both = first + second
        values = both + turn[0], first - second + turn[1], both - turn[0]
        for quarter, value in enumerate(values):
            for block in range(4):
                part = value[32 * block : 32 * block + 32]
                begin = block * HOP + quarter * (HOP // 3) + step * COLUMNS
                traces[:, begin : begin + COLUMNS] = part
                part = part * part
                for lane in range(0, COLUMNS, 128):
                    squares = squares + part[:, lane : lane + 128]
    energy[...] = jnp.broadcast_to(jnp.sum(squares, axis=1, keepdims=True), (32, 128))


def inverse_traces(mine, other, core):
    table = inverse_table()
    vmem = pl.BlockSpec(memory_space=pltpu.VMEM)
    return pl.pallas_call(
        inverse_kernel,
        out_shape=(
            jax.ShapeDtypeStruct((32, 4 * HOP), F32),
            jax.ShapeDtypeStruct((32, 128), F32),
        ),
        in_specs=[pl.BlockSpec(memory_space=pltpu.SMEM), vmem, vmem, pl.BlockSpec(memory_space=pl.ANY)],
        out_specs=(vmem, vmem),
        scratch_shapes=[
            pltpu.VMEM((128, 2 * BAND), BF),
            pltpu.VMEM(table.shape, BF),
            pltpu.SemaphoreType.DMA((table.shape[0],)),
        ],
        compiler_params=pltpu.CompilerParams(vmem_limit_bytes=55 * 2**20),
    )(core.reshape(1), mine, other, jnp.asarray(table))


def split_store(upper, lower, source, rows, columns, value):
    high = value.astype(BF)
    upper[source, rows, columns] = high
    lower[source, rows, columns] = (value - high.astype(F32)).astype(BF)


def times(value, turns):
    real, imag = value
    cosine = math.cos(2.0 * math.pi * turns / POINTS)
    sine = math.sin(2.0 * math.pi * turns / POINTS)
    if turns == 0:
        return value
    if imag is None:
        return real * cosine, real * -sine
    return real * cosine + imag * sine, imag * cosine - real * sine


def sixteen_point(values):
    inner = []
    for a in range(4):
        x = values[a::4]
        even, odd = x[0] + x[2], x[1] + x[3]
        step = (x[0] - x[2], x[3] - x[1])
        inner.append([(even + odd, None), step, (even - odd, None), (step[0], -step[1])])
    sums = [None] * 9
    for low in range(4):
        v = [times(inner[a][low], (low * a) % POINTS) for a in range(4)]
        real = [part[0] for part in v]
        if low == 0:
            even, odd = real[0] + real[2], real[1] + real[3]
            sums[0], sums[8] = (even + odd, None), (even - odd, None)
            sums[4] = (real[0] - real[2], real[3] - real[1])
            continue
        imag = [jnp.zeros_like(real[0]) if part[1] is None else part[1] for part in v]
        even = (real[0] + real[2], imag[0] + imag[2])
        odd = (real[1] + real[3], imag[1] + imag[3])
        sums[low] = (even[0] + odd[0], even[1] + odd[1])
        even = (real[0] - real[2], imag[0] - imag[2])
        odd = (real[1] - real[3], imag[1] - imag[3])
        sums[low + 4] = (even[0] + odd[1], even[1] - odd[0])
    return sums


def source_places():
    return {group[0]: source for source, group in enumerate(sources())}


def forward_kernel(records, following, table, bank, out, upper, lower):
    out[:, 2 * BINS :, :] = bank[...]

    def mix(i, carry):
        rows = pl.ds(pl.multiple_of(16 * i, 16), 16)
        for start in range(0, SPAN, 128):
            values = []
            for a in range(POINTS):
                begin = SPAN * a + start
                part = records if begin < HOP else following
                begin = begin % HOP
                values.append(part[rows, begin : begin + 128].astype(F32))
            for residue, value in enumerate(sixteen_point(values)):
                source = source_places()[residue]
                for part in range(2):
                    if value[part] is not None:
                        columns = slice(SPAN * part + start, SPAN * part + start + 128)
                        split_store(upper, lower, source, rows, columns, value[part])
        return carry

    lax.fori_loop(0, 8, mix, 0)

    def sink(first, residue, total):
        out[first : first + BINS, : 2 * BINS] = total.astype(BF).reshape(BINS, 2 * BINS, 128)

    band_products(table, upper, lower, sink)


def bank_kernel(first, waveforms, lags, live, table, out, upper, lower):
    for i in range(4):
        rows = slice(SLOTS * i, SLOTS * i + SLOTS)
        wave = waveforms[first[0] + i].astype(F32)
        begin, end = wave[:, :SPAN], wave[:, SPAN:]
        for group in sources():
            source = source_places()[group[0]]
            cosine = math.cos(2.0 * math.pi * group[0] / POINTS)
            sine = math.sin(2.0 * math.pi * group[0] / POINTS)
            split_store(upper, lower, source, rows, slice(0, SPAN), begin + end * cosine)
            if len(group) == 2:
                split_store(upper, lower, source, rows, slice(SPAN, 2 * SPAN), end * -sine)
    turn = 2.0 * math.pi / NFFT
    lag = lags[...]
    fine = lax.broadcasted_iota(jnp.int32, (BINS * BINS, 128), 0) * POINTS
    fine = jnp.bitwise_and(fine * lag, NFFT - 1).astype(F32) * turn
    fine_cos, fine_sin = jnp.cos(fine), jnp.sin(fine)
    step = lax.broadcasted_iota(jnp.int32, (POINTS, 128), 0)
    step = jnp.bitwise_and(step * lag, NFFT - 1).astype(F32) * turn
    step_cos, step_sin = jnp.cos(step) * live[...], jnp.sin(step) * live[...]

    def sink(place, residue, total):
        total = total.reshape(BINS, 2, BINS, 128)
        base_real = total[:, 0].reshape(BINS * BINS, 128)
        base_imag = -total[:, 1].reshape(BINS * BINS, 128)
        low_cos, low_sin = (v[residue : residue + 1] for v in (step_cos, step_sin))
        cosine = fine_cos * low_cos - fine_sin * low_sin
        sine = fine_sin * low_cos + fine_cos * low_sin
        real = base_real * cosine - base_imag * sine
        imag = base_real * sine + base_imag * cosine
        both = [part.reshape(BINS, 1, BINS, 128) for part in (real, imag)]
        both = jnp.concatenate(both, axis=1).reshape(BINS, 2 * BINS, 128)
        out[place : place + BINS] = both.astype(BF)

    band_products(table, upper, lower, sink)


def spectra_call(kernel, rows, smem_count, operands):
    vmem = pl.BlockSpec(memory_space=pltpu.VMEM)
    smem = pl.BlockSpec(memory_space=pltpu.SMEM)
    return pl.pallas_call(
        kernel,
        out_shape=jax.ShapeDtypeStruct((SHARES, rows, 128), BF),
        in_specs=[smem] * smem_count + [vmem] * (len(operands) - smem_count),
        out_specs=vmem,
        scratch_shapes=[pltpu.VMEM((9, 128, 2 * SPAN), BF)] * 2,
        compiler_params=pltpu.CompilerParams(vmem_limit_bytes=24 * 2**20),
    )(*operands)


def forward_spectra(records, following, bank):
    operands = (records, following, jnp.asarray(band_table()), bank)
    return spectra_call(forward_kernel, 4 * BINS, 0, operands)


def bank_spectra(first, waveforms, lags, live):
    operands = (first.reshape(1), waveforms, lags, live, jnp.asarray(band_table()))
    return spectra_call(bank_kernel, 2 * BINS, 1, operands)


def swap_blocks(parts, lane):
    count = len(parts)
    size = 128 // count
    step = count // 2
    while step:
        low = (lane // (size * step)) % 2 == 0
        fresh = list(parts)
        for i in range(count):
            if i & step:
                continue
            j = i + step
            fresh[i] = jnp.where(low, parts[i], pltpu.roll(parts[j], size * step, 1))
            fresh[j] = jnp.where(low, pltpu.roll(parts[i], 128 - size * step, 1), parts[j])
        parts = fresh
        step //= 2
    return parts


def turned(unit, block):
    return lax.dot_general(unit[...], block, ROTATED, preferred_element_type=F32)


def weights_kernel(chunks, own, spread, unit, weights, live, count):
    def expand(g, position):
        block = jnp.concatenate([own[g * 8 + i, 16:32, :] for i in range(8)], axis=0)
        compact = turned(unit, block).astype(BF)
        for i in range(4):
            wide = jnp.dot(compact, spread[i], preferred_element_type=F32)
            for j in range(2):
                first = (g * 8 + 2 * i + j) * 16
                part = wide[:, 128 * j : 128 * (j + 1)]
                weights[pl.ds(first, 16)] = part.reshape(16, 8, 128)
        for i in range(32):
            t = g * 32 + i
            for s in range(4):
                live[position + s] = t * 4 + s
            position = position + chunks[t]
        return position

    total = lax.fori_loop(0, 16, expand, 0)
    for s in range(UNROLL):
        live[total + s] = 2048
    weights[2048] = jnp.zeros((8, 128), F32)
    count[0] = total


def correlate_kernel(place, live, count, own, other, weights, unit, out, table, sums):
    for half, source in enumerate((own, other)):
        for y in range(4):
            start = half * 512 + y * 128
            for s in range(4):
                tiles = [source[(8 * s + i) * 4 + y, 0:16, :] for i in range(8)]
                block = jnp.concatenate(tiles, axis=0)
                table[start : start + 128, s, :] = turned(unit, block)
                wide = [tile.astype(F32) for tile in tiles]
                swapped = [part for tile in wide for part in (tile[8:], tile[:8])]
                block = jnp.concatenate(swapped, axis=0).astype(BF)
                table[start : start + 128, 4 + s, :] = turned(unit, block)
    sums[...] = jnp.zeros_like(sums)

    def some_chunks(step, carry):
        for i in range(UNROLL):
            chunk = live[step * UNROLL + i]
            tile = weights[chunk]
            totals = [None, None]
            for u in range(8):
                row = table_rows(table, place[chunk * 8 + u])
                term = row * tile[u : u + 1]
                totals[u % 2] = term if u < 2 else totals[u % 2] + term
            t = lax.shift_right_logical(chunk, 2)
            sums[t] = sums[t] + (totals[0] + totals[1])
        return carry

    lax.fori_loop(0, lax.div(count[0] + UNROLL - 1, UNROLL), some_chunks, 0)

    lane = lax.broadcasted_iota(jnp.int32, (128, 128), 1)
    is_real = (lane // BINS) % 2 == 0
    for g in range(4):
        for y in range(4):
            first = sums[g * 128 : (g + 1) * 128, y, :]
            second = sums[g * 128 : (g + 1) * 128, 4 + y, :]
            real = first - pltpu.roll(first, 128 - BINS, 1)
            imag = second + pltpu.roll(second, BINS, 1)
            total = turned(unit, jnp.where(is_real, real, imag).astype(BF))
            parts = [total[16 * i : 16 * (i + 1)] for i in range(8)]
            for i, part in enumerate(swap_blocks(parts, lane[:16])):
                out[(8 * g + i) * 4 + y] = part.astype(BF)


def table_rows(table, first):
    rows = table.reshape(8192, 128)
    return rows[pl.ds(pl.multiple_of(first, 8), 8)]


def spread_table():
    lane = np.arange(128)
    one = np.zeros((2, BINS, 128))
    for part in range(2):
        one[part, lane % BINS, lane] = (lane // BINS) % 2 == part
    one = one.reshape(2 * BINS, 128)
    table = np.zeros((4, 8, 2 * BINS, 2, 128))
    for share in range(8):
        table[share // 2, share, :, share % 2] = one
    return table.reshape(4, 128, 256).astype(BF)


def correlate(place, chunks, own, other):
    vmem = pl.BlockSpec(memory_space=pltpu.VMEM)
    smem = pl.BlockSpec(memory_space=pltpu.SMEM)
    unit = jnp.eye(128, dtype=BF)
    weights, live, count = pl.pallas_call(
        weights_kernel,
        out_shape=(
            jax.ShapeDtypeStruct((2049, 8, 128), F32),
            jax.ShapeDtypeStruct((2048 + 2 * UNROLL,), jnp.int32),
            jax.ShapeDtypeStruct((1,), jnp.int32),
        ),
        in_specs=[smem, vmem, vmem, vmem],
        out_specs=(vmem, smem, smem),
        compiler_params=pltpu.CompilerParams(vmem_limit_bytes=16 * 2**20),
        cost_estimate=pl.CostEstimate(flops=2**29, bytes_accessed=10**7, transcendentals=0),
    )(chunks, own, jnp.asarray(spread_table()), unit)
    return pl.pallas_call(
        correlate_kernel,
        out_shape=jax.ShapeDtypeStruct((SHARES, 16, 128), BF),
        in_specs=[smem, smem, smem, vmem, vmem, vmem, vmem],
        out_specs=vmem,
        scratch_shapes=[
            pltpu.VMEM((1024, 8, 128), F32),
            pltpu.VMEM((513, 8, 128), F32),
        ],
        compiler_params=pltpu.CompilerParams(vmem_limit_bytes=22 * 2**20),
    )(place, live, count, own, other, weights, unit)


def on_device(records, waveforms, slot_channels, slot_counts, slot_lags):
    core = lax.axis_index("c")
    quarter = lax.axis_index("y")
    following = lax.ppermute(records[:, : NFFT - HOP], ("z", "x"), [(i, i - 1) for i in range(1, 32)])

    half_channels = lax.dynamic_slice_in_dim(slot_channels, core * 16, 16, 0)
    half_counts = lax.dynamic_slice_in_dim(slot_counts, core * 16, 16, 0)
    home = half_channels // 128
    place = ((home % 2) ^ core) * 512 + (home // 2) * 128 + half_channels % 128
    chunks = jnp.pad((half_counts + 7) // 8, (0, 112))
    slots = jnp.concatenate([8 * place.reshape(4, 128), chunks[None]])
    group = lax.axis_index(("z", "x"))
    is_own = (jnp.arange(32, dtype=jnp.int32) == group)[:, None, None]
    slots = jnp.where(is_own, slots[None], 0).astype(F32)
    slots = lax.psum(slots.reshape(160, 128), ("z", "x"))
    slots = slots.astype(jnp.int32).reshape(32, 5, 128)
    place = jnp.pad(slots[:, :4].reshape(512 * SLOTS), (0, 128))
    chunks = slots[:, 4, :16].reshape(512)

    first = core * 16 + quarter * 4
    lags = lax.dynamic_slice_in_dim(slot_lags, first, 4, 0).reshape(1, 128)
    counts = lax.dynamic_slice_in_dim(slot_counts, first, 4, 0)
    live = (jnp.arange(SLOTS, dtype=jnp.int32)[None] < counts[:, None]).reshape(1, 128)
    bank = bank_spectra(first, waveforms, lags, live.astype(F32))

    shares = forward_spectra(records, following, bank)
    own = lax.all_to_all(shares, ("z", "x", "y"), split_axis=0, concat_axis=0, tiled=True)
    other = lax.ppermute(own[:, : 2 * BINS], "c", [(0, 1), (1, 0)])
    correlated = correlate(place, chunks, own, other)
    here = lax.all_to_all(correlated, ("z", "x", "y"), split_axis=0, concat_axis=0, tiled=True)
    there = lax.ppermute(here, "c", [(0, 1), (1, 0)])
    traces, energy = inverse_traces(here, there, core)
    energy = energy + lax.ppermute(energy, "c", [(0, 1), (1, 0)])
    shifts = [[(i, (i + d) % 4) for i in range(4)] for d in range(1, 4)]
    energy = sum((lax.ppermute(energy, "y", shift) for shift in shifts), energy)
    return traces * lax.rsqrt(energy[:, :1] / (32 * HOP) + EPS)


def solution(mesh):
    fine = Mesh(mesh.devices.reshape(8, 4, 4, 2), ("z", "x", "y", "c"))
    tmpl, chan = ("z", "x"), ("y", "c")
    in_specs = (P(chan, tmpl), P(tmpl, None, None), P(tmpl, None), P(tmpl), P(tmpl, None))
    return jax.shard_map(
        on_device, mesh=fine, in_specs=in_specs, out_specs=P(tmpl, chan), check_vma=False
    )
```

```python
import functools
import math

import jax
import jax.numpy as jnp
import numpy as np
from jax import lax
from jax.experimental import pallas as pl
from jax.experimental.pallas import tpu as pltpu
from jax.sharding import Mesh
from jax.sharding import PartitionSpec as P

NFFT = 4096
BAND = 1024
HOP = 3072
SLOTS = 32
EPS = 1e-06
POINTS = 16
SPAN = NFFT // POINTS
ROTATED = (((1,), (1,)), ((), ()))
BINS = 8
SHARES = BAND // BINS
UNROLL = 8
COLUMNS = 256
BF = jnp.bfloat16
F32 = jnp.float32


def halves(matrix):
    upper = matrix.astype(BF)
    lower = (matrix - upper.astype(np.float64)).astype(BF)
    return upper, lower


def residues():
    place = np.arange(POINTS)
    return 4 * (place % 4) + place // 4


def share_bins():
    share = np.arange(SHARES)
    fine = BINS * (share % BINS)[:, None] + np.arange(BINS)[None, :]
    return POINTS * fine + residues()[share // BINS][:, None]


def sources():
    return [(0,), (8,)] + [(low, POINTS - low) for low in range(1, POINTS // 2)]


def band_table():
    samples = np.arange(SPAN)
    tables = []
    for group in sources():
        for residue in group:
            bins = POINTS * np.arange(BINS * BINS).reshape(BINS, BINS) + residue
            angle = 2.0 * np.pi * ((bins[..., None] * samples) % NFFT) / NFFT
            cosine, sine = np.cos(angle), np.sin(angle)
            sign = 1.0 if residue == group[0] else -1.0
            real = np.concatenate([cosine, sign * sine], axis=2)
            imag = np.concatenate([-sine, sign * cosine], axis=2)
            tables.append(np.stack([real, imag], axis=1).reshape(2 * BINS * BINS, 2 * SPAN))
    return np.stack(halves(np.stack(tables)))


def band_products(table, upper, lower, sink):
    order = list(residues())
    begin = 0
    for source, group in enumerate(sources()):
        depth = SPAN if len(group) == 1 else 2 * SPAN
        count = len(group)
        coarse, fine = (
            table[part, begin : begin + count, :, :depth].reshape(count * 128, depth)
            for part in range(2)
        )
        dot = functools.partial(
            lax.dot_general, dimension_numbers=ROTATED, preferred_element_type=F32
        )
        high, low = upper[source, :, :depth], lower[source, :, :depth]
        total = dot(coarse, high) + (dot(fine, high) + dot(coarse, low))
        for i, residue in enumerate(group):
            sink(BINS * order.index(residue), residue, total[128 * i : 128 * i + 128])
        begin += count


def inverse_table():
    bins = share_bins()
    angle = 2.0 * np.pi * ((bins[..., None] * np.arange(HOP // 3)) % NFFT) / NFFT
    weight = np.where(bins == 0, 1.0, 2.0)[..., None] / NFFT
    real = np.stack([np.cos(angle) * weight, -np.sin(angle) * weight], axis=1)
    imag = np.stack([np.sin(angle) * weight, np.cos(angle) * weight], axis=1)
    real, imag = (table.reshape(4, 512, HOP // 3) for table in (real, imag))
    table = np.concatenate([real[0], real[2], real[1], real[3], -imag[1], imag[3]])
    return table.reshape(-1, HOP // 3 // COLUMNS, COLUMNS).swapaxes(0, 1).astype(BF)


def inverse_kernel(core, mine, other, table, traces, energy, left, held, arrived):
    steps = table.shape[0]
    copies = [
        pltpu.make_async_copy(table.at[step], held.at[step], arrived.at[step])
        for step in range(steps)
    ]
    for copy in copies:
        copy.start()
    row = lax.broadcasted_iota(jnp.int32, (128, 256), 0)
    lane = lax.broadcasted_iota(jnp.int32, (128, 256), 1)
    half = lax.shift_right_logical(row, 4) & 1
    wanted = 128 * (half ^ core[0]) + 64 * core[0]
    wanted = wanted + 16 * lax.shift_right_logical(row, 5) + (row & 15)
    pick = jnp.where(lane == wanted, 1.0, 0.0).astype(BF)
    for i in range(16):
        rows = slice(8 * i, 8 * i + 8)
        block = jnp.concatenate([q[rows].reshape(128, 128) for q in (mine, other)], axis=1)
        chosen = lax.dot_general(pick, block, ROTATED, preferred_element_type=F32)
        left[:, 128 * i : 128 * i + 128] = chosen.astype(BF)
    dot = functools.partial(jnp.dot, preferred_element_type=F32)
    squares = jnp.zeros((32, 128), F32)
    for step, copy in enumerate(copies):
        copy.wait()
        first = dot(left[:, 0:512], held[step, 0:512])
        second = dot(left[:, 1024:1536], held[step, 512:1024])
        turn = []
        for part in (1024, 2048):
            low = dot(left[:, 512:1024], held[step, part : part + 512])
            turn.append(low + dot(left[:, 1536:2048], held[step, part + 512 : part + 1024]))
        both = first + second
        values = both + turn[0], first - second + turn[1], both - turn[0]
        for quarter, value in enumerate(values):
            for block in range(4):
                part = value[32 * block : 32 * block + 32]
                begin = block * HOP + quarter * (HOP // 3) + step * COLUMNS
                traces[:, begin : begin + COLUMNS] = part
                part = part * part
                for lane in range(0, COLUMNS, 128):
                    squares = squares + part[:, lane : lane + 128]
    energy[...] = jnp.sum(squares.T, axis=0, keepdims=True)


def inverse_traces(mine, other, core):
    table = inverse_table()
    vmem = pl.BlockSpec(memory_space=pltpu.VMEM)
    return pl.pallas_call(
        inverse_kernel,
        out_shape=(
            jax.ShapeDtypeStruct((32, 4 * HOP), F32),
            jax.ShapeDtypeStruct((1, 32), F32),
        ),
        in_specs=[pl.BlockSpec(memory_space=pltpu.SMEM), vmem, vmem, pl.BlockSpec(memory_space=pltpu.HBM)],
        out_specs=(vmem, vmem),
        scratch_shapes=[
            pltpu.VMEM((128, 2 * BAND), BF),
            pltpu.VMEM(table.shape, BF),
            pltpu.SemaphoreType.DMA((table.shape[0],)),
        ],
        compiler_params=pltpu.CompilerParams(vmem_limit_bytes=20 * 2**20),
    )(core.reshape(1), mine, other, jnp.asarray(table))


def split_store(upper, lower, source, rows, columns, value):
    high = value.astype(BF)
    upper[source, rows, columns] = high
    lower[source, rows, columns] = (value - high.astype(F32)).astype(BF)


def times(value, turns):
    real, imag = value
    cosine = math.cos(2.0 * math.pi * turns / POINTS)
    sine = math.sin(2.0 * math.pi * turns / POINTS)
    if turns == 0:
        return value
    if imag is None:
        return real * cosine, real * -sine
    return real * cosine + imag * sine, imag * cosine - real * sine


def sixteen_point(values):
    inner = []
    for a in range(4):
        x = values[a::4]
        even, odd = x[0] + x[2], x[1] + x[3]
        step = (x[0] - x[2], x[3] - x[1])
        inner.append([(even + odd, None), step, (even - odd, None), (step[0], -step[1])])
    sums = [None] * 9
    for low in range(4):
        v = [times(inner[a][low], (low * a) % POINTS) for a in range(4)]
        real = [part[0] for part in v]
        if low == 0:
            even, odd = real[0] + real[2], real[1] + real[3]
            sums[0], sums[8] = (even + odd, None), (even - odd, None)
            sums[4] = (real[0] - real[2], real[3] - real[1])
            continue
        imag = [jnp.zeros_like(real[0]) if part[1] is None else part[1] for part in v]
        even = (real[0] + real[2], imag[0] + imag[2])
        odd = (real[1] + real[3], imag[1] + imag[3])
        sums[low] = (even[0] + odd[0], even[1] + odd[1])
        even = (real[0] - real[2], imag[0] - imag[2])
        odd = (real[1] - real[3], imag[1] - imag[3])
        sums[low + 4] = (even[0] + odd[1], even[1] - odd[0])
    return sums


def source_places():
    return {group[0]: source for source, group in enumerate(sources())}


def forward_kernel(records, following, table, bank, out, upper, lower):
    out[:, 2 * BINS :, :] = bank[...]

    def mix(i, carry):
        rows = pl.ds(pl.multiple_of(16 * i, 16), 16)
        for start in range(0, SPAN, 128):
            values = []
            for a in range(POINTS):
                begin = SPAN * a + start
                part = records if begin < HOP else following
                begin = begin % HOP
                values.append(part[rows, begin : begin + 128].astype(F32))
            for residue, value in enumerate(sixteen_point(values)):
                source = source_places()[residue]
                for part in range(2):
                    if value[part] is not None:
                        columns = slice(SPAN * part + start, SPAN * part + start + 128)
                        split_store(upper, lower, source, rows, columns, value[part])
        return carry

    lax.fori_loop(0, 8, mix, 0)

    def sink(first, residue, total):
        out[first : first + BINS, : 2 * BINS] = total.astype(BF).reshape(BINS, 2 * BINS, 128)

    band_products(table, upper, lower, sink)


def bank_kernel(first, waveforms, lags, live, table, out, upper, lower):
    for i in range(4):
        rows = slice(SLOTS * i, SLOTS * i + SLOTS)
        wave = waveforms[first[0] + i].astype(F32)
        begin, end = wave[:, :SPAN], wave[:, SPAN:]
        for group in sources():
            source = source_places()[group[0]]
            cosine = math.cos(2.0 * math.pi * group[0] / POINTS)
            sine = math.sin(2.0 * math.pi * group[0] / POINTS)
            split_store(upper, lower, source, rows, slice(0, SPAN), begin + end * cosine)
            if len(group) == 2:
                split_store(upper, lower, source, rows, slice(SPAN, 2 * SPAN), end * -sine)
    turn = 2.0 * math.pi / NFFT
    lag = lags[...]
    fine = lax.broadcasted_iota(jnp.int32, (BINS * BINS, 128), 0) * POINTS
    fine = jnp.bitwise_and(fine * lag, NFFT - 1).astype(F32) * turn
    fine_cos, fine_sin = jnp.cos(fine), jnp.sin(fine)
    step = lax.broadcasted_iota(jnp.int32, (POINTS, 128), 0)
    step = jnp.bitwise_and(step * lag, NFFT - 1).astype(F32) * turn
    step_cos, step_sin = jnp.cos(step) * live[...], jnp.sin(step) * live[...]

    def sink(place, residue, total):
        total = total.reshape(BINS, 2, BINS, 128)
        base_real = total[:, 0].reshape(BINS * BINS, 128)
        base_imag = -total[:, 1].reshape(BINS * BINS, 128)
        low_cos, low_sin = (v[residue : residue + 1] for v in (step_cos, step_sin))
        cosine = fine_cos * low_cos - fine_sin * low_sin
        sine = fine_sin * low_cos + fine_cos * low_sin
        real = base_real * cosine - base_imag * sine
        imag = base_real * sine + base_imag * cosine
        both = [part.reshape(BINS, 1, BINS, 128) for part in (real, imag)]
        both = jnp.concatenate(both, axis=1).reshape(BINS, 2 * BINS, 128)
        out[place : place + BINS] = both.astype(BF)

    band_products(table, upper, lower, sink)


def spectra_call(kernel, rows, smem_count, operands):
    vmem = pl.BlockSpec(memory_space=pltpu.VMEM)
    smem = pl.BlockSpec(memory_space=pltpu.SMEM)
    return pl.pallas_call(
        kernel,
        out_shape=jax.ShapeDtypeStruct((SHARES, rows, 128), BF),
        in_specs=[smem] * smem_count + [vmem] * (len(operands) - smem_count),
        out_specs=vmem,
        scratch_shapes=[pltpu.VMEM((9, 128, 2 * SPAN), BF)] * 2,
        compiler_params=pltpu.CompilerParams(vmem_limit_bytes=24 * 2**20),
    )(*operands)


def forward_spectra(records, following, bank):
    operands = (records, following, jnp.asarray(band_table()), bank)
    return spectra_call(forward_kernel, 4 * BINS, 0, operands)


def bank_spectra(first, waveforms, lags, live):
    operands = (first.reshape(1), waveforms, lags, live, jnp.asarray(band_table()))
    return spectra_call(bank_kernel, 2 * BINS, 1, operands)


def swap_blocks(parts, lane):
    count = len(parts)
    size = 128 // count
    step = count // 2
    while step:
        low = (lane // (size * step)) % 2 == 0
        fresh = list(parts)
        for i in range(count):
            if i & step:
                continue
            j = i + step
            fresh[i] = jnp.where(low, parts[i], pltpu.roll(parts[j], size * step, 1))
            fresh[j] = jnp.where(low, pltpu.roll(parts[i], 128 - size * step, 1), parts[j])
        parts = fresh
        step //= 2
    return parts


def turned(unit, block):
    return lax.dot_general(unit[...], block, ROTATED, preferred_element_type=F32)


def weights_kernel(chunks, bank, spread, unit, weights, live, count):
    def expand(g, position):
        block = jnp.concatenate([bank[g * 8 + i] for i in range(8)], axis=0)
        compact = turned(unit, block).astype(BF)
        for i in range(4):
            wide = jnp.dot(compact, spread[i], preferred_element_type=F32)
            for j in range(2):
                first = (g * 8 + 2 * i + j) * 16
                part = wide[:, 128 * j : 128 * (j + 1)]
                weights[pl.ds(first, 16)] = part.reshape(16, 8, 128)
        for i in range(32):
            t = g * 32 + i
            for s in range(4):
                live[position + s] = t * 4 + s
            position = position + chunks[t]
        return position

    total = lax.fori_loop(0, 16, expand, 0)
    for s in range(UNROLL):
        live[total + s] = 2048
    weights[2048] = jnp.zeros((8, 128), F32)
    count[0] = total


def correlate_kernel(place, live, count, own, other, weights, unit, out, table, sums):
    for half, source in enumerate((own, other)):
        for y in range(4):
            start = half * 512 + y * 128
            for s in range(4):
                tiles = [source[(8 * s + i) * 4 + y] for i in range(8)]
                block = jnp.concatenate(tiles, axis=0)
                table[start : start + 128, s, :] = turned(unit, block)
                wide = [tile.astype(F32) for tile in tiles]
                swapped = [part for tile in wide for part in (tile[8:], tile[:8])]
                block = jnp.concatenate(swapped, axis=0).astype(BF)
                table[start : start + 128, 4 + s, :] = turned(unit, block)
    sums[...] = jnp.zeros_like(sums)

    def some_chunks(step, carry):
        for i in range(UNROLL):
            chunk = live[step * UNROLL + i]
            tile = weights[chunk]
            totals = [None, None]
            for u in range(8):
                row = table_rows(table, place[chunk * 8 + u])
                term = row * tile[u : u + 1]
                totals[u % 2] = term if u < 2 else totals[u % 2] + term
            t = lax.shift_right_logical(chunk, 2)
            sums[t] = sums[t] + (totals[0] + totals[1])
        return carry

    lax.fori_loop(0, lax.div(count[0] + UNROLL - 1, UNROLL), some_chunks, 0)

    lane = lax.broadcasted_iota(jnp.int32, (128, 128), 1)
    is_real = (lane // BINS) % 2 == 0
    for g in range(4):
        for y in range(4):
            first = sums[g * 128 : (g + 1) * 128, y, :]
            second = sums[g * 128 : (g + 1) * 128, 4 + y, :]
            real = first - pltpu.roll(first, 128 - BINS, 1)
            imag = second + pltpu.roll(second, BINS, 1)
            total = turned(unit, jnp.where(is_real, real, imag).astype(BF))
            parts = [total[16 * i : 16 * (i + 1)] for i in range(8)]
            for i, part in enumerate(swap_blocks(parts, lane[:16])):
                out[(8 * g + i) * 4 + y] = part.astype(BF)


def table_rows(table, first):
    rows = table.reshape(8192, 128)
    return rows[pl.ds(pl.multiple_of(first, 8), 8)]


def spread_table():
    lane = np.arange(128)
    one = np.zeros((2, BINS, 128))
    for part in range(2):
        one[part, lane % BINS, lane] = (lane // BINS) % 2 == part
    one = one.reshape(2 * BINS, 128)
    table = np.zeros((4, 8, 2 * BINS, 2, 128))
    for share in range(8):
        table[share // 2, share, :, share % 2] = one
    return table.reshape(4, 128, 256).astype(BF)


def correlate(place, chunks, own, other, bank):
    vmem = pl.BlockSpec(memory_space=pltpu.VMEM)
    smem = pl.BlockSpec(memory_space=pltpu.SMEM)
    unit = jnp.eye(128, dtype=BF)
    weights, live, count = pl.pallas_call(
        weights_kernel,
        out_shape=(
            jax.ShapeDtypeStruct((2049, 8, 128), F32),
            jax.ShapeDtypeStruct((2048 + 2 * UNROLL,), jnp.int32),
            jax.ShapeDtypeStruct((1,), jnp.int32),
        ),
        in_specs=[smem, vmem, vmem, vmem],
        out_specs=(vmem, smem, smem),
        compiler_params=pltpu.CompilerParams(vmem_limit_bytes=16 * 2**20),
        cost_estimate=pl.CostEstimate(flops=2**29, bytes_accessed=10**7, transcendentals=0),
    )(chunks, bank, jnp.asarray(spread_table()), unit)
    return pl.pallas_call(
        correlate_kernel,
        out_shape=jax.ShapeDtypeStruct((SHARES, 16, 128), BF),
        in_specs=[smem, smem, smem, vmem, vmem, vmem, vmem],
        out_specs=vmem,
        scratch_shapes=[
            pltpu.VMEM((1024, 8, 128), F32),
            pltpu.VMEM((513, 8, 128), F32),
        ],
        compiler_params=pltpu.CompilerParams(vmem_limit_bytes=22 * 2**20),
    )(place, live, count, own, other, weights, unit)


def on_device(records, waveforms, slot_channels, slot_counts, slot_lags):
    core = lax.axis_index("c")
    quarter = lax.axis_index("y")
    following = lax.ppermute(records[:, : NFFT - HOP], ("z", "x"), [(i, i - 1) for i in range(1, 32)])

    first = core * 16 + quarter * 4
    lags = lax.dynamic_slice_in_dim(slot_lags, first, 4, 0).reshape(1, 128)
    counts = lax.dynamic_slice_in_dim(slot_counts, first, 4, 0)
    channels = lax.dynamic_slice_in_dim(slot_channels, first, 4, 0).reshape(128)
    live = (jnp.arange(SLOTS, dtype=jnp.int32)[None] < counts[:, None]).reshape(128)
    bank = bank_spectra(first, waveforms, lags, live.astype(F32)[None])
    digits = jnp.stack([channels // 32 + jnp.where(live, 32, 0), channels % 32]).astype(BF)
    digits = jnp.broadcast_to(digits, (SHARES, 1, 2, 128))

    shares = forward_spectra(records, following, bank).reshape(SHARES, 16, 2, 128)
    shares = jnp.concatenate([shares, digits], axis=1)
    shares = lax.all_to_all(shares, ("z", "x", "y"), split_axis=0, concat_axis=0, tiled=True)
    own = shares[:, :8].reshape(SHARES, 2 * BINS, 128)
    bank = shares[:, 8:16].reshape(SHARES, 2 * BINS, 128)
    other = lax.ppermute(own, "c", [(0, 1), (1, 0)])
    digits = shares[:, 16].astype(jnp.int32)
    channels = (digits[:, 0] % 32) * 32 + digits[:, 1]
    home = channels // 128
    place = ((home % 2) ^ core) * 512 + (home // 2) * 128 + channels % 128
    place = jnp.pad(8 * place.reshape(512 * SLOTS), (0, 128))
    counts = jnp.sum((digits[:, 0] // 32).reshape(512, SLOTS), axis=1)
    chunks = (counts + 7) // 8
    correlated = correlate(place, chunks, own, other, bank)
    here = lax.all_to_all(correlated, ("z", "x", "y"), split_axis=0, concat_axis=0, tiled=True)
    there = lax.ppermute(here, "c", [(0, 1), (1, 0)])
    traces, energy = inverse_traces(here, there, core)
    energy = energy + lax.ppermute(energy, "c", [(0, 1), (1, 0)])
    shifts = [[(i, (i + d) % 4) for i in range(4)] for d in range(1, 4)]
    energy = sum((lax.ppermute(energy, "y", shift) for shift in shifts), energy)
    return traces * lax.rsqrt(energy / (32 * HOP) + EPS).reshape(32, 1)


def solution(mesh):
    fine = Mesh(mesh.devices.reshape(8, 4, 4, 2), ("z", "x", "y", "c"))
    tmpl, chan = ("z", "x"), ("y", "c")
    in_specs = (P(chan, tmpl), P(tmpl, None, None), P(tmpl, None), P(tmpl), P(tmpl, None))
    return jax.shard_map(
        on_device, mesh=fine, in_specs=in_specs, out_specs=P(tmpl, chan), check_vma=False
    )
```

```python
import functools
import math

import jax
import jax.numpy as jnp
import numpy as np
from jax import lax
from jax.experimental import pallas as pl
from jax.experimental.pallas import tpu as pltpu
from jax.sharding import Mesh
from jax.sharding import PartitionSpec as P

NFFT = 4096
BAND = 1024
HOP = 3072
SLOTS = 32
EPS = 1e-06
POINTS = 16
SPAN = NFFT // POINTS
ROTATED = (((1,), (1,)), ((), ()))
BINS = 8
SHARES = BAND // BINS
UNROLL = 16
COLUMNS = 256
BF = jnp.bfloat16
F32 = jnp.float32


def halves(matrix):
    upper = matrix.astype(BF)
    lower = (matrix - upper.astype(np.float64)).astype(BF)
    return upper, lower


def residues():
    place = np.arange(POINTS)
    return 4 * (place % 4) + place // 4


def share_bins():
    share = np.arange(SHARES)
    fine = BINS * (share % BINS)[:, None] + np.arange(BINS)[None, :]
    return POINTS * fine + residues()[share // BINS][:, None]


def sources():
    return [(0,), (8,)] + [(low, POINTS - low) for low in range(1, POINTS // 2)]


def band_table():
    samples = np.arange(SPAN)
    tables = []
    for group in sources():
        for residue in group:
            bins = POINTS * np.arange(BINS * BINS).reshape(BINS, BINS) + residue
            angle = 2.0 * np.pi * ((bins[..., None] * samples) % NFFT) / NFFT
            cosine, sine = np.cos(angle), np.sin(angle)
            sign = 1.0 if residue == group[0] else -1.0
            real = np.concatenate([cosine, sign * sine], axis=2)
            imag = np.concatenate([-sine, sign * cosine], axis=2)
            tables.append(np.stack([real, imag], axis=1).reshape(2 * BINS * BINS, 2 * SPAN))
    return np.stack(halves(np.stack(tables)))


def band_products(table, upper, lower, sink):
    order = list(residues())
    begin = 0
    for source, group in enumerate(sources()):
        depth = SPAN if len(group) == 1 else 2 * SPAN
        count = len(group)
        coarse, fine = (
            table[part, begin : begin + count, :, :depth].reshape(count * 128, depth)
            for part in range(2)
        )
        dot = functools.partial(
            lax.dot_general, dimension_numbers=ROTATED, preferred_element_type=F32
        )
        high, low = upper[source, :, :depth], lower[source, :, :depth]
        total = dot(coarse, high) + (dot(fine, high) + dot(coarse, low))
        for i, residue in enumerate(group):
            sink(BINS * order.index(residue), residue, total[128 * i : 128 * i + 128])
        begin += count


def inverse_table():
    bins = share_bins()
    angle = 2.0 * np.pi * ((bins[..., None] * np.arange(HOP // 3)) % NFFT) / NFFT
    weight = np.where(bins == 0, 1.0, 2.0)[..., None] / NFFT
    real = np.stack([np.cos(angle) * weight, -np.sin(angle) * weight], axis=1)
    imag = np.stack([np.sin(angle) * weight, np.cos(angle) * weight], axis=1)
    real, imag = (table.reshape(4, 512, HOP // 3) for table in (real, imag))
    table = np.concatenate([real[0], real[2], real[1], real[3], -imag[1], imag[3]])
    return table.reshape(-1, HOP // 3 // COLUMNS, COLUMNS).swapaxes(0, 1).astype(BF)


def inverse_kernel(core, mine, other, held, traces, energy, left):
    row = lax.broadcasted_iota(jnp.int32, (128, 256), 0)
    lane = lax.broadcasted_iota(jnp.int32, (128, 256), 1)
    half = lax.shift_right_logical(row, 4) & 1
    wanted = 128 * (half ^ core[0]) + 64 * core[0]
    wanted = wanted + 16 * lax.shift_right_logical(row, 5) + (row & 15)
    pick = jnp.where(lane == wanted, 1.0, 0.0).astype(BF)
    for i in range(16):
        rows = slice(8 * i, 8 * i + 8)
        block = jnp.concatenate([q[rows].reshape(128, 128) for q in (mine, other)], axis=1)
        chosen = lax.dot_general(pick, block, ROTATED, preferred_element_type=F32)
        left[:, 128 * i : 128 * i + 128] = chosen.astype(BF)
    dot = functools.partial(jnp.dot, preferred_element_type=F32)
    squares = jnp.zeros((32, 128), F32)
    for step in range(held.shape[0]):
        first = dot(left[:, 0:512], held[step, 0:512])
        second = dot(left[:, 1024:1536], held[step, 512:1024])
        turn = []
        for part in (1024, 2048):
            low = dot(left[:, 512:1024], held[step, part : part + 512])
            turn.append(low + dot(left[:, 1536:2048], held[step, part + 512 : part + 1024]))
        both = first + second
        values = both + turn[0], first - second + turn[1], both - turn[0]
        for quarter, value in enumerate(values):
            for block in range(4):
                part = value[32 * block : 32 * block + 32]
                begin = block * HOP + quarter * (HOP // 3) + step * COLUMNS
                traces[:, begin : begin + COLUMNS] = part
                part = part * part
                for lane in range(0, COLUMNS, 128):
                    squares = squares + part[:, lane : lane + 128]
    energy[...] = jnp.sum(squares.T, axis=0, keepdims=True)


def inverse_traces(mine, other, core, table):
    vmem = pl.BlockSpec(memory_space=pltpu.VMEM)
    return pl.pallas_call(
        inverse_kernel,
        out_shape=(
            jax.ShapeDtypeStruct((32, 4 * HOP), F32),
            jax.ShapeDtypeStruct((1, 32), F32),
        ),
        in_specs=[pl.BlockSpec(memory_space=pltpu.SMEM), vmem, vmem, vmem],
        out_specs=(vmem, vmem),
        scratch_shapes=[pltpu.VMEM((128, 2 * BAND), BF)],
        compiler_params=pltpu.CompilerParams(vmem_limit_bytes=20 * 2**20),
    )(core.reshape(1), mine, other, table)


def split_store(upper, lower, source, rows, columns, value):
    high = value.astype(BF)
    upper[source, rows, columns] = high
    lower[source, rows, columns] = (value - high.astype(F32)).astype(BF)


def times(value, turns):
    real, imag = value
    cosine = math.cos(2.0 * math.pi * turns / POINTS)
    sine = math.sin(2.0 * math.pi * turns / POINTS)
    if turns == 0:
        return value
    if imag is None:
        return real * cosine, real * -sine
    return real * cosine + imag * sine, imag * cosine - real * sine


def sixteen_point(values):
    inner = []
    for a in range(4):
        x = values[a::4]
        even, odd = x[0] + x[2], x[1] + x[3]
        step = (x[0] - x[2], x[3] - x[1])
        inner.append([(even + odd, None), step, (even - odd, None), (step[0], -step[1])])
    sums = [None] * 9
    for low in range(4):
        v = [times(inner[a][low], (low * a) % POINTS) for a in range(4)]
        real = [part[0] for part in v]
        if low == 0:
            even, odd = real[0] + real[2], real[1] + real[3]
            sums[0], sums[8] = (even + odd, None), (even - odd, None)
            sums[4] = (real[0] - real[2], real[3] - real[1])
            continue
        imag = [jnp.zeros_like(real[0]) if part[1] is None else part[1] for part in v]
        even = (real[0] + real[2], imag[0] + imag[2])
        odd = (real[1] + real[3], imag[1] + imag[3])
        sums[low] = (even[0] + odd[0], even[1] + odd[1])
        even = (real[0] - real[2], imag[0] - imag[2])
        odd = (real[1] - real[3], imag[1] - imag[3])
        sums[low + 4] = (even[0] + odd[1], even[1] - odd[0])
    return sums


def source_places():
    return {group[0]: source for source, group in enumerate(sources())}


def forward_kernel(records, following, table, out, upper, lower):

    def mix(i, carry):
        rows = pl.ds(pl.multiple_of(16 * i, 16), 16)
        for start in range(0, SPAN, 128):
            values = []
            for a in range(POINTS):
                begin = SPAN * a + start
                part = records if begin < HOP else following
                begin = begin % HOP
                values.append(part[rows, begin : begin + 128].astype(F32))
            for residue, value in enumerate(sixteen_point(values)):
                source = source_places()[residue]
                for part in range(2):
                    if value[part] is not None:
                        columns = slice(SPAN * part + start, SPAN * part + start + 128)
                        split_store(upper, lower, source, rows, columns, value[part])
        return carry

    lax.fori_loop(0, 8, mix, 0)

    def sink(first, residue, total):
        out[first : first + BINS] = total.astype(BF).reshape(BINS, 2 * BINS, 128)

    band_products(table, upper, lower, sink)


def bank_kernel(first, waveforms, lags, live, table, out, upper, lower):
    for i in range(4):
        rows = slice(SLOTS * i, SLOTS * i + SLOTS)
        wave = waveforms[first[0] + i].astype(F32)
        begin, end = wave[:, :SPAN], wave[:, SPAN:]
        for group in sources():
            source = source_places()[group[0]]
            cosine = math.cos(2.0 * math.pi * group[0] / POINTS)
            sine = math.sin(2.0 * math.pi * group[0] / POINTS)
            split_store(upper, lower, source, rows, slice(0, SPAN), begin + end * cosine)
            if len(group) == 2:
                split_store(upper, lower, source, rows, slice(SPAN, 2 * SPAN), end * -sine)
    turn = 2.0 * math.pi / NFFT
    lag = lags[...]
    fine = lax.broadcasted_iota(jnp.int32, (BINS * BINS, 128), 0) * POINTS
    fine = jnp.bitwise_and(fine * lag, NFFT - 1).astype(F32) * turn
    fine_cos, fine_sin = jnp.cos(fine), jnp.sin(fine)
    step = lax.broadcasted_iota(jnp.int32, (POINTS, 128), 0)
    step = jnp.bitwise_and(step * lag, NFFT - 1).astype(F32) * turn
    step_cos, step_sin = jnp.cos(step) * live[...], jnp.sin(step) * live[...]

    def sink(place, residue, total):
        total = total.reshape(BINS, 2, BINS, 128)
        base_real = total[:, 0].reshape(BINS * BINS, 128)
        base_imag = -total[:, 1].reshape(BINS * BINS, 128)
        low_cos, low_sin = (v[residue : residue + 1] for v in (step_cos, step_sin))
        cosine = fine_cos * low_cos - fine_sin * low_sin
        sine = fine_sin * low_cos + fine_cos * low_sin
        real = base_real * cosine - base_imag * sine
        imag = base_real * sine + base_imag * cosine
        both = [part.reshape(BINS, 1, BINS, 128) for part in (real, imag)]
        both = jnp.concatenate(both, axis=1).reshape(BINS, 2 * BINS, 128)
        out[place : place + BINS] = both.astype(BF)

    band_products(table, upper, lower, sink)


def spectra_call(kernel, smem_count, operands):
    vmem = pl.BlockSpec(memory_space=pltpu.VMEM)
    smem = pl.BlockSpec(memory_space=pltpu.SMEM)
    return pl.pallas_call(
        kernel,
        out_shape=jax.ShapeDtypeStruct((SHARES, 2 * BINS, 128), BF),
        in_specs=[smem] * smem_count + [vmem] * (len(operands) - smem_count),
        out_specs=vmem,
        scratch_shapes=[pltpu.VMEM((9, 128, 2 * SPAN), BF)] * 2,
        compiler_params=pltpu.CompilerParams(vmem_limit_bytes=24 * 2**20),
    )(*operands)


def forward_spectra(records, following):
    return spectra_call(forward_kernel, 0, (records, following, jnp.asarray(band_table())))


def bank_spectra(first, waveforms, lags, live):
    operands = (first.reshape(1), waveforms, lags, live, jnp.asarray(band_table()))
    return spectra_call(bank_kernel, 1, operands)


def swap_blocks(parts, lane):
    count = len(parts)
    size = 128 // count
    step = count // 2
    while step:
        low = (lane // (size * step)) % 2 == 0
        fresh = list(parts)
        for i in range(count):
            if i & step:
                continue
            j = i + step
            fresh[i] = jnp.where(low, parts[i], pltpu.roll(parts[j], size * step, 1))
            fresh[j] = jnp.where(low, pltpu.roll(parts[i], 128 - size * step, 1), parts[j])
        parts = fresh
        step //= 2
    return parts


def turned(unit, block):
    return lax.dot_general(unit[...], block, ROTATED, preferred_element_type=F32)


def weights_kernel(chunks, bank, spread, unit, later, weights, live, count, held, compact, landed):
    copy = pltpu.make_async_copy(later, held, landed)
    copy.start()
    for g in range(16):
        block = jnp.concatenate([bank[g * 8 + i] for i in range(8)], axis=0)
        compact[128 * g : 128 * g + 128, :] = turned(unit, block).astype(BF)

    def expand(g, position):
        rows = pl.ds(pl.multiple_of(256 * g, 256), 256)
        for i in range(4):
            wide = jnp.dot(compact[rows, :], spread[i], preferred_element_type=F32)
            for half in range(2):
                for j in range(2):
                    first = ((2 * g + half) * 8 + 2 * i + j) * 16
                    part = wide[128 * half : 128 * half + 128, 128 * j : 128 * j + 128]
                    weights[pl.ds(first, 16)] = part.reshape(16, 8, 128)
        for i in range(64):
            t = g * 64 + i
            for s in range(4):
                live[position + s] = t * 4 + s
            position = position + chunks[t]
        return position

    total = lax.fori_loop(0, 8, expand, 0)
    for s in range(UNROLL):
        live[total + s] = 2048
    weights[2048] = jnp.zeros((8, 128), F32)
    count[0] = total
    copy.wait()


def correlate_kernel(places, live, count, own, other, weights, unit, out, table, sums, place, landed):
    copy = pltpu.make_async_copy(places, place, landed)
    copy.start()
    lane = lax.broadcasted_iota(jnp.int32, (128, 128), 1)
    is_real = (lane // BINS) % 2 == 0
    for half, source in enumerate((own, other)):
        for y in range(4):
            start = half * 512 + y * 128
            for s in range(4):
                tiles = [source[(8 * s + i) * 4 + y] for i in range(8)]
                block = jnp.concatenate(tiles, axis=0)
                value = turned(unit, block)
                table[start : start + 128, s, :] = value
                ahead, behind = pltpu.roll(value, 128 - BINS, 1), pltpu.roll(value, BINS, 1)
                table[start : start + 128, 4 + s, :] = jnp.where(is_real, ahead, behind)
    sums[...] = jnp.zeros_like(sums)
    copy.wait()

    def some_chunks(step, carry):
        for i in range(UNROLL):
            chunk = live[step * UNROLL + i]
            tile = weights[chunk]
            totals = [None, None]
            for u in range(8):
                row = table_rows(table, place[chunk * 8 + u])
                term = row * tile[u : u + 1]
                totals[u % 2] = term if u < 2 else totals[u % 2] + term
            t = lax.shift_right_logical(chunk, 2)
            sums[t] = sums[t] + (totals[0] + totals[1])
        return carry

    lax.fori_loop(0, lax.div(count[0] + UNROLL - 1, UNROLL), some_chunks, 0)

    lane = lax.broadcasted_iota(jnp.int32, (128, 128), 1)
    is_real = (lane // BINS) % 2 == 0
    for g in range(4):
        for y in range(4):
            first = sums[g * 128 : (g + 1) * 128, y, :]
            second = sums[g * 128 : (g + 1) * 128, 4 + y, :]
            real = first - pltpu.roll(first, 128 - BINS, 1)
            imag = second + pltpu.roll(second, BINS, 1)
            total = turned(unit, jnp.where(is_real, real, imag).astype(BF))
            parts = [total[16 * i : 16 * (i + 1)] for i in range(8)]
            for i, part in enumerate(swap_blocks(parts, lane[:16])):
                out[(8 * g + i) * 4 + y] = part.astype(BF)


def table_rows(table, first):
    rows = table.reshape(8192, 128)
    return rows[pl.ds(pl.multiple_of(first, 8), 8)]


def spread_table():
    lane = np.arange(128)
    one = np.zeros((2, BINS, 128))
    for part in range(2):
        one[part, lane % BINS, lane] = (lane // BINS) % 2 == part
    one = one.reshape(2 * BINS, 128)
    table = np.zeros((4, 8, 2 * BINS, 2, 128))
    for share in range(8):
        table[share // 2, share, :, share % 2] = one
    return table.reshape(4, 128, 256).astype(BF)


def correlate(place, chunks, own, other, bank):
    vmem = pl.BlockSpec(memory_space=pltpu.VMEM)
    smem = pl.BlockSpec(memory_space=pltpu.SMEM)
    unit = jnp.eye(128, dtype=BF)
    later = inverse_table()
    weights, live, count, later = pl.pallas_call(
        weights_kernel,
        out_shape=(
            jax.ShapeDtypeStruct((2049, 8, 128), F32),
            jax.ShapeDtypeStruct((2048 + 2 * UNROLL,), jnp.int32),
            jax.ShapeDtypeStruct((1,), jnp.int32),
            jax.ShapeDtypeStruct(later.shape, BF),
        ),
        in_specs=[smem, vmem, vmem, vmem, pl.BlockSpec(memory_space=pltpu.HBM)],
        out_specs=(vmem, smem, smem, vmem),
        scratch_shapes=[pltpu.VMEM((2048, 128), BF), pltpu.SemaphoreType.DMA],
        compiler_params=pltpu.CompilerParams(vmem_limit_bytes=20 * 2**20),
        cost_estimate=pl.CostEstimate(flops=2**29, bytes_accessed=10**7, transcendentals=0),
    )(chunks, bank, jnp.asarray(spread_table()), unit, jnp.asarray(later))
    correlated = pl.pallas_call(
        correlate_kernel,
        out_shape=jax.ShapeDtypeStruct((SHARES, 16, 128), BF),
        in_specs=[pl.BlockSpec(memory_space=pl.ANY), smem, smem, vmem, vmem, vmem, vmem],
        out_specs=vmem,
        scratch_shapes=[
            pltpu.VMEM((1024, 8, 128), F32),
            pltpu.VMEM((513, 8, 128), F32),
            pltpu.SMEM(place.shape, jnp.int32),
            pltpu.SemaphoreType.DMA,
        ],
        compiler_params=pltpu.CompilerParams(vmem_limit_bytes=22 * 2**20),
    )(place, live, count, own, other, weights, unit)
    return correlated, later


def on_device(records, waveforms, slot_channels, slot_counts, slot_lags):
    core = lax.axis_index("c")
    quarter = lax.axis_index("y")
    following = lax.ppermute(records[:, : NFFT - HOP], ("z", "x"), [(i, i - 1) for i in range(1, 32)])

    first = core * 16 + quarter * 4
    lags = lax.dynamic_slice_in_dim(slot_lags, first, 4, 0).reshape(1, 128)
    counts = lax.dynamic_slice_in_dim(slot_counts, first, 4, 0)
    channels = lax.dynamic_slice_in_dim(slot_channels, first, 4, 0).reshape(128)
    live = (jnp.arange(SLOTS, dtype=jnp.int32)[None] < counts[:, None]).reshape(128)
    bank = bank_spectra(first, waveforms, lags, live.astype(F32)[None])
    digits = jnp.stack([channels // 32 + jnp.where(live, 32, 0), channels % 32]).astype(BF)
    digits = jnp.broadcast_to(digits, (SHARES, 1, 2, 128))

    rows = jnp.concatenate([bank.reshape(SHARES, 8, 2, 128), digits], axis=1)
    shares = lax.optimization_barrier(jnp.pad(rows, ((0, 0), (8, 0), (0, 0), (0, 0))))
    spectra = forward_spectra(records, following).reshape(SHARES, 8, 2, 128)
    shares = lax.dynamic_update_slice(shares, spectra, (0, 0, 0, 0))
    shares = lax.all_to_all(shares, ("z", "x", "y"), split_axis=0, concat_axis=0, tiled=True)
    own = shares[:, :8].reshape(SHARES, 2 * BINS, 128)
    bank = shares[:, 8:16].reshape(SHARES, 2 * BINS, 128)
    other = lax.ppermute(own, "c", [(0, 1), (1, 0)])
    digits = shares[:, 16].astype(jnp.int32)
    channels = (digits[:, 0] % 32) * 32 + digits[:, 1]
    home = channels // 128
    place = ((home % 2) ^ core) * 512 + (home // 2) * 128 + channels % 128
    place = jnp.pad(8 * place.reshape(512 * SLOTS), (0, 128))
    counts = jnp.sum((digits[:, 0] // 32).reshape(512, SLOTS), axis=1)
    chunks = (counts + 7) // 8
    correlated, later = correlate(place, chunks, own, other, bank)
    here = lax.all_to_all(correlated, ("z", "x", "y"), split_axis=0, concat_axis=0, tiled=True)
    there = lax.ppermute(here, "c", [(0, 1), (1, 0)])
    traces, energy = inverse_traces(here, there, core, later)
    energy = energy + lax.ppermute(energy, "c", [(0, 1), (1, 0)])
    shifts = [[(i, (i + d) % 4) for i in range(4)] for d in range(1, 4)]
    energy = sum((lax.ppermute(energy, "y", shift) for shift in shifts), energy)
    return traces * lax.rsqrt(energy / (32 * HOP) + EPS).reshape(32, 1)


def solution(mesh):
    fine = Mesh(mesh.devices.reshape(8, 4, 4, 2), ("z", "x", "y", "c"))
    tmpl, chan = ("z", "x"), ("y", "c")
    in_specs = (P(chan, tmpl), P(tmpl, None, None), P(tmpl, None), P(tmpl), P(tmpl, None))
    return jax.shard_map(
        on_device, mesh=fine, in_specs=in_specs, out_specs=P(tmpl, chan), check_vma=False
    )
```

```python
import functools
import math

import jax
import jax.numpy as jnp
import numpy as np
from jax import lax
from jax.experimental import pallas as pl
from jax.experimental.pallas import tpu as pltpu
from jax.sharding import Mesh
from jax.sharding import PartitionSpec as P

NFFT = 4096
BAND = 1024
HOP = 3072
SLOTS = 32
EPS = 1e-06
POINTS = 16
SPAN = NFFT // POINTS
ROTATED = (((1,), (1,)), ((), ()))
BINS = 8
SHARES = BAND // BINS
UNROLL = 16
COLUMNS = 256
BF = jnp.bfloat16
F32 = jnp.float32


def halves(matrix):
    upper = matrix.astype(BF)
    lower = (matrix - upper.astype(np.float64)).astype(BF)
    return upper, lower


def residues():
    place = np.arange(POINTS)
    return 4 * (place % 4) + place // 4


def share_bins():
    share = np.arange(SHARES)
    fine = BINS * (share % BINS)[:, None] + np.arange(BINS)[None, :]
    return POINTS * fine + residues()[share // BINS][:, None]


def sources():
    return [(0,), (8,)] + [(low, POINTS - low) for low in range(1, POINTS // 2)]


def band_table():
    samples = np.arange(SPAN)
    tables = []
    for group in sources():
        for residue in group:
            bins = POINTS * np.arange(BINS * BINS).reshape(BINS, BINS) + residue
            angle = 2.0 * np.pi * ((bins[..., None] * samples) % NFFT) / NFFT
            cosine, sine = np.cos(angle), np.sin(angle)
            sign = 1.0 if residue == group[0] else -1.0
            real = np.concatenate([cosine, sign * sine], axis=2)
            imag = np.concatenate([-sine, sign * cosine], axis=2)
            tables.append(np.stack([real, imag], axis=1).reshape(2 * BINS * BINS, 2 * SPAN))
    return np.stack(halves(np.stack(tables)))


def band_products(table, upper, lower, sink):
    order = list(residues())
    begin = 0
    for source, group in enumerate(sources()):
        depth = SPAN if len(group) == 1 else 2 * SPAN
        count = len(group)
        coarse, fine = (
            table[part, begin : begin + count, :, :depth].reshape(count * 128, depth)
            for part in range(2)
        )
        dot = functools.partial(
            lax.dot_general, dimension_numbers=ROTATED, preferred_element_type=F32
        )
        high, low = upper[source, :, :depth], lower[source, :, :depth]
        total = dot(coarse, high) + (dot(fine, high) + dot(coarse, low))
        for i, residue in enumerate(group):
            sink(BINS * order.index(residue), residue, total[128 * i : 128 * i + 128])
        begin += count


def inverse_table():
    bins = share_bins()
    angle = 2.0 * np.pi * ((bins[..., None] * np.arange(HOP // 3)) % NFFT) / NFFT
    weight = np.where(bins == 0, 1.0, 2.0)[..., None] / NFFT
    real = np.stack([np.cos(angle) * weight, -np.sin(angle) * weight], axis=1)
    imag = np.stack([np.sin(angle) * weight, np.cos(angle) * weight], axis=1)
    real, imag = (table.reshape(4, 512, HOP // 3) for table in (real, imag))
    table = np.concatenate([real[0], real[2], real[1], real[3], -imag[1], imag[3]])
    return table.reshape(-1, HOP // 3 // COLUMNS, COLUMNS).swapaxes(0, 1).astype(BF)


def inverse_kernel(core, mine, other, held, traces, energy, left):
    row = lax.broadcasted_iota(jnp.int32, (128, 256), 0)
    lane = lax.broadcasted_iota(jnp.int32, (128, 256), 1)
    half = lax.shift_right_logical(row, 4) & 1
    wanted = 128 * (half ^ core[0]) + 64 * core[0]
    wanted = wanted + 16 * lax.shift_right_logical(row, 5) + (row & 15)
    pick = jnp.where(lane == wanted, 1.0, 0.0).astype(BF)
    for i in range(16):
        rows = slice(8 * i, 8 * i + 8)
        block = jnp.concatenate([q[rows].reshape(128, 128) for q in (mine, other)], axis=1)
        chosen = lax.dot_general(pick, block, ROTATED, preferred_element_type=F32)
        left[:, 128 * i : 128 * i + 128] = chosen.astype(BF)
    dot = functools.partial(jnp.dot, preferred_element_type=F32)
    squares = jnp.zeros((32, 128), F32)
    for step in range(held.shape[0]):
        first = dot(left[:, 0:512], held[step, 0:512])
        second = dot(left[:, 1024:1536], held[step, 512:1024])
        turn = []
        for part in (1024, 2048):
            low = dot(left[:, 512:1024], held[step, part : part + 512])
            turn.append(low + dot(left[:, 1536:2048], held[step, part + 512 : part + 1024]))
        both = first + second
        values = both + turn[0], first - second + turn[1], both - turn[0]
        for quarter, value in enumerate(values):
            for block in range(4):
                part = value[32 * block : 32 * block + 32]
                begin = block * HOP + quarter * (HOP // 3) + step * COLUMNS
                traces[:, begin : begin + COLUMNS] = part
                part = part * part
                for lane in range(0, COLUMNS, 128):
                    squares = squares + part[:, lane : lane + 128]
    energy[...] = jnp.sum(squares.T, axis=0, keepdims=True)


def inverse_traces(mine, other, core):
    table = inverse_table()
    vmem = pl.BlockSpec(memory_space=pltpu.VMEM)
    return pl.pallas_call(
        inverse_kernel,
        out_shape=(
            jax.ShapeDtypeStruct((32, 4 * HOP), F32),
            jax.ShapeDtypeStruct((1, 32), F32),
        ),
        in_specs=[pl.BlockSpec(memory_space=pltpu.SMEM), vmem, vmem, vmem],
        out_specs=(vmem, vmem),
        scratch_shapes=[pltpu.VMEM((128, 2 * BAND), BF)],
        compiler_params=pltpu.CompilerParams(vmem_limit_bytes=20 * 2**20),
    )(core.reshape(1), mine, other, jnp.asarray(table))


def split_store(upper, lower, source, rows, columns, value):
    high = value.astype(BF)
    upper[source, rows, columns] = high
    lower[source, rows, columns] = (value - high.astype(F32)).astype(BF)


def times(value, turns):
    real, imag = value
    cosine = math.cos(2.0 * math.pi * turns / POINTS)
    sine = math.sin(2.0 * math.pi * turns / POINTS)
    if turns == 0:
        return value
    if imag is None:
        return real * cosine, real * -sine
    return real * cosine + imag * sine, imag * cosine - real * sine


def sixteen_point(values):
    inner = []
    for a in range(4):
        x = values[a::4]
        even, odd = x[0] + x[2], x[1] + x[3]
        step = (x[0] - x[2], x[3] - x[1])
        inner.append([(even + odd, None), step, (even - odd, None), (step[0], -step[1])])
    sums = [None] * 9
    for low in range(4):
        v = [times(inner[a][low], (low * a) % POINTS) for a in range(4)]
        real = [part[0] for part in v]
        if low == 0:
            even, odd = real[0] + real[2], real[1] + real[3]
            sums[0], sums[8] = (even + odd, None), (even - odd, None)
            sums[4] = (real[0] - real[2], real[3] - real[1])
            continue
        imag = [jnp.zeros_like(real[0]) if part[1] is None else part[1] for part in v]
        even = (real[0] + real[2], imag[0] + imag[2])
        odd = (real[1] + real[3], imag[1] + imag[3])
        sums[low] = (even[0] + odd[0], even[1] + odd[1])
        even = (real[0] - real[2], imag[0] - imag[2])
        odd = (real[1] - real[3], imag[1] - imag[3])
        sums[low + 4] = (even[0] + odd[1], even[1] - odd[0])
    return sums


def source_places():
    return {group[0]: source for source, group in enumerate(sources())}


def forward_kernel(records, following, table, out, upper, lower):

    def mix(i, carry):
        rows = pl.ds(pl.multiple_of(16 * i, 16), 16)
        for start in range(0, SPAN, 128):
            values = []
            for a in range(POINTS):
                begin = SPAN * a + start
                part = records if begin < HOP else following
                begin = begin % HOP
                values.append(part[rows, begin : begin + 128].astype(F32))
            for residue, value in enumerate(sixteen_point(values)):
                source = source_places()[residue]
                for part in range(2):
                    if value[part] is not None:
                        columns = slice(SPAN * part + start, SPAN * part + start + 128)
                        split_store(upper, lower, source, rows, columns, value[part])
        return carry

    lax.fori_loop(0, 8, mix, 0)

    def sink(first, residue, total):
        out[first : first + BINS] = total.astype(BF).reshape(BINS, 2 * BINS, 128)

    band_products(table, upper, lower, sink)


def bank_kernel(first, waveforms, lags, live, table, out, upper, lower):
    for i in range(4):
        rows = slice(SLOTS * i, SLOTS * i + SLOTS)
        wave = waveforms[first[0] + i].astype(F32)
        begin, end = wave[:, :SPAN], wave[:, SPAN:]
        for group in sources():
            source = source_places()[group[0]]
            cosine = math.cos(2.0 * math.pi * group[0] / POINTS)
            sine = math.sin(2.0 * math.pi * group[0] / POINTS)
            split_store(upper, lower, source, rows, slice(0, SPAN), begin + end * cosine)
            if len(group) == 2:
                split_store(upper, lower, source, rows, slice(SPAN, 2 * SPAN), end * -sine)
    turn = 2.0 * math.pi / NFFT
    lag = lags[...]
    fine = lax.broadcasted_iota(jnp.int32, (BINS * BINS, 128), 0) * POINTS
    fine = jnp.bitwise_and(fine * lag, NFFT - 1).astype(F32) * turn
    fine_cos, fine_sin = jnp.cos(fine), jnp.sin(fine)
    step = lax.broadcasted_iota(jnp.int32, (POINTS, 128), 0)
    step = jnp.bitwise_and(step * lag, NFFT - 1).astype(F32) * turn
    step_cos, step_sin = jnp.cos(step) * live[...], jnp.sin(step) * live[...]

    def sink(place, residue, total):
        total = total.reshape(BINS, 2, BINS, 128)
        base_real = total[:, 0].reshape(BINS * BINS, 128)
        base_imag = -total[:, 1].reshape(BINS * BINS, 128)
        low_cos, low_sin = (v[residue : residue + 1] for v in (step_cos, step_sin))
        cosine = fine_cos * low_cos - fine_sin * low_sin
        sine = fine_sin * low_cos + fine_cos * low_sin
        real = base_real * cosine - base_imag * sine
        imag = base_real * sine + base_imag * cosine
        both = [part.reshape(BINS, 1, BINS, 128) for part in (real, imag)]
        both = jnp.concatenate(both, axis=1).reshape(BINS, 2 * BINS, 128)
        out[place : place + BINS] = both.astype(BF)

    band_products(table, upper, lower, sink)


def spectra_call(kernel, operands, scalars=0):
    vmem = pl.BlockSpec(memory_space=pltpu.VMEM)
    smem = pl.BlockSpec(memory_space=pltpu.SMEM)
    return pl.pallas_call(
        kernel,
        out_shape=jax.ShapeDtypeStruct((SHARES, 2 * BINS, 128), BF),
        in_specs=[smem] * scalars + [vmem] * (len(operands) - scalars),
        out_specs=vmem,
        scratch_shapes=[pltpu.VMEM((9, 128, 2 * SPAN), BF)] * 2,
        compiler_params=pltpu.CompilerParams(vmem_limit_bytes=24 * 2**20),
    )(*operands)


def forward_spectra(records, following):
    return spectra_call(forward_kernel, (records, following, jnp.asarray(band_table())))


def bank_spectra(first, waveforms, lags, live):
    operands = (first.reshape(1), waveforms, lags, live, jnp.asarray(band_table()))
    return spectra_call(bank_kernel, operands, 1)


def swap_blocks(parts, lane):
    count = len(parts)
    size = 128 // count
    step = count // 2
    while step:
        low = (lane // (size * step)) % 2 == 0
        fresh = list(parts)
        for i in range(count):
            if i & step:
                continue
            j = i + step
            fresh[i] = jnp.where(low, parts[i], pltpu.roll(parts[j], size * step, 1))
            fresh[j] = jnp.where(low, pltpu.roll(parts[i], 128 - size * step, 1), parts[j])
        parts = fresh
        step //= 2
    return parts


def turned(unit, block):
    return lax.dot_general(unit[...], block, ROTATED, preferred_element_type=F32)


def weights_kernel(chunks, bank, spread, unit, weights, live, count, compact):
    for g in range(16):
        block = jnp.concatenate([bank[g * 8 + i] for i in range(8)], axis=0)
        compact[128 * g : 128 * g + 128, :] = turned(unit, block).astype(BF)

    def expand(g, position):
        rows = pl.ds(pl.multiple_of(256 * g, 256), 256)
        for i in range(4):
            wide = jnp.dot(compact[rows, :], spread[i], preferred_element_type=F32)
            for half in range(2):
                for j in range(2):
                    first = ((2 * g + half) * 8 + 2 * i + j) * 16
                    part = wide[128 * half : 128 * half + 128, 128 * j : 128 * j + 128]
                    weights[pl.ds(first, 16)] = part.reshape(16, 8, 128)
        for i in range(64):
            t = g * 64 + i
            for s in range(4):
                live[position + s] = t * 4 + s
            position = position + chunks[t]
        return position

    total = lax.fori_loop(0, 8, expand, 0)
    for s in range(UNROLL):
        live[total + s] = 2048
    weights[2048] = jnp.zeros((8, 128), F32)
    count[0] = total


def correlate_kernel(places, live, count, own, other, weights, unit, out, table, sums, place, landed):
    copy = pltpu.make_async_copy(places, place, landed)
    copy.start()
    lane = lax.broadcasted_iota(jnp.int32, (128, 128), 1)
    is_real = (lane // BINS) % 2 == 0
    for half, source in enumerate((own, other)):
        for y in range(4):
            start = half * 512 + y * 128
            for s in range(4):
                tiles = [source[(8 * s + i) * 4 + y] for i in range(8)]
                block = jnp.concatenate(tiles, axis=0)
                value = turned(unit, block)
                table[start : start + 128, s, :] = value
                ahead, behind = pltpu.roll(value, 128 - BINS, 1), pltpu.roll(value, BINS, 1)
                table[start : start + 128, 4 + s, :] = jnp.where(is_real, ahead, behind)
    sums[...] = jnp.zeros_like(sums)
    copy.wait()

    def some_chunks(step, carry):
        for i in range(UNROLL):
            chunk = live[step * UNROLL + i]
            tile = weights[chunk]
            totals = [None, None]
            for u in range(8):
                row = table_rows(table, place[chunk * 8 + u])
                term = row * tile[u : u + 1]
                totals[u % 2] = term if u < 2 else totals[u % 2] + term
            t = lax.shift_right_logical(chunk, 2)
            sums[t] = sums[t] + (totals[0] + totals[1])
        return carry

    lax.fori_loop(0, lax.div(count[0] + UNROLL - 1, UNROLL), some_chunks, 0)

    lane = lax.broadcasted_iota(jnp.int32, (128, 128), 1)
    is_real = (lane // BINS) % 2 == 0
    for g in range(4):
        for y in range(4):
            first = sums[g * 128 : (g + 1) * 128, y, :]
            second = sums[g * 128 : (g + 1) * 128, 4 + y, :]
            real = first - pltpu.roll(first, 128 - BINS, 1)
            imag = second + pltpu.roll(second, BINS, 1)
            total = turned(unit, jnp.where(is_real, real, imag).astype(BF)).astype(BF)
            parts = [total[16 * i : 16 * (i + 1)] for i in range(8)]
            for i, part in enumerate(swap_blocks(parts, lane[:16])):
                out[(8 * g + i) * 4 + y] = part


def table_rows(table, first):
    rows = table.reshape(8192, 128)
    return rows[pl.ds(pl.multiple_of(first, 8), 8)]


def spread_table():
    lane = np.arange(128)
    one = np.zeros((2, BINS, 128))
    for part in range(2):
        one[part, lane % BINS, lane] = (lane // BINS) % 2 == part
    one = one.reshape(2 * BINS, 128)
    table = np.zeros((4, 8, 2 * BINS, 2, 128))
    for share in range(8):
        table[share // 2, share, :, share % 2] = one
    return table.reshape(4, 128, 256).astype(BF)


def correlate(place, chunks, own, other, bank):
    vmem = pl.BlockSpec(memory_space=pltpu.VMEM)
    smem = pl.BlockSpec(memory_space=pltpu.SMEM)
    unit = jnp.eye(128, dtype=BF)
    weights, live, count = pl.pallas_call(
        weights_kernel,
        out_shape=(
            jax.ShapeDtypeStruct((2049, 8, 128), F32),
            jax.ShapeDtypeStruct((2048 + 2 * UNROLL,), jnp.int32),
            jax.ShapeDtypeStruct((1,), jnp.int32),
        ),
        in_specs=[smem, vmem, vmem, vmem],
        out_specs=(vmem, smem, smem),
        scratch_shapes=[pltpu.VMEM((2048, 128), BF)],
        compiler_params=pltpu.CompilerParams(vmem_limit_bytes=20 * 2**20),
        cost_estimate=pl.CostEstimate(flops=2**29, bytes_accessed=10**7, transcendentals=0),
    )(chunks, bank, jnp.asarray(spread_table()), unit)
    correlated = pl.pallas_call(
        correlate_kernel,
        out_shape=jax.ShapeDtypeStruct((SHARES, 16, 128), BF),
        in_specs=[pl.BlockSpec(memory_space=pl.ANY), smem, smem, vmem, vmem, vmem, vmem],
        out_specs=vmem,
        scratch_shapes=[
            pltpu.VMEM((1024, 8, 128), F32),
            pltpu.VMEM((513, 8, 128), F32),
            pltpu.SMEM(place.shape, jnp.int32),
            pltpu.SemaphoreType.DMA,
        ],
        compiler_params=pltpu.CompilerParams(vmem_limit_bytes=22 * 2**20),
    )(place, live, count, own, other, weights, unit)
    return correlated


def on_device(records, waveforms, slot_channels, slot_counts, slot_lags):
    core = lax.axis_index("c")
    quarter = lax.axis_index("y")
    following = lax.ppermute(records[:, : NFFT - HOP], ("z", "x"), [(i, i - 1) for i in range(1, 32)])

    first = core * 16 + quarter * 4
    lags = lax.dynamic_slice_in_dim(slot_lags, first, 4, 0).reshape(1, 128)
    counts = lax.dynamic_slice_in_dim(slot_counts, first, 4, 0)
    channels = lax.dynamic_slice_in_dim(slot_channels, first, 4, 0).reshape(128)
    live = (jnp.arange(SLOTS, dtype=jnp.int32)[None] < counts[:, None]).reshape(128)
    bank = bank_spectra(first, waveforms, lags, live.astype(F32)[None])
    digits = jnp.stack([channels // 32 + jnp.where(live, 32, 0), channels % 32]).astype(BF)
    digits = jnp.broadcast_to(digits, (SHARES, 1, 2, 128))

    rows = jnp.concatenate([bank.reshape(SHARES, 8, 2, 128), digits], axis=1)
    shares = lax.optimization_barrier(jnp.pad(rows, ((0, 0), (8, 0), (0, 0), (0, 0))))
    spectra = forward_spectra(records, following).reshape(SHARES, 8, 2, 128)
    shares = lax.dynamic_update_slice(shares, spectra, (0, 0, 0, 0))
    shares = lax.all_to_all(shares, ("z", "x", "y"), split_axis=0, concat_axis=0, tiled=True)
    own = shares[:, :8].reshape(SHARES, 2 * BINS, 128)
    bank = shares[:, 8:16].reshape(SHARES, 2 * BINS, 128)
    other = lax.ppermute(own, "c", [(0, 1), (1, 0)])
    digits = shares[:, 16].astype(jnp.int32)
    channels = (digits[:, 0] % 32) * 32 + digits[:, 1]
    home = channels // 128
    place = ((home % 2) ^ core) * 512 + (home // 2) * 128 + channels % 128
    place = jnp.pad(8 * place.reshape(512 * SLOTS), (0, 128))
    counts = jnp.sum((digits[:, 0] // 32).reshape(512, SLOTS), axis=1)
    chunks = (counts + 7) // 8
    correlated = correlate(place, chunks, own, other, bank)
    here = lax.all_to_all(correlated, ("z", "x", "y"), split_axis=0, concat_axis=0, tiled=True)
    there = lax.ppermute(here, "c", [(0, 1), (1, 0)])
    traces, energy = inverse_traces(here, there, core)
    energy = energy + lax.ppermute(energy, "c", [(0, 1), (1, 0)])
    shifts = [[(i, (i + d) % 4) for i in range(4)] for d in range(1, 4)]
    energy = sum((lax.ppermute(energy, "y", shift) for shift in shifts), energy)
    return traces * lax.rsqrt(energy / (32 * HOP) + EPS).reshape(32, 1)


def solution(mesh):
    fine = Mesh(mesh.devices.reshape(8, 4, 4, 2), ("z", "x", "y", "c"))
    tmpl, chan = ("z", "x"), ("y", "c")
    in_specs = (P(chan, tmpl), P(tmpl, None, None), P(tmpl, None), P(tmpl), P(tmpl, None))
    return jax.shard_map(
        on_device, mesh=fine, in_specs=in_specs, out_specs=P(tmpl, chan), check_vma=False
    )
```

```python
import functools
import math

import jax
import jax.numpy as jnp
import numpy as np
from jax import lax
from jax.experimental import pallas as pl
from jax.experimental.pallas import tpu as pltpu
from jax.sharding import Mesh
from jax.sharding import PartitionSpec as P

NFFT = 4096
BAND = 1024
HOP = 3072
SLOTS = 32
EPS = 1e-06
POINTS = 16
SPAN = NFFT // POINTS
ROTATED = (((1,), (1,)), ((), ()))
BINS = 8
SHARES = BAND // BINS
UNROLL = 16
COLUMNS = 256
BF = jnp.bfloat16
F32 = jnp.float32


def halves(matrix):
    upper = matrix.astype(BF)
    lower = (matrix - upper.astype(np.float64)).astype(BF)
    return upper, lower


def residues():
    place = np.arange(POINTS)
    return 4 * (place % 4) + place // 4


def share_bins():
    share = np.arange(SHARES)
    fine = BINS * (share % BINS)[:, None] + np.arange(BINS)[None, :]
    return POINTS * fine + residues()[share // BINS][:, None]


def sources():
    return [(0,), (8,)] + [(low, POINTS - low) for low in range(1, POINTS // 2)]


def band_table():
    samples = np.arange(SPAN)
    tables = []
    for group in sources():
        for residue in group:
            bins = POINTS * np.arange(BINS * BINS).reshape(BINS, BINS) + residue
            angle = 2.0 * np.pi * ((bins[..., None] * samples) % NFFT) / NFFT
            cosine, sine = np.cos(angle), np.sin(angle)
            sign = 1.0 if residue == group[0] else -1.0
            real = np.concatenate([cosine, sign * sine], axis=2)
            imag = np.concatenate([-sine, sign * cosine], axis=2)
            tables.append(np.stack([real, imag], axis=1).reshape(2 * BINS * BINS, 2 * SPAN))
    return np.stack(halves(np.stack(tables)))


def band_products(table, upper, lower, sink):
    order = list(residues())
    begin = 0
    for source, group in enumerate(sources()):
        depth = SPAN if len(group) == 1 else 2 * SPAN
        count = len(group)
        coarse, fine = (
            table[part, begin : begin + count, :, :depth].reshape(count * 128, depth)
            for part in range(2)
        )
        dot = functools.partial(
            lax.dot_general, dimension_numbers=ROTATED, preferred_element_type=F32
        )
        high, low = upper[source, :, :depth], lower[source, :, :depth]
        total = dot(coarse, high) + (dot(fine, high) + dot(coarse, low))
        for i, residue in enumerate(group):
            sink(BINS * order.index(residue), residue, total[128 * i : 128 * i + 128])
        begin += count


def inverse_table():
    bins = share_bins()
    angle = 2.0 * np.pi * ((bins[..., None] * np.arange(HOP // 3)) % NFFT) / NFFT
    weight = np.where(bins == 0, 1.0, 2.0)[..., None] / NFFT
    real = np.stack([np.cos(angle) * weight, -np.sin(angle) * weight], axis=1)
    imag = np.stack([np.sin(angle) * weight, np.cos(angle) * weight], axis=1)
    real, imag = (table.reshape(4, 512, HOP // 3) for table in (real, imag))
    table = np.concatenate([real[0], real[2], real[1], real[3], -imag[1], imag[3]])
    return table.reshape(-1, HOP // 3 // COLUMNS, COLUMNS).swapaxes(0, 1).astype(BF)


def inverse_kernel(core, mine, other, held, traces, energy, left):
    row = lax.broadcasted_iota(jnp.int32, (128, 256), 0)
    lane = lax.broadcasted_iota(jnp.int32, (128, 256), 1)
    half = lax.shift_right_logical(row, 4) & 1
    wanted = 128 * (half ^ core[0]) + 64 * core[0]
    wanted = wanted + 16 * lax.shift_right_logical(row, 5) + (row & 15)
    pick = jnp.where(lane == wanted, 1.0, 0.0).astype(BF)
    for i in range(16):
        rows = slice(8 * i, 8 * i + 8)
        block = jnp.concatenate([q[rows].reshape(128, 128) for q in (mine, other)], axis=1)
        chosen = lax.dot_general(pick, block, ROTATED, preferred_element_type=F32)
        left[:, 128 * i : 128 * i + 128] = chosen.astype(BF)
    dot = functools.partial(jnp.dot, preferred_element_type=F32)
    squares = jnp.zeros((32, 128), F32)
    for step in range(held.shape[0]):
        first = dot(left[:, 0:512], held[step, 0:512])
        second = dot(left[:, 1024:1536], held[step, 512:1024])
        turn = []
        for part in (1024, 2048):
            low = dot(left[:, 512:1024], held[step, part : part + 512])
            turn.append(low + dot(left[:, 1536:2048], held[step, part + 512 : part + 1024]))
        both = first + second
        values = both + turn[0], first - second + turn[1], both - turn[0]
        for quarter, value in enumerate(values):
            for block in range(4):
                part = value[32 * block : 32 * block + 32]
                begin = block * HOP + quarter * (HOP // 3) + step * COLUMNS
                traces[:, begin : begin + COLUMNS] = part
                part = part * part
                for lane in range(0, COLUMNS, 128):
                    squares = squares + part[:, lane : lane + 128]
    energy[...] = jnp.sum(squares.T, axis=0, keepdims=True)


def inverse_traces(mine, other, core):
    table = inverse_table()
    vmem = pl.BlockSpec(memory_space=pltpu.VMEM)
    return pl.pallas_call(
        inverse_kernel,
        out_shape=(
            jax.ShapeDtypeStruct((32, 4 * HOP), F32),
            jax.ShapeDtypeStruct((1, 32), F32),
        ),
        in_specs=[pl.BlockSpec(memory_space=pltpu.SMEM), vmem, vmem, vmem],
        out_specs=(vmem, vmem),
        scratch_shapes=[pltpu.VMEM((128, 2 * BAND), BF)],
        compiler_params=pltpu.CompilerParams(vmem_limit_bytes=20 * 2**20),
    )(core.reshape(1), mine, other, jnp.asarray(table))


def split_store(upper, lower, source, rows, columns, value):
    high = value.astype(BF)
    upper[source, rows, columns] = high
    lower[source, rows, columns] = (value - high.astype(F32)).astype(BF)


def times(value, turns):
    real, imag = value
    cosine = math.cos(2.0 * math.pi * turns / POINTS)
    sine = math.sin(2.0 * math.pi * turns / POINTS)
    if turns == 0:
        return value
    if imag is None:
        return real * cosine, real * -sine
    return real * cosine + imag * sine, imag * cosine - real * sine


def sixteen_point(values):
    inner = []
    for a in range(4):
        x = values[a::4]
        even, odd = x[0] + x[2], x[1] + x[3]
        step = (x[0] - x[2], x[3] - x[1])
        inner.append([(even + odd, None), step, (even - odd, None), (step[0], -step[1])])
    sums = [None] * 9
    for low in range(4):
        v = [times(inner[a][low], (low * a) % POINTS) for a in range(4)]
        real = [part[0] for part in v]
        if low == 0:
            even, odd = real[0] + real[2], real[1] + real[3]
            sums[0], sums[8] = (even + odd, None), (even - odd, None)
            sums[4] = (real[0] - real[2], real[3] - real[1])
            continue
        imag = [jnp.zeros_like(real[0]) if part[1] is None else part[1] for part in v]
        even = (real[0] + real[2], imag[0] + imag[2])
        odd = (real[1] + real[3], imag[1] + imag[3])
        sums[low] = (even[0] + odd[0], even[1] + odd[1])
        even = (real[0] - real[2], imag[0] - imag[2])
        odd = (real[1] - real[3], imag[1] - imag[3])
        sums[low + 4] = (even[0] + odd[1], even[1] - odd[0])
    return sums


def source_places():
    return {group[0]: source for source, group in enumerate(sources())}


def forward_kernel(records, following, table, out, upper, lower):

    def mix(i, carry):
        rows = pl.ds(pl.multiple_of(16 * i, 16), 16)
        for start in range(0, SPAN, 128):
            values = []
            for a in range(POINTS):
                begin = SPAN * a + start
                part = records if begin < HOP else following
                begin = begin % HOP
                values.append(part[rows, begin : begin + 128].astype(F32))
            for residue, value in enumerate(sixteen_point(values)):
                source = source_places()[residue]
                for part in range(2):
                    if value[part] is not None:
                        columns = slice(SPAN * part + start, SPAN * part + start + 128)
                        split_store(upper, lower, source, rows, columns, value[part])
        return carry

    lax.fori_loop(0, 8, mix, 0)

    def sink(first, residue, total):
        out[first : first + BINS] = total.astype(BF).reshape(BINS, 2 * BINS, 128)

    band_products(table, upper, lower, sink)


def bank_kernel(first, waveforms, lags, live, table, out, upper, lower):
    for i in range(4):
        rows = slice(SLOTS * i, SLOTS * i + SLOTS)
        wave = waveforms[first[0] + i].astype(F32)
        begin, end = wave[:, :SPAN], wave[:, SPAN:]
        for group in sources():
            source = source_places()[group[0]]
            cosine = math.cos(2.0 * math.pi * group[0] / POINTS)
            sine = math.sin(2.0 * math.pi * group[0] / POINTS)
            split_store(upper, lower, source, rows, slice(0, SPAN), begin + end * cosine)
            if len(group) == 2:
                split_store(upper, lower, source, rows, slice(SPAN, 2 * SPAN), end * -sine)
    turn = 2.0 * math.pi / NFFT
    lag = lags[...]
    fine = lax.broadcasted_iota(jnp.int32, (BINS * BINS, 128), 0) * POINTS
    fine = jnp.bitwise_and(fine * lag, NFFT - 1).astype(F32) * turn
    fine_cos, fine_sin = jnp.cos(fine), jnp.sin(fine)
    step = lax.broadcasted_iota(jnp.int32, (POINTS, 128), 0)
    step = jnp.bitwise_and(step * lag, NFFT - 1).astype(F32) * turn
    step_cos, step_sin = jnp.cos(step) * live[...], jnp.sin(step) * live[...]

    def sink(place, residue, total):
        total = total.reshape(BINS, 2, BINS, 128)
        base_real = total[:, 0].reshape(BINS * BINS, 128)
        base_imag = -total[:, 1].reshape(BINS * BINS, 128)
        low_cos, low_sin = (v[residue : residue + 1] for v in (step_cos, step_sin))
        cosine = fine_cos * low_cos - fine_sin * low_sin
        sine = fine_sin * low_cos + fine_cos * low_sin
        real = base_real * cosine - base_imag * sine
        imag = base_real * sine + base_imag * cosine
        both = [part.reshape(BINS, 1, BINS, 128) for part in (real, imag)]
        both = jnp.concatenate(both, axis=1).reshape(BINS, 2 * BINS, 128)
        out[place : place + BINS] = both.astype(BF)

    band_products(table, upper, lower, sink)


def spectra_call(kernel, operands, scalars=0):
    vmem = pl.BlockSpec(memory_space=pltpu.VMEM)
    smem = pl.BlockSpec(memory_space=pltpu.SMEM)
    return pl.pallas_call(
        kernel,
        out_shape=jax.ShapeDtypeStruct((SHARES, 2 * BINS, 128), BF),
        in_specs=[smem] * scalars + [vmem] * (len(operands) - scalars),
        out_specs=vmem,
        scratch_shapes=[pltpu.VMEM((9, 128, 2 * SPAN), BF)] * 2,
        compiler_params=pltpu.CompilerParams(vmem_limit_bytes=24 * 2**20),
    )(*operands)


def forward_spectra(records, following):
    return spectra_call(forward_kernel, (records, following, jnp.asarray(band_table())))


def bank_spectra(first, waveforms, lags, live):
    operands = (first.reshape(1), waveforms, lags, live, jnp.asarray(band_table()))
    return spectra_call(bank_kernel, operands, 1)


def swap_blocks(parts, lane):
    count = len(parts)
    size = 128 // count
    step = count // 2
    while step:
        low = (lane // (size * step)) % 2 == 0
        fresh = list(parts)
        for i in range(count):
            if i & step:
                continue
            j = i + step
            fresh[i] = jnp.where(low, parts[i], pltpu.roll(parts[j], size * step, 1))
            fresh[j] = jnp.where(low, pltpu.roll(parts[i], 128 - size * step, 1), parts[j])
        parts = fresh
        step //= 2
    return parts


def arrival(z, x, y):
    return (y * 4 + x) * 8 + z


def turned(unit, block):
    return lax.dot_general(unit[...], block, ROTATED, preferred_element_type=F32)


def weights_kernel(chunks, bank, spread, unit, weights, live, count, compact):
    for g in range(16):
        block = jnp.concatenate([bank[g * 8 + i] for i in range(8)], axis=0)
        compact[128 * g : 128 * g + 128, :] = turned(unit, block).astype(BF)

    def expand(g, position):
        rows = pl.ds(pl.multiple_of(256 * g, 256), 256)
        for i in range(4):
            wide = jnp.dot(compact[rows, :], spread[i], preferred_element_type=F32)
            for half in range(2):
                for j in range(2):
                    first = ((2 * g + half) * 8 + 2 * i + j) * 16
                    part = wide[128 * half : 128 * half + 128, 128 * j : 128 * j + 128]
                    weights[pl.ds(first, 16)] = part.reshape(16, 8, 128)
        base = (g & 1) * 256 + lax.shift_right_logical(g, 1) * 4
        for i in range(64):
            t = g * 64 + i
            target = base + (i // 4) * 16 + i % 4
            for s in range(4):
                live[position + s] = target * 4096 + (t * 4 + s)
            position = position + chunks[t]
        return position

    total = lax.fori_loop(0, 8, expand, 0)
    for s in range(UNROLL):
        live[total + s] = 512 * 4096 + 2048
    weights[2048] = jnp.zeros((8, 128), F32)
    count[0] = total


def correlate_kernel(places, live, count, own, other, weights, unit, out, table, sums, place, landed):
    copy = pltpu.make_async_copy(places, place, landed)
    copy.start()
    lane = lax.broadcasted_iota(jnp.int32, (128, 128), 1)
    is_real = (lane // BINS) % 2 == 0
    for half, source in enumerate((own, other)):
        for y in range(4):
            start = half * 512 + y * 128
            for s in range(4):
                blocks = [8 * s + i for i in range(8)]
                tiles = [source[arrival(b // 4, b % 4, y)] for b in blocks]
                block = jnp.concatenate(tiles, axis=0)
                value = turned(unit, block)
                table[start : start + 128, s, :] = value
                ahead, behind = pltpu.roll(value, 128 - BINS, 1), pltpu.roll(value, BINS, 1)
                table[start : start + 128, 4 + s, :] = jnp.where(is_real, ahead, behind)
    sums[...] = jnp.zeros_like(sums)
    copy.wait()

    def some_chunks(step, carry):
        for i in range(UNROLL):
            entry = live[step * UNROLL + i]
            chunk = entry & 4095
            tile = weights[chunk]
            totals = [None, None]
            for u in range(8):
                row = table_rows(table, place[chunk * 8 + u])
                term = row * tile[u : u + 1]
                totals[u % 2] = term if u < 2 else totals[u % 2] + term
            t = lax.shift_right_logical(entry, 12)
            sums[t] = sums[t] + (totals[0] + totals[1])
        return carry

    lax.fori_loop(0, lax.div(count[0] + UNROLL - 1, UNROLL), some_chunks, 0)

    lane = lax.broadcasted_iota(jnp.int32, (128, 128), 1)
    is_real = (lane // BINS) % 2 == 0
    for g in range(4):
        for y in range(4):
            first = sums[g * 128 : (g + 1) * 128, y, :]
            second = sums[g * 128 : (g + 1) * 128, 4 + y, :]
            real = first - pltpu.roll(first, 128 - BINS, 1)
            imag = second + pltpu.roll(second, BINS, 1)
            total = turned(unit, jnp.where(is_real, real, imag).astype(BF)).astype(BF)
            parts = [total[16 * i : 16 * (i + 1)] for i in range(8)]
            for i, part in enumerate(swap_blocks(parts, lane[:16])):
                out[arrival(i, g, y)] = part


def table_rows(table, first):
    rows = table.reshape(8192, 128)
    return rows[pl.ds(pl.multiple_of(first, 8), 8)]


def spread_table():
    lane = np.arange(128)
    one = np.zeros((2, BINS, 128))
    for part in range(2):
        one[part, lane % BINS, lane] = (lane // BINS) % 2 == part
    one = one.reshape(2 * BINS, 128)
    table = np.zeros((4, 8, 2 * BINS, 2, 128))
    for share in range(8):
        table[share // 2, share, :, share % 2] = one
    return table.reshape(4, 128, 256).astype(BF)


def correlate(place, chunks, own, other, bank):
    vmem = pl.BlockSpec(memory_space=pltpu.VMEM)
    smem = pl.BlockSpec(memory_space=pltpu.SMEM)
    unit = jnp.eye(128, dtype=BF)
    weights, live, count = pl.pallas_call(
        weights_kernel,
        out_shape=(
            jax.ShapeDtypeStruct((2049, 8, 128), F32),
            jax.ShapeDtypeStruct((2048 + 2 * UNROLL,), jnp.int32),
            jax.ShapeDtypeStruct((1,), jnp.int32),
        ),
        in_specs=[smem, vmem, vmem, vmem],
        out_specs=(vmem, smem, smem),
        scratch_shapes=[pltpu.VMEM((2048, 128), BF)],
        compiler_params=pltpu.CompilerParams(vmem_limit_bytes=20 * 2**20),
        cost_estimate=pl.CostEstimate(flops=2**29, bytes_accessed=10**7, transcendentals=0),
    )(chunks, bank, jnp.asarray(spread_table()), unit)
    correlated = pl.pallas_call(
        correlate_kernel,
        out_shape=jax.ShapeDtypeStruct((SHARES, 16, 128), BF),
        in_specs=[pl.BlockSpec(memory_space=pl.ANY), smem, smem, vmem, vmem, vmem, vmem],
        out_specs=vmem,
        scratch_shapes=[
            pltpu.VMEM((1024, 8, 128), F32),
            pltpu.VMEM((513, 8, 128), F32),
            pltpu.SMEM(place.shape, jnp.int32),
            pltpu.SemaphoreType.DMA,
        ],
        compiler_params=pltpu.CompilerParams(vmem_limit_bytes=22 * 2**20),
    )(place, live, count, own, other, weights, unit)
    return correlated


def on_device(records, waveforms, slot_channels, slot_counts, slot_lags):
    core = lax.axis_index("c")
    quarter = lax.axis_index("y")
    following = lax.ppermute(records[:, : NFFT - HOP], ("z", "x"), [(i, i - 1) for i in range(1, 32)])

    first = core * 16 + quarter * 4
    lags = lax.dynamic_slice_in_dim(slot_lags, first, 4, 0).reshape(1, 128)
    counts = lax.dynamic_slice_in_dim(slot_counts, first, 4, 0)
    channels = lax.dynamic_slice_in_dim(slot_channels, first, 4, 0).reshape(128)
    live = (jnp.arange(SLOTS, dtype=jnp.int32)[None] < counts[:, None]).reshape(128)
    bank = bank_spectra(first, waveforms, lags, live.astype(F32)[None])
    digits = jnp.stack([channels // 32 + jnp.where(live, 32, 0), channels % 32]).astype(BF)
    digits = jnp.broadcast_to(digits, (SHARES, 1, 2, 128))

    rows = jnp.concatenate([bank.reshape(SHARES, 8, 2, 128), digits], axis=1)
    shares = lax.optimization_barrier(jnp.pad(rows, ((0, 0), (8, 0), (0, 0), (0, 0))))
    spectra = forward_spectra(records, following).reshape(SHARES, 8, 2, 128)
    shares = lax.dynamic_update_slice(shares, spectra, (0, 0, 0, 0))
    shares = lax.all_to_all(shares, ("y", "x", "z"), split_axis=0, concat_axis=0, tiled=True)
    own = shares[:, :8].reshape(SHARES, 2 * BINS, 128)
    bank = shares[:, 8:16].reshape(SHARES, 2 * BINS, 128)
    other = lax.ppermute(own, "c", [(0, 1), (1, 0)])
    digits = shares[:, 16].astype(jnp.int32)
    channels = (digits[:, 0] % 32) * 32 + digits[:, 1]
    home = channels // 128
    place = ((home % 2) ^ core) * 512 + (home // 2) * 128 + channels % 128
    place = jnp.pad(8 * place.reshape(512 * SLOTS), (0, 128))
    counts = jnp.sum((digits[:, 0] // 32).reshape(512, SLOTS), axis=1)
    chunks = (counts + 7) // 8
    correlated = correlate(place, chunks, own, other, bank)
    here = lax.all_to_all(correlated, ("y", "x", "z"), split_axis=0, concat_axis=0, tiled=True)
    there = lax.ppermute(here, "c", [(0, 1), (1, 0)])
    traces, energy = inverse_traces(here, there, core)
    energy = energy + lax.ppermute(energy, "c", [(0, 1), (1, 0)])
    shifts = [[(i, (i + d) % 4) for i in range(4)] for d in range(1, 4)]
    energy = sum((lax.ppermute(energy, "y", shift) for shift in shifts), energy)
    return traces * lax.rsqrt(energy / (32 * HOP) + EPS).reshape(32, 1)


def solution(mesh):
    fine = Mesh(mesh.devices.reshape(8, 4, 4, 2), ("z", "x", "y", "c"))
    tmpl, chan = ("z", "x"), ("y", "c")
    in_specs = (P(chan, tmpl), P(tmpl, None, None), P(tmpl, None), P(tmpl), P(tmpl, None))
    return jax.shard_map(
        on_device, mesh=fine, in_specs=in_specs, out_specs=P(tmpl, chan), check_vma=False
    )
```

```python
import functools
import math

import jax
import jax.numpy as jnp
import numpy as np
from jax import lax
from jax.experimental import pallas as pl
from jax.experimental.pallas import tpu as pltpu
from jax.sharding import Mesh
from jax.sharding import PartitionSpec as P

NFFT = 4096
BAND = 1024
HOP = 3072
SLOTS = 32
EPS = 1e-06
POINTS = 16
SPAN = NFFT // POINTS
ROTATED = (((1,), (1,)), ((), ()))
BINS = 8
SHARES = BAND // BINS
UNROLL = 16
COLUMNS = 256
BF = jnp.bfloat16
F32 = jnp.float32


def halves(matrix):
    upper = matrix.astype(BF)
    lower = (matrix - upper.astype(np.float64)).astype(BF)
    return upper, lower


def residues():
    place = np.arange(POINTS)
    return 4 * (place % 4) + place // 4


def share_bins():
    share = np.arange(SHARES)
    fine = BINS * (share % BINS)[:, None] + np.arange(BINS)[None, :]
    return POINTS * fine + residues()[share // BINS][:, None]


def sources():
    return [(0,), (8,)] + [(low, POINTS - low) for low in range(1, POINTS // 2)]


def band_table():
    samples = np.arange(SPAN)
    tables = []
    for group in sources():
        for residue in group:
            bins = POINTS * np.arange(BINS * BINS).reshape(BINS, BINS) + residue
            angle = 2.0 * np.pi * ((bins[..., None] * samples) % NFFT) / NFFT
            cosine, sine = np.cos(angle), np.sin(angle)
            sign = 1.0 if residue == group[0] else -1.0
            real = np.concatenate([cosine, sign * sine], axis=2)
            imag = np.concatenate([-sine, sign * cosine], axis=2)
            tables.append(np.stack([real, imag], axis=1).reshape(2 * BINS * BINS, 2 * SPAN))
    return np.stack(halves(np.stack(tables)))


def band_products(table, upper, lower, sink):
    order = list(residues())
    begin = 0
    for source, group in enumerate(sources()):
        depth = SPAN if len(group) == 1 else 2 * SPAN
        count = len(group)
        coarse, fine = (
            table[part, begin : begin + count, :, :depth].reshape(count * 128, depth)
            for part in range(2)
        )
        dot = functools.partial(
            lax.dot_general, dimension_numbers=ROTATED, preferred_element_type=F32
        )
        high, low = upper[source, :, :depth], lower[source, :, :depth]
        total = dot(coarse, high) + (dot(fine, high) + dot(coarse, low))
        for i, residue in enumerate(group):
            sink(BINS * order.index(residue), residue, total[128 * i : 128 * i + 128])
        begin += count


def inverse_table():
    bins = share_bins()
    angle = 2.0 * np.pi * ((bins[..., None] * np.arange(HOP // 3)) % NFFT) / NFFT
    weight = np.where(bins == 0, 1.0, 2.0)[..., None] / NFFT
    real = np.stack([np.cos(angle) * weight, -np.sin(angle) * weight], axis=1)
    imag = np.stack([np.sin(angle) * weight, np.cos(angle) * weight], axis=1)
    real, imag = (table.reshape(4, 512, HOP // 3) for table in (real, imag))
    table = np.concatenate([real[0], real[2], real[1], real[3], -imag[1], imag[3]])
    return table.reshape(-1, HOP // 3 // COLUMNS, COLUMNS).swapaxes(0, 1).astype(BF)


def inverse_kernel(core, mine, other, held, traces, energy, left):
    row = lax.broadcasted_iota(jnp.int32, (128, 256), 0)
    lane = lax.broadcasted_iota(jnp.int32, (128, 256), 1)
    half = lax.shift_right_logical(row, 4) & 1
    wanted = 128 * (half ^ core[0]) + 64 * core[0]
    wanted = wanted + 16 * lax.shift_right_logical(row, 5) + (row & 15)
    pick = jnp.where(lane == wanted, 1.0, 0.0).astype(BF)
    for i in range(16):
        rows = slice(8 * i, 8 * i + 8)
        block = jnp.concatenate([q[rows].reshape(128, 128) for q in (mine, other)], axis=1)
        chosen = lax.dot_general(pick, block, ROTATED, preferred_element_type=F32)
        left[:, 128 * i : 128 * i + 128] = chosen.astype(BF)
    dot = functools.partial(jnp.dot, preferred_element_type=F32)
    squares = jnp.zeros((32, 128), F32)
    for step in range(held.shape[0]):
        first = dot(left[:, 0:512], held[step, 0:512])
        second = dot(left[:, 1024:1536], held[step, 512:1024])
        turn = []
        for part in (1024, 2048):
            low = dot(left[:, 512:1024], held[step, part : part + 512])
            turn.append(low + dot(left[:, 1536:2048], held[step, part + 512 : part + 1024]))
        both = first + second
        values = both + turn[0], first - second + turn[1], both - turn[0]
        for quarter, value in enumerate(values):
            for block in range(4):
                part = value[32 * block : 32 * block + 32]
                begin = block * HOP + quarter * (HOP // 3) + step * COLUMNS
                traces[:, begin : begin + COLUMNS] = part
                part = part * part
                for lane in range(0, COLUMNS, 128):
                    squares = squares + part[:, lane : lane + 128]
    energy[...] = jnp.sum(squares.T, axis=0, keepdims=True)


def inverse_traces(mine, other, core):
    table = inverse_table()
    vmem = pl.BlockSpec(memory_space=pltpu.VMEM)
    return pl.pallas_call(
        inverse_kernel,
        out_shape=(
            jax.ShapeDtypeStruct((32, 4 * HOP), F32),
            jax.ShapeDtypeStruct((1, 32), F32),
        ),
        in_specs=[pl.BlockSpec(memory_space=pltpu.SMEM), vmem, vmem, vmem],
        out_specs=(vmem, vmem),
        scratch_shapes=[pltpu.VMEM((128, 2 * BAND), BF)],
        compiler_params=pltpu.CompilerParams(vmem_limit_bytes=20 * 2**20),
    )(core.reshape(1), mine, other, jnp.asarray(table))


def split_store(upper, lower, source, rows, columns, value):
    high = value.astype(BF)
    upper[source, rows, columns] = high
    lower[source, rows, columns] = (value - high.astype(F32)).astype(BF)


def times(value, turns):
    real, imag = value
    cosine = math.cos(2.0 * math.pi * turns / POINTS)
    sine = math.sin(2.0 * math.pi * turns / POINTS)
    if turns == 0:
        return value
    if imag is None:
        return real * cosine, real * -sine
    return real * cosine + imag * sine, imag * cosine - real * sine


def sixteen_point(values):
    inner = []
    for a in range(4):
        x = values[a::4]
        even, odd = x[0] + x[2], x[1] + x[3]
        step = (x[0] - x[2], x[3] - x[1])
        inner.append([(even + odd, None), step, (even - odd, None), (step[0], -step[1])])
    sums = [None] * 9
    for low in range(4):
        v = [times(inner[a][low], (low * a) % POINTS) for a in range(4)]
        real = [part[0] for part in v]
        if low == 0:
            even, odd = real[0] + real[2], real[1] + real[3]
            sums[0], sums[8] = (even + odd, None), (even - odd, None)
            sums[4] = (real[0] - real[2], real[3] - real[1])
            continue
        imag = [jnp.zeros_like(real[0]) if part[1] is None else part[1] for part in v]
        even = (real[0] + real[2], imag[0] + imag[2])
        odd = (real[1] + real[3], imag[1] + imag[3])
        sums[low] = (even[0] + odd[0], even[1] + odd[1])
        even = (real[0] - real[2], imag[0] - imag[2])
        odd = (real[1] - real[3], imag[1] - imag[3])
        sums[low + 4] = (even[0] + odd[1], even[1] - odd[0])
    return sums


def source_places():
    return {group[0]: source for source, group in enumerate(sources())}


def forward_kernel(records, following, table, out, upper, lower):

    def mix(i, carry):
        rows = pl.ds(pl.multiple_of(16 * i, 16), 16)
        for start in range(0, SPAN, 128):
            values = []
            for a in range(POINTS):
                begin = SPAN * a + start
                part = records if begin < HOP else following
                begin = begin % HOP
                values.append(part[rows, begin : begin + 128].astype(F32))
            for residue, value in enumerate(sixteen_point(values)):
                source = source_places()[residue]
                for part in range(2):
                    if value[part] is not None:
                        columns = slice(SPAN * part + start, SPAN * part + start + 128)
                        split_store(upper, lower, source, rows, columns, value[part])
        return carry

    lax.fori_loop(0, 8, mix, 0)

    def sink(first, residue, total):
        out[first : first + BINS] = total.astype(BF).reshape(BINS, 2 * BINS, 128)

    band_products(table, upper, lower, sink)


def bank_kernel(first, waveforms, lags, live, table, out, upper, lower):
    for i in range(4):
        rows = slice(SLOTS * i, SLOTS * i + SLOTS)
        wave = waveforms[first[0] + i].astype(F32)
        begin, end = wave[:, :SPAN], wave[:, SPAN:]
        for group in sources():
            source = source_places()[group[0]]
            cosine = math.cos(2.0 * math.pi * group[0] / POINTS)
            sine = math.sin(2.0 * math.pi * group[0] / POINTS)
            split_store(upper, lower, source, rows, slice(0, SPAN), begin + end * cosine)
            if len(group) == 2:
                split_store(upper, lower, source, rows, slice(SPAN, 2 * SPAN), end * -sine)
    turn = 2.0 * math.pi / NFFT
    lag = lags[...]
    fine = lax.broadcasted_iota(jnp.int32, (BINS * BINS, 128), 0) * POINTS
    fine = jnp.bitwise_and(fine * lag, NFFT - 1).astype(F32) * turn
    fine_cos, fine_sin = jnp.cos(fine), jnp.sin(fine)
    step = lax.broadcasted_iota(jnp.int32, (POINTS, 128), 0)
    step = jnp.bitwise_and(step * lag, NFFT - 1).astype(F32) * turn
    step_cos, step_sin = jnp.cos(step) * live[...], jnp.sin(step) * live[...]

    def sink(place, residue, total):
        total = total.reshape(BINS, 2, BINS, 128)
        base_real = total[:, 0].reshape(BINS * BINS, 128)
        base_imag = -total[:, 1].reshape(BINS * BINS, 128)
        low_cos, low_sin = (v[residue : residue + 1] for v in (step_cos, step_sin))
        cosine = fine_cos * low_cos - fine_sin * low_sin
        sine = fine_sin * low_cos + fine_cos * low_sin
        real = base_real * cosine - base_imag * sine
        imag = base_real * sine + base_imag * cosine
        both = [part.reshape(BINS, 1, BINS, 128) for part in (real, imag)]
        both = jnp.concatenate(both, axis=1).reshape(BINS, 2 * BINS, 128)
        out[place : place + BINS] = both.astype(BF)

    band_products(table, upper, lower, sink)


def spectra_call(kernel, operands, scalars=0):
    vmem = pl.BlockSpec(memory_space=pltpu.VMEM)
    smem = pl.BlockSpec(memory_space=pltpu.SMEM)
    return pl.pallas_call(
        kernel,
        out_shape=jax.ShapeDtypeStruct((SHARES, 2 * BINS, 128), BF),
        in_specs=[smem] * scalars + [vmem] * (len(operands) - scalars),
        out_specs=vmem,
        scratch_shapes=[pltpu.VMEM((9, 128, 2 * SPAN), BF)] * 2,
        compiler_params=pltpu.CompilerParams(vmem_limit_bytes=24 * 2**20),
    )(*operands)


def forward_spectra(records, following):
    return spectra_call(forward_kernel, (records, following, jnp.asarray(band_table())))


def bank_spectra(first, waveforms, lags, live):
    operands = (first.reshape(1), waveforms, lags, live, jnp.asarray(band_table()))
    return spectra_call(bank_kernel, operands, 1)


def swap_blocks(parts, lane):
    count = len(parts)
    size = 128 // count
    step = count // 2
    while step:
        low = (lane // (size * step)) % 2 == 0
        fresh = list(parts)
        for i in range(count):
            if i & step:
                continue
            j = i + step
            fresh[i] = jnp.where(low, parts[i], pltpu.roll(parts[j], size * step, 1))
            fresh[j] = jnp.where(low, pltpu.roll(parts[i], 128 - size * step, 1), parts[j])
        parts = fresh
        step //= 2
    return parts


def turned(unit, block):
    return lax.dot_general(unit[...], block, ROTATED, preferred_element_type=F32)


def weights_kernel(chunks, bank, spread, unit, weights, live, count, compact):
    for g in range(16):
        block = jnp.concatenate([bank[g * 8 + i] for i in range(8)], axis=0)
        compact[128 * g : 128 * g + 128, :] = turned(unit, block).astype(BF)

    def expand(g, position):
        rows = pl.ds(pl.multiple_of(256 * g, 256), 256)
        for i in range(4):
            wide = jnp.dot(compact[rows, :], spread[i], preferred_element_type=F32)
            for half in range(2):
                for j in range(2):
                    first = ((2 * g + half) * 8 + 2 * i + j) * 16
                    part = wide[128 * half : 128 * half + 128, 128 * j : 128 * j + 128]
                    weights[pl.ds(first, 16)] = part.reshape(16, 8, 128)
        for i in range(64):
            t = g * 64 + i
            for s in range(4):
                live[position + s] = t * 4 + s
            position = position + chunks[t]
        return position

    total = lax.fori_loop(0, 8, expand, 0)
    for s in range(UNROLL):
        live[total + s] = 2048
    weights[2048] = jnp.zeros((8, 128), F32)
    count[0] = total


def correlate_kernel(places, live, count, own, other, weights, unit, out, table, sums, place, landed):
    copy = pltpu.make_async_copy(places, place, landed)
    copy.start()
    lane = lax.broadcasted_iota(jnp.int32, (128, 128), 1)
    is_real = (lane // BINS) % 2 == 0
    for half, source in enumerate((own, other)):
        for y in range(4):
            start = half * 512 + y * 128
            for s in range(4):
                tiles = [source[(8 * s + i) * 4 + y] for i in range(8)]
                block = jnp.concatenate(tiles, axis=0)
                value = turned(unit, block)
                table[start : start + 128, s, :] = value
                ahead, behind = pltpu.roll(value, 128 - BINS, 1), pltpu.roll(value, BINS, 1)
                table[start : start + 128, 4 + s, :] = jnp.where(is_real, ahead, behind)
    sums[...] = jnp.zeros_like(sums)
    copy.wait()

    def some_chunks(step, carry):
        for i in range(UNROLL):
            chunk = live[step * UNROLL + i]
            tile = weights[chunk]
            totals = [None, None]
            for u in range(8):
                row = table_rows(table, place[chunk * 8 + u])
                term = row * tile[u : u + 1]
                totals[u % 2] = term if u < 2 else totals[u % 2] + term
            t = lax.shift_right_logical(chunk, 2)
            sums[t] = sums[t] + (totals[0] + totals[1])
        return carry

    lax.fori_loop(0, lax.div(count[0] + UNROLL - 1, UNROLL), some_chunks, 0)

    lane = lax.broadcasted_iota(jnp.int32, (128, 128), 1)
    is_real = (lane // BINS) % 2 == 0
    for g in range(4):
        for y in range(4):
            first = sums[g * 128 : (g + 1) * 128, y, :]
            second = sums[g * 128 : (g + 1) * 128, 4 + y, :]
            real = first - pltpu.roll(first, 128 - BINS, 1)
            imag = second + pltpu.roll(second, BINS, 1)
            total = turned(unit, jnp.where(is_real, real, imag).astype(BF)).astype(BF)
            parts = [total[16 * i : 16 * (i + 1)] for i in range(8)]
            for i, part in enumerate(swap_blocks(parts, lane[:16])):
                out[(8 * g + i) * 4 + y] = part


def table_rows(table, first):
    rows = table.reshape(8192, 128)
    return rows[pl.ds(pl.multiple_of(first, 8), 8)]


def spread_table():
    lane = np.arange(128)
    one = np.zeros((2, BINS, 128))
    for part in range(2):
        one[part, lane % BINS, lane] = (lane // BINS) % 2 == part
    one = one.reshape(2 * BINS, 128)
    table = np.zeros((4, 8, 2 * BINS, 2, 128))
    for share in range(8):
        table[share // 2, share, :, share % 2] = one
    return table.reshape(4, 128, 256).astype(BF)


def correlate(place, chunks, own, other, bank):
    vmem = pl.BlockSpec(memory_space=pltpu.VMEM)
    smem = pl.BlockSpec(memory_space=pltpu.SMEM)
    unit = jnp.eye(128, dtype=BF)
    weights, live, count = pl.pallas_call(
        weights_kernel,
        out_shape=(
            jax.ShapeDtypeStruct((2049, 8, 128), F32),
            jax.ShapeDtypeStruct((2048 + 2 * UNROLL,), jnp.int32),
            jax.ShapeDtypeStruct((1,), jnp.int32),
        ),
        in_specs=[smem, vmem, vmem, vmem],
        out_specs=(vmem, smem, smem),
        scratch_shapes=[pltpu.VMEM((2048, 128), BF)],
        compiler_params=pltpu.CompilerParams(vmem_limit_bytes=20 * 2**20),
        cost_estimate=pl.CostEstimate(flops=2**29, bytes_accessed=10**7, transcendentals=0),
    )(chunks, bank, jnp.asarray(spread_table()), unit)
    correlated = pl.pallas_call(
        correlate_kernel,
        out_shape=jax.ShapeDtypeStruct((SHARES, 16, 128), BF),
        in_specs=[pl.BlockSpec(memory_space=pl.ANY), smem, smem, vmem, vmem, vmem, vmem],
        out_specs=vmem,
        scratch_shapes=[
            pltpu.VMEM((1024, 8, 128), F32),
            pltpu.VMEM((513, 8, 128), F32),
            pltpu.SMEM(place.shape, jnp.int32),
            pltpu.SemaphoreType.DMA,
        ],
        compiler_params=pltpu.CompilerParams(vmem_limit_bytes=22 * 2**20),
    )(place, live, count, own, other, weights, unit)
    return correlated


def on_device(records, waveforms, slot_channels, slot_counts, slot_lags):
    core = lax.axis_index("c")
    quarter = lax.axis_index("y")
    following = lax.ppermute(records[:, : NFFT - HOP], ("z", "x"), [(i, i - 1) for i in range(1, 32)])

    first = core * 16 + quarter * 4
    lags = lax.dynamic_slice_in_dim(slot_lags, first, 4, 0).reshape(1, 128)
    counts = lax.dynamic_slice_in_dim(slot_counts, first, 4, 0)
    channels = lax.dynamic_slice_in_dim(slot_channels, first, 4, 0).reshape(128)
    live = (jnp.arange(SLOTS, dtype=jnp.int32)[None] < counts[:, None]).reshape(128)
    bank = bank_spectra(first, waveforms, lags, live.astype(F32)[None])
    digits = jnp.stack([channels // 32 + jnp.where(live, 32, 0), channels % 32]).astype(BF)
    digits = jnp.broadcast_to(digits, (SHARES, 1, 2, 128))

    rows = jnp.concatenate([bank.reshape(SHARES, 8, 2, 128), digits], axis=1)
    shares = lax.optimization_barrier(jnp.pad(rows, ((0, 0), (8, 0), (0, 0), (0, 0))))
    spectra = forward_spectra(records, following).reshape(SHARES, 8, 2, 128)
    shares = lax.dynamic_update_slice(shares, spectra, (0, 0, 0, 0))
    shares = lax.all_to_all(shares, ("z", "x", "y"), split_axis=0, concat_axis=0, tiled=True)
    own = shares[:, :8].reshape(SHARES, 2 * BINS, 128)
    bank = shares[:, 8:16].reshape(SHARES, 2 * BINS, 128)
    other = lax.ppermute(own, "c", [(0, 1), (1, 0)])
    digits = shares[:, 16].astype(jnp.int32)
    channels = (digits[:, 0] % 32) * 32 + digits[:, 1]
    home = channels // 128
    place = ((home % 2) ^ core) * 512 + (home // 2) * 128 + channels % 128
    place = jnp.pad(8 * place.reshape(512 * SLOTS), (0, 128))
    counts = jnp.sum((digits[:, 0] // 32).reshape(512, SLOTS), axis=1)
    chunks = (counts + 7) // 8
    correlated = correlate(place, chunks, own, other, bank)
    here = lax.all_to_all(correlated, ("z", "x", "y"), split_axis=0, concat_axis=0, tiled=True)
    there = lax.ppermute(here, "c", [(0, 1), (1, 0)])
    traces, energy = inverse_traces(here, there, core)
    energy = energy + lax.ppermute(energy, "c", [(0, 1), (1, 0)])
    for pairs in (((0, 1), (2, 3)), ((0, 3), (1, 2))):
        moves = [move for pair in pairs for move in (pair, pair[::-1])]
        energy = energy + lax.ppermute(energy, "y", moves)
    return traces * lax.rsqrt(energy / (32 * HOP) + EPS).reshape(32, 1)


def solution(mesh):
    fine = Mesh(mesh.devices.reshape(8, 4, 4, 2), ("z", "x", "y", "c"))
    tmpl, chan = ("z", "x"), ("y", "c")
    in_specs = (P(chan, tmpl), P(tmpl, None, None), P(tmpl, None), P(tmpl), P(tmpl, None))
    return jax.shard_map(
        on_device, mesh=fine, in_specs=in_specs, out_specs=P(tmpl, chan), check_vma=False
    )
```

```python
import functools
import math

import jax
import jax.numpy as jnp
import numpy as np
from jax import lax
from jax.experimental import pallas as pl
from jax.experimental.pallas import tpu as pltpu
from jax.sharding import Mesh
from jax.sharding import PartitionSpec as P

NFFT = 4096
BAND = 1024
HOP = 3072
SLOTS = 32
EPS = 1e-06
POINTS = 16
SPAN = NFFT // POINTS
ROTATED = (((1,), (1,)), ((), ()))
BINS = 8
SHARES = BAND // BINS
UNROLL = 16
COLUMNS = 256
BF = jnp.bfloat16
F32 = jnp.float32


def halves(matrix):
    upper = matrix.astype(BF)
    lower = (matrix - upper.astype(np.float64)).astype(BF)
    return upper, lower


def residues():
    place = np.arange(POINTS)
    return 4 * (place % 4) + place // 4


def share_bins():
    share = np.arange(SHARES)
    fine = BINS * (share % BINS)[:, None] + np.arange(BINS)[None, :]
    return POINTS * fine + residues()[share // BINS][:, None]


def sources():
    return [(0,), (8,)] + [(low, POINTS - low) for low in range(1, POINTS // 2)]


def band_table():
    samples = np.arange(SPAN)
    tables = []
    for group in sources():
        for residue in group:
            bins = POINTS * np.arange(BINS * BINS).reshape(BINS, BINS) + residue
            angle = 2.0 * np.pi * ((bins[..., None] * samples) % NFFT) / NFFT
            cosine, sine = np.cos(angle), np.sin(angle)
            sign = 1.0 if residue == group[0] else -1.0
            real = np.concatenate([cosine, sign * sine], axis=2)
            imag = np.concatenate([-sine, sign * cosine], axis=2)
            tables.append(np.stack([real, imag], axis=1).reshape(2 * BINS * BINS, 2 * SPAN))
    return np.stack(halves(np.stack(tables)))


def band_products(table, upper, lower, sink):
    order = list(residues())
    begin = 0
    for source, group in enumerate(sources()):
        depth = SPAN if len(group) == 1 else 2 * SPAN
        count = len(group)
        coarse, fine = (
            table[part, begin : begin + count, :, :depth].reshape(count * 128, depth)
            for part in range(2)
        )
        dot = functools.partial(
            lax.dot_general, dimension_numbers=ROTATED, preferred_element_type=F32
        )
        high, low = upper[source, :, :depth], lower[source, :, :depth]
        total = dot(coarse, high) + (dot(fine, high) + dot(coarse, low))
        for i, residue in enumerate(group):
            sink(BINS * order.index(residue), residue, total[128 * i : 128 * i + 128])
        begin += count


def inverse_table():
    bins = share_bins()
    angle = 2.0 * np.pi * ((bins[..., None] * np.arange(HOP // 3)) % NFFT) / NFFT
    weight = np.where(bins == 0, 1.0, 2.0)[..., None] / NFFT
    real = np.stack([np.cos(angle) * weight, -np.sin(angle) * weight], axis=1)
    imag = np.stack([np.sin(angle) * weight, np.cos(angle) * weight], axis=1)
    real, imag = (table.reshape(4, 512, HOP // 3) for table in (real, imag))
    table = np.concatenate([real[0], real[2], real[1], real[3], -imag[1], imag[3]])
    return table.reshape(-1, HOP // 3 // COLUMNS, COLUMNS).swapaxes(0, 1).astype(BF)


def inverse_kernel(core, mine, other, held, traces, energy, left):
    row = lax.broadcasted_iota(jnp.int32, (128, 256), 0)
    lane = lax.broadcasted_iota(jnp.int32, (128, 256), 1)
    half = lax.shift_right_logical(row, 4) & 1
    wanted = 128 * (half ^ core[0]) + 64 * core[0]
    wanted = wanted + 16 * lax.shift_right_logical(row, 5) + (row & 15)
    pick = jnp.where(lane == wanted, 1.0, 0.0).astype(BF)
    for i in range(16):
        rows = slice(8 * i, 8 * i + 8)
        block = jnp.concatenate([q[rows].reshape(128, 128) for q in (mine, other)], axis=1)
        chosen = lax.dot_general(pick, block, ROTATED, preferred_element_type=F32)
        left[:, 128 * i : 128 * i + 128] = chosen.astype(BF)
    dot = functools.partial(jnp.dot, preferred_element_type=F32)
    squares = jnp.zeros((32, 128), F32)
    for step in range(held.shape[0]):
        first = dot(left[:, 0:512], held[step, 0:512])
        second = dot(left[:, 1024:1536], held[step, 512:1024])
        turn = []
        for part in (1024, 2048):
            low = dot(left[:, 512:1024], held[step, part : part + 512])
            turn.append(low + dot(left[:, 1536:2048], held[step, part + 512 : part + 1024]))
        both = first + second
        values = both + turn[0], first - second + turn[1], both - turn[0]
        for quarter, value in enumerate(values):
            for block in range(4):
                part = value[32 * block : 32 * block + 32]
                begin = block * HOP + quarter * (HOP // 3) + step * COLUMNS
                traces[:, begin : begin + COLUMNS] = part
                part = part * part
                for lane in range(0, COLUMNS, 128):
                    squares = squares + part[:, lane : lane + 128]
    energy[...] = jnp.sum(squares.T, axis=0, keepdims=True)


def inverse_traces(mine, other, core):
    table = inverse_table()
    vmem = pl.BlockSpec(memory_space=pltpu.VMEM)
    return pl.pallas_call(
        inverse_kernel,
        out_shape=(
            jax.ShapeDtypeStruct((32, 4 * HOP), F32),
            jax.ShapeDtypeStruct((1, 32), F32),
        ),
        in_specs=[pl.BlockSpec(memory_space=pltpu.SMEM), vmem, vmem, vmem],
        out_specs=(vmem, vmem),
        scratch_shapes=[pltpu.VMEM((128, 2 * BAND), BF)],
        compiler_params=pltpu.CompilerParams(vmem_limit_bytes=20 * 2**20),
    )(core.reshape(1), mine, other, jnp.asarray(table))


def split_store(upper, lower, source, rows, columns, value):
    high = value.astype(BF)
    upper[source, rows, columns] = high
    lower[source, rows, columns] = (value - high.astype(F32)).astype(BF)


def times(value, turns):
    real, imag = value
    cosine = math.cos(2.0 * math.pi * turns / POINTS)
    sine = math.sin(2.0 * math.pi * turns / POINTS)
    if turns == 0:
        return value
    if imag is None:
        return real * cosine, real * -sine
    return real * cosine + imag * sine, imag * cosine - real * sine


def sixteen_point(values):
    inner = []
    for a in range(4):
        x = values[a::4]
        even, odd = x[0] + x[2], x[1] + x[3]
        step = (x[0] - x[2], x[3] - x[1])
        inner.append([(even + odd, None), step, (even - odd, None), (step[0], -step[1])])
    sums = [None] * 9
    for low in range(4):
        v = [times(inner[a][low], (low * a) % POINTS) for a in range(4)]
        real = [part[0] for part in v]
        if low == 0:
            even, odd = real[0] + real[2], real[1] + real[3]
            sums[0], sums[8] = (even + odd, None), (even - odd, None)
            sums[4] = (real[0] - real[2], real[3] - real[1])
            continue
        imag = [jnp.zeros_like(real[0]) if part[1] is None else part[1] for part in v]
        even = (real[0] + real[2], imag[0] + imag[2])
        odd = (real[1] + real[3], imag[1] + imag[3])
        sums[low] = (even[0] + odd[0], even[1] + odd[1])
        even = (real[0] - real[2], imag[0] - imag[2])
        odd = (real[1] - real[3], imag[1] - imag[3])
        sums[low + 4] = (even[0] + odd[1], even[1] - odd[0])
    return sums


def source_places():
    return {group[0]: source for source, group in enumerate(sources())}


def forward_kernel(records, following, table, bank, out, upper, lower):
    out[:, 2 * BINS :, :] = bank[...]

    def mix(i, carry):
        rows = pl.ds(pl.multiple_of(16 * i, 16), 16)
        for start in range(0, SPAN, 128):
            values = []
            for a in range(POINTS):
                begin = SPAN * a + start
                part = records if begin < HOP else following
                begin = begin % HOP
                values.append(part[rows, begin : begin + 128].astype(F32))
            for residue, value in enumerate(sixteen_point(values)):
                source = source_places()[residue]
                for part in range(2):
                    if value[part] is not None:
                        columns = slice(SPAN * part + start, SPAN * part + start + 128)
                        split_store(upper, lower, source, rows, columns, value[part])
        return carry

    lax.fori_loop(0, 8, mix, 0)

    def sink(first, residue, total):
        out[first : first + BINS, : 2 * BINS] = total.astype(BF).reshape(BINS, 2 * BINS, 128)

    band_products(table, upper, lower, sink)


def bank_kernel(first, waveforms, lags, live, table, out, upper, lower):
    for i in range(4):
        rows = slice(SLOTS * i, SLOTS * i + SLOTS)
        wave = waveforms[first[0] + i].astype(F32)
        begin, end = wave[:, :SPAN], wave[:, SPAN:]
        for group in sources():
            source = source_places()[group[0]]
            cosine = math.cos(2.0 * math.pi * group[0] / POINTS)
            sine = math.sin(2.0 * math.pi * group[0] / POINTS)
            split_store(upper, lower, source, rows, slice(0, SPAN), begin + end * cosine)
            if len(group) == 2:
                split_store(upper, lower, source, rows, slice(SPAN, 2 * SPAN), end * -sine)
    turn = 2.0 * math.pi / NFFT
    lag = lags[...]
    fine = lax.broadcasted_iota(jnp.int32, (BINS * BINS, 128), 0) * POINTS
    fine = jnp.bitwise_and(fine * lag, NFFT - 1).astype(F32) * turn
    fine_cos, fine_sin = jnp.cos(fine), jnp.sin(fine)
    step = lax.broadcasted_iota(jnp.int32, (POINTS, 128), 0)
    step = jnp.bitwise_and(step * lag, NFFT - 1).astype(F32) * turn
    step_cos, step_sin = jnp.cos(step) * live[...], jnp.sin(step) * live[...]

    def sink(place, residue, total):
        total = total.reshape(BINS, 2, BINS, 128)
        base_real = total[:, 0].reshape(BINS * BINS, 128)
        base_imag = -total[:, 1].reshape(BINS * BINS, 128)
        low_cos, low_sin = (v[residue : residue + 1] for v in (step_cos, step_sin))
        cosine = fine_cos * low_cos - fine_sin * low_sin
        sine = fine_sin * low_cos + fine_cos * low_sin
        real = base_real * cosine - base_imag * sine
        imag = base_real * sine + base_imag * cosine
        both = [part.reshape(BINS, 1, BINS, 128) for part in (real, imag)]
        both = jnp.concatenate(both, axis=1).reshape(BINS, 2 * BINS, 128)
        out[place : place + BINS] = both.astype(BF)

    band_products(table, upper, lower, sink)


def spectra_call(kernel, operands, scalars=0, rows=2 * BINS):
    vmem = pl.BlockSpec(memory_space=pltpu.VMEM)
    smem = pl.BlockSpec(memory_space=pltpu.SMEM)
    return pl.pallas_call(
        kernel,
        out_shape=jax.ShapeDtypeStruct((SHARES, rows, 128), BF),
        in_specs=[smem] * scalars + [vmem] * (len(operands) - scalars),
        out_specs=vmem,
        scratch_shapes=[pltpu.VMEM((9, 128, 2 * SPAN), BF)] * 2,
        compiler_params=pltpu.CompilerParams(vmem_limit_bytes=24 * 2**20),
    )(*operands)


def forward_spectra(records, following, bank):
    operands = (records, following, jnp.asarray(band_table()), bank)
    return spectra_call(forward_kernel, operands, rows=4 * BINS)


def bank_spectra(first, waveforms, lags, live):
    operands = (first.reshape(1), waveforms, lags, live, jnp.asarray(band_table()))
    return spectra_call(bank_kernel, operands, 1)


def swap_blocks(parts, lane):
    count = len(parts)
    size = 128 // count
    step = count // 2
    while step:
        low = (lane // (size * step)) % 2 == 0
        fresh = list(parts)
        for i in range(count):
            if i & step:
                continue
            j = i + step
            fresh[i] = jnp.where(low, parts[i], pltpu.roll(parts[j], size * step, 1))
            fresh[j] = jnp.where(low, pltpu.roll(parts[i], 128 - size * step, 1), parts[j])
        parts = fresh
        step //= 2
    return parts


def turned(unit, block):
    return lax.dot_general(unit[...], block, ROTATED, preferred_element_type=F32)


def weights_kernel(chunks, bank, spread, unit, weights, live, count, compact):
    for g in range(16):
        block = jnp.concatenate([bank[g * 8 + i] for i in range(8)], axis=0)
        compact[128 * g : 128 * g + 128, :] = turned(unit, block).astype(BF)

    def expand(g, position):
        rows = pl.ds(pl.multiple_of(256 * g, 256), 256)
        for i in range(4):
            wide = jnp.dot(compact[rows, :], spread[i], preferred_element_type=F32)
            for half in range(2):
                for j in range(2):
                    first = ((2 * g + half) * 8 + 2 * i + j) * 16
                    part = wide[128 * half : 128 * half + 128, 128 * j : 128 * j + 128]
                    weights[pl.ds(first, 16)] = part.reshape(16, 8, 128)
        for i in range(64):
            t = g * 64 + i
            for s in range(4):
                live[position + s] = t * 4 + s
            position = position + chunks[t]
        return position

    total = lax.fori_loop(0, 8, expand, 0)
    for s in range(UNROLL):
        live[total + s] = 2048
    weights[2048] = jnp.zeros((8, 128), F32)
    count[0] = total


def correlate_kernel(places, live, count, own, other, weights, unit, out, table, sums, place, landed):
    copy = pltpu.make_async_copy(places, place, landed)
    copy.start()
    lane = lax.broadcasted_iota(jnp.int32, (128, 128), 1)
    is_real = (lane // BINS) % 2 == 0
    for half, source in enumerate((own, other)):
        for y in range(4):
            start = half * 512 + y * 128
            for s in range(4):
                tiles = [source[(8 * s + i) * 4 + y] for i in range(8)]
                block = jnp.concatenate(tiles, axis=0)
                value = turned(unit, block)
                table[start : start + 128, s, :] = value
                ahead, behind = pltpu.roll(value, 128 - BINS, 1), pltpu.roll(value, BINS, 1)
                table[start : start + 128, 4 + s, :] = jnp.where(is_real, ahead, behind)
    sums[...] = jnp.zeros_like(sums)
    copy.wait()

    def some_chunks(step, carry):
        for i in range(UNROLL):
            chunk = live[step * UNROLL + i]
            tile = weights[chunk]
            totals = [None, None]
            for u in range(8):
                row = table_rows(table, place[chunk * 8 + u])
                term = row * tile[u : u + 1]
                totals[u % 2] = term if u < 2 else totals[u % 2] + term
            t = lax.shift_right_logical(chunk, 2)
            sums[t] = sums[t] + (totals[0] + totals[1])
        return carry

    lax.fori_loop(0, lax.div(count[0] + UNROLL - 1, UNROLL), some_chunks, 0)

    lane = lax.broadcasted_iota(jnp.int32, (128, 128), 1)
    is_real = (lane // BINS) % 2 == 0
    for g in range(4):
        for y in range(4):
            first = sums[g * 128 : (g + 1) * 128, y, :]
            second = sums[g * 128 : (g + 1) * 128, 4 + y, :]
            real = first - pltpu.roll(first, 128 - BINS, 1)
            imag = second + pltpu.roll(second, BINS, 1)
            total = turned(unit, jnp.where(is_real, real, imag).astype(BF)).astype(BF)
            parts = [total[16 * i : 16 * (i + 1)] for i in range(8)]
            for i, part in enumerate(swap_blocks(parts, lane[:16])):
                out[(8 * g + i) * 4 + y] = part


def table_rows(table, first):
    rows = table.reshape(8192, 128)
    return rows[pl.ds(pl.multiple_of(first, 8), 8)]


def spread_table():
    lane = np.arange(128)
    one = np.zeros((2, BINS, 128))
    for part in range(2):
        one[part, lane % BINS, lane] = (lane // BINS) % 2 == part
    one = one.reshape(2 * BINS, 128)
    table = np.zeros((4, 8, 2 * BINS, 2, 128))
    for share in range(8):
        table[share // 2, share, :, share % 2] = one
    return table.reshape(4, 128, 256).astype(BF)


def correlate(place, chunks, own, other, bank):
    vmem = pl.BlockSpec(memory_space=pltpu.VMEM)
    smem = pl.BlockSpec(memory_space=pltpu.SMEM)
    unit = jnp.eye(128, dtype=BF)
    weights, live, count = pl.pallas_call(
        weights_kernel,
        out_shape=(
            jax.ShapeDtypeStruct((2049, 8, 128), F32),
            jax.ShapeDtypeStruct((2048 + 2 * UNROLL,), jnp.int32),
            jax.ShapeDtypeStruct((1,), jnp.int32),
        ),
        in_specs=[smem, vmem, vmem, vmem],
        out_specs=(vmem, smem, smem),
        scratch_shapes=[pltpu.VMEM((2048, 128), BF)],
        compiler_params=pltpu.CompilerParams(vmem_limit_bytes=20 * 2**20),
        cost_estimate=pl.CostEstimate(flops=2**29, bytes_accessed=10**7, transcendentals=0),
    )(chunks, bank, jnp.asarray(spread_table()), unit)
    correlated = pl.pallas_call(
        correlate_kernel,
        out_shape=jax.ShapeDtypeStruct((SHARES, 16, 128), BF),
        in_specs=[pl.BlockSpec(memory_space=pl.ANY), smem, smem, vmem, vmem, vmem, vmem],
        out_specs=vmem,
        scratch_shapes=[
            pltpu.VMEM((1024, 8, 128), F32),
            pltpu.VMEM((513, 8, 128), F32),
            pltpu.SMEM(place.shape, jnp.int32),
            pltpu.SemaphoreType.DMA,
        ],
        compiler_params=pltpu.CompilerParams(vmem_limit_bytes=22 * 2**20),
    )(place, live, count, own, other, weights, unit)
    return correlated


def on_device(records, waveforms, slot_channels, slot_counts, slot_lags):
    core = lax.axis_index("c")
    quarter = lax.axis_index("y")
    following = lax.ppermute(records[:, : NFFT - HOP], ("z", "x"), [(i, i - 1) for i in range(1, 32)])

    first = core * 16 + quarter * 4
    lags = lax.dynamic_slice_in_dim(slot_lags, first, 4, 0).reshape(1, 128)
    counts = lax.dynamic_slice_in_dim(slot_counts, first, 4, 0)
    channels = lax.dynamic_slice_in_dim(slot_channels, first, 4, 0).reshape(128)
    live = (jnp.arange(SLOTS, dtype=jnp.int32)[None] < counts[:, None]).reshape(128)
    bank = bank_spectra(first, waveforms, lags, live.astype(F32)[None])
    digits = jnp.stack([channels // 32 + jnp.where(live, 32, 0), channels % 32]).astype(BF)
    digits = jnp.broadcast_to(digits, (SHARES, 1, 2, 128))

    shares = forward_spectra(records, following, bank).reshape(SHARES, 16, 2, 128)
    shares = jnp.concatenate([shares, digits], axis=1)
    shares = lax.all_to_all(shares, ("z", "x", "y"), split_axis=0, concat_axis=0, tiled=True)
    own = shares[:, :8].reshape(SHARES, 2 * BINS, 128)
    bank = shares[:, 8:16].reshape(SHARES, 2 * BINS, 128)
    other = lax.ppermute(own, "c", [(0, 1), (1, 0)])
    digits = shares[:, 16].astype(jnp.int32)
    channels = (digits[:, 0] % 32) * 32 + digits[:, 1]
    home = channels // 128
    place = ((home % 2) ^ core) * 512 + (home // 2) * 128 + channels % 128
    place = jnp.pad(8 * place.reshape(512 * SLOTS), (0, 128))
    counts = jnp.sum((digits[:, 0] // 32).reshape(512, SLOTS), axis=1)
    chunks = (counts + 7) // 8
    correlated = correlate(place, chunks, own, other, bank)
    here = lax.all_to_all(correlated, ("z", "x", "y"), split_axis=0, concat_axis=0, tiled=True)
    there = lax.ppermute(here, "c", [(0, 1), (1, 0)])
    traces, energy = inverse_traces(here, there, core)
    energy = energy + lax.ppermute(energy, "c", [(0, 1), (1, 0)])
    shifts = [[(i, (i + d) % 4) for i in range(4)] for d in range(1, 4)]
    energy = sum((lax.ppermute(energy, "y", shift) for shift in shifts), energy)
    return traces * lax.rsqrt(energy / (32 * HOP) + EPS).reshape(32, 1)


def solution(mesh):
    fine = Mesh(mesh.devices.reshape(8, 4, 4, 2), ("z", "x", "y", "c"))
    tmpl, chan = ("z", "x"), ("y", "c")
    in_specs = (P(chan, tmpl), P(tmpl, None, None), P(tmpl, None), P(tmpl), P(tmpl, None))
    return jax.shard_map(
        on_device, mesh=fine, in_specs=in_specs, out_specs=P(tmpl, chan), check_vma=False
    )
```

```python
import functools
import math

import jax
import jax.numpy as jnp
import numpy as np
from jax import lax
from jax.experimental import pallas as pl
from jax.experimental.pallas import tpu as pltpu
from jax.sharding import Mesh
from jax.sharding import PartitionSpec as P

NFFT = 4096
BAND = 1024
HOP = 3072
SLOTS = 32
EPS = 1e-06
POINTS = 16
SPAN = NFFT // POINTS
ROTATED = (((1,), (1,)), ((), ()))
BINS = 8
SHARES = BAND // BINS
UNROLL = 16
COLUMNS = 256
BF = jnp.bfloat16
F32 = jnp.float32


def halves(matrix):
    upper = matrix.astype(BF)
    lower = (matrix - upper.astype(np.float64)).astype(BF)
    return upper, lower


def residues():
    place = np.arange(POINTS)
    return 4 * (place % 4) + place // 4


def share_bins():
    share = np.arange(SHARES)
    fine = BINS * (share % BINS)[:, None] + np.arange(BINS)[None, :]
    return POINTS * fine + residues()[share // BINS][:, None]


def sources():
    return [(0,), (8,)] + [(low, POINTS - low) for low in range(1, POINTS // 2)]


def band_table():
    samples = np.arange(SPAN)
    tables = []
    for group in sources():
        for residue in group:
            bins = POINTS * np.arange(BINS * BINS).reshape(BINS, BINS) + residue
            angle = 2.0 * np.pi * ((bins[..., None] * samples) % NFFT) / NFFT
            cosine, sine = np.cos(angle), np.sin(angle)
            sign = 1.0 if residue == group[0] else -1.0
            real = np.concatenate([cosine, sign * sine], axis=2)
            imag = np.concatenate([-sine, sign * cosine], axis=2)
            tables.append(np.stack([real, imag], axis=1).reshape(2 * BINS * BINS, 2 * SPAN))
    return np.stack(halves(np.stack(tables)))


def band_products(table, upper, lower, sink):
    order = list(residues())
    begin = 0
    for source, group in enumerate(sources()):
        depth = SPAN if len(group) == 1 else 2 * SPAN
        count = len(group)
        coarse, fine = (
            table[part, begin : begin + count, :, :depth].reshape(count * 128, depth)
            for part in range(2)
        )
        dot = functools.partial(
            lax.dot_general, dimension_numbers=ROTATED, preferred_element_type=F32
        )
        high, low = upper[source, :, :depth], lower[source, :, :depth]
        total = dot(coarse, high) + (dot(fine, high) + dot(coarse, low))
        for i, residue in enumerate(group):
            sink(BINS * order.index(residue), residue, total[128 * i : 128 * i + 128])
        begin += count


def inverse_table():
    bins = share_bins()
    angle = 2.0 * np.pi * ((bins[..., None] * np.arange(HOP // 3)) % NFFT) / NFFT
    weight = np.where(bins == 0, 1.0, 2.0)[..., None] / NFFT
    real = np.stack([np.cos(angle) * weight, -np.sin(angle) * weight], axis=1)
    imag = np.stack([np.sin(angle) * weight, np.cos(angle) * weight], axis=1)
    real, imag = (table.reshape(4, 512, HOP // 3) for table in (real, imag))
    table = np.concatenate([real[0], real[2], real[1], real[3], -imag[1], imag[3]])
    return table.reshape(-1, HOP // 3 // COLUMNS, COLUMNS).swapaxes(0, 1).astype(BF)


def inverse_kernel(core, mine, other, held, traces, energy, left):
    row = lax.broadcasted_iota(jnp.int32, (128, 256), 0)
    lane = lax.broadcasted_iota(jnp.int32, (128, 256), 1)
    half = lax.shift_right_logical(row, 4) & 1
    wanted = 128 * (half ^ core[0]) + 64 * core[0]
    wanted = wanted + 16 * lax.shift_right_logical(row, 5) + (row & 15)
    pick = jnp.where(lane == wanted, 1.0, 0.0).astype(BF)
    for i in range(16):
        rows = slice(8 * i, 8 * i + 8)
        block = jnp.concatenate([q[rows].reshape(128, 128) for q in (mine, other)], axis=1)
        chosen = lax.dot_general(pick, block, ROTATED, preferred_element_type=F32)
        left[:, 128 * i : 128 * i + 128] = chosen.astype(BF)
    dot = functools.partial(jnp.dot, preferred_element_type=F32)
    squares = jnp.zeros((32, 128), F32)
    for step in range(held.shape[0]):
        first = dot(left[:, 0:512], held[step, 0:512])
        second = dot(left[:, 1024:1536], held[step, 512:1024])
        turn = []
        for part in (1024, 2048):
            low = dot(left[:, 512:1024], held[step, part : part + 512])
            turn.append(low + dot(left[:, 1536:2048], held[step, part + 512 : part + 1024]))
        both = first + second
        values = both + turn[0], first - second + turn[1], both - turn[0]
        for quarter, value in enumerate(values):
            for block in range(4):
                part = value[32 * block : 32 * block + 32]
                begin = block * HOP + quarter * (HOP // 3) + step * COLUMNS
                traces[:, begin : begin + COLUMNS] = part
                part = part * part
                for lane in range(0, COLUMNS, 128):
                    squares = squares + part[:, lane : lane + 128]
    energy[...] = jnp.sum(squares.T, axis=0, keepdims=True)


def inverse_traces(mine, other, core):
    table = inverse_table()
    vmem = pl.BlockSpec(memory_space=pltpu.VMEM)
    return pl.pallas_call(
        inverse_kernel,
        out_shape=(
            jax.ShapeDtypeStruct((32, 4 * HOP), F32),
            jax.ShapeDtypeStruct((1, 32), F32),
        ),
        in_specs=[pl.BlockSpec(memory_space=pltpu.SMEM), vmem, vmem, vmem],
        out_specs=(vmem, vmem),
        scratch_shapes=[pltpu.VMEM((128, 2 * BAND), BF)],
        compiler_params=pltpu.CompilerParams(vmem_limit_bytes=14 * 2**20),
    )(core.reshape(1), mine, other, jnp.asarray(table))


def split_store(upper, lower, source, rows, columns, value):
    high = value.astype(BF)
    upper[source, rows, columns] = high
    lower[source, rows, columns] = (value - high.astype(F32)).astype(BF)


def times(value, turns):
    real, imag = value
    cosine = math.cos(2.0 * math.pi * turns / POINTS)
    sine = math.sin(2.0 * math.pi * turns / POINTS)
    if turns == 0:
        return value
    if imag is None:
        return real * cosine, real * -sine
    return real * cosine + imag * sine, imag * cosine - real * sine


def sixteen_point(values):
    inner = []
    for a in range(4):
        x = values[a::4]
        even, odd = x[0] + x[2], x[1] + x[3]
        step = (x[0] - x[2], x[3] - x[1])
        inner.append([(even + odd, None), step, (even - odd, None), (step[0], -step[1])])
    sums = [None] * 9
    for low in range(4):
        v = [times(inner[a][low], (low * a) % POINTS) for a in range(4)]
        real = [part[0] for part in v]
        if low == 0:
            even, odd = real[0] + real[2], real[1] + real[3]
            sums[0], sums[8] = (even + odd, None), (even - odd, None)
            sums[4] = (real[0] - real[2], real[3] - real[1])
            continue
        imag = [jnp.zeros_like(real[0]) if part[1] is None else part[1] for part in v]
        even = (real[0] + real[2], imag[0] + imag[2])
        odd = (real[1] + real[3], imag[1] + imag[3])
        sums[low] = (even[0] + odd[0], even[1] + odd[1])
        even = (real[0] - real[2], imag[0] - imag[2])
        odd = (real[1] - real[3], imag[1] - imag[3])
        sums[low + 4] = (even[0] + odd[1], even[1] - odd[0])
    return sums


def source_places():
    return {group[0]: source for source, group in enumerate(sources())}


def forward_kernel(records, following, table, out, upper, lower):

    def mix(i, carry):
        rows = pl.ds(pl.multiple_of(16 * i, 16), 16)
        for start in range(0, SPAN, 128):
            values = []
            for a in range(POINTS):
                begin = SPAN * a + start
                part = records if begin < HOP else following
                begin = begin % HOP
                values.append(part[rows, begin : begin + 128].astype(F32))
            for residue, value in enumerate(sixteen_point(values)):
                source = source_places()[residue]
                for part in range(2):
                    if value[part] is not None:
                        columns = slice(SPAN * part + start, SPAN * part + start + 128)
                        split_store(upper, lower, source, rows, columns, value[part])
        return carry

    lax.fori_loop(0, 8, mix, 0)

    def sink(first, residue, total):
        out[first : first + BINS] = total.astype(BF).reshape(BINS, 2 * BINS, 128)

    band_products(table, upper, lower, sink)


def bank_kernel(waveforms, lags, live, table, out, upper, lower):
    for i in range(4):
        rows = slice(SLOTS * i, SLOTS * i + SLOTS)
        wave = waveforms[i].astype(F32)
        begin, end = wave[:, :SPAN], wave[:, SPAN:]
        for group in sources():
            source = source_places()[group[0]]
            cosine = math.cos(2.0 * math.pi * group[0] / POINTS)
            sine = math.sin(2.0 * math.pi * group[0] / POINTS)
            split_store(upper, lower, source, rows, slice(0, SPAN), begin + end * cosine)
            if len(group) == 2:
                split_store(upper, lower, source, rows, slice(SPAN, 2 * SPAN), end * -sine)
    turn = 2.0 * math.pi / NFFT
    lag = lags[...]
    fine = lax.broadcasted_iota(jnp.int32, (BINS * BINS, 128), 0) * POINTS
    fine = jnp.bitwise_and(fine * lag, NFFT - 1).astype(F32) * turn
    fine_cos, fine_sin = jnp.cos(fine), jnp.sin(fine)
    step = lax.broadcasted_iota(jnp.int32, (POINTS, 128), 0)
    step = jnp.bitwise_and(step * lag, NFFT - 1).astype(F32) * turn
    step_cos, step_sin = jnp.cos(step) * live[...], jnp.sin(step) * live[...]

    def sink(place, residue, total):
        total = total.reshape(BINS, 2, BINS, 128)
        base_real = total[:, 0].reshape(BINS * BINS, 128)
        base_imag = -total[:, 1].reshape(BINS * BINS, 128)
        low_cos, low_sin = (v[residue : residue + 1] for v in (step_cos, step_sin))
        cosine = fine_cos * low_cos - fine_sin * low_sin
        sine = fine_sin * low_cos + fine_cos * low_sin
        real = base_real * cosine - base_imag * sine
        imag = base_real * sine + base_imag * cosine
        both = [part.reshape(BINS, 1, BINS, 128) for part in (real, imag)]
        both = jnp.concatenate(both, axis=1).reshape(BINS, 2 * BINS, 128)
        out[place : place + BINS] = both.astype(BF)

    band_products(table, upper, lower, sink)


def spectra_call(kernel, operands):
    vmem = pl.BlockSpec(memory_space=pltpu.VMEM)
    return pl.pallas_call(
        kernel,
        out_shape=jax.ShapeDtypeStruct((SHARES, 2 * BINS, 128), BF),
        in_specs=[vmem] * len(operands),
        out_specs=vmem,
        scratch_shapes=[pltpu.VMEM((9, 128, 2 * SPAN), BF)] * 2,
        compiler_params=pltpu.CompilerParams(vmem_limit_bytes=12 * 2**20),
    )(*operands)


def forward_spectra(records, following):
    return spectra_call(forward_kernel, (records, following, jnp.asarray(band_table())))


def bank_spectra(waveforms, lags, live):
    return spectra_call(bank_kernel, (waveforms, lags, live, jnp.asarray(band_table())))


def swap_blocks(parts, lane):
    count = len(parts)
    size = 128 // count
    step = count // 2
    while step:
        low = (lane // (size * step)) % 2 == 0
        fresh = list(parts)
        for i in range(count):
            if i & step:
                continue
            j = i + step
            fresh[i] = jnp.where(low, parts[i], pltpu.roll(parts[j], size * step, 1))
            fresh[j] = jnp.where(low, pltpu.roll(parts[i], 128 - size * step, 1), parts[j])
        parts = fresh
        step //= 2
    return parts


def turned(unit, block):
    return lax.dot_general(unit[...], block, ROTATED, preferred_element_type=F32)


def weights_kernel(chunks, bank, spread, unit, weights, live, count, compact):
    for g in range(16):
        block = jnp.concatenate([bank[g * 8 + i] for i in range(8)], axis=0)
        compact[128 * g : 128 * g + 128, :] = turned(unit, block).astype(BF)

    def expand(g, position):
        rows = pl.ds(pl.multiple_of(256 * g, 256), 256)
        for i in range(4):
            wide = jnp.dot(compact[rows, :], spread[i], preferred_element_type=F32)
            for half in range(2):
                for j in range(2):
                    first = ((2 * g + half) * 8 + 2 * i + j) * 16
                    part = wide[128 * half : 128 * half + 128, 128 * j : 128 * j + 128]
                    weights[pl.ds(first, 16)] = part.reshape(16, 8, 128)
        for i in range(64):
            t = g * 64 + i
            for s in range(4):
                live[position + s] = t * 4 + s
            position = position + chunks[t]
        return position

    total = lax.fori_loop(0, 8, expand, 0)
    for s in range(UNROLL):
        live[total + s] = 2048
    weights[2048] = jnp.zeros((8, 128), F32)
    count[0] = total


def correlate_kernel(places, live, count, own, other, weights, unit, out, table, sums, place, landed):
    copy = pltpu.make_async_copy(places, place, landed)
    copy.start()
    lane = lax.broadcasted_iota(jnp.int32, (128, 128), 1)
    is_real = (lane // BINS) % 2 == 0
    for half, source in enumerate((own, other)):
        for y in range(4):
            start = half * 512 + y * 128
            for s in range(4):
                tiles = [source[(8 * s + i) * 4 + y] for i in range(8)]
                block = jnp.concatenate(tiles, axis=0)
                value = turned(unit, block)
                table[start : start + 128, s, :] = value
                ahead, behind = pltpu.roll(value, 128 - BINS, 1), pltpu.roll(value, BINS, 1)
                table[start : start + 128, 4 + s, :] = jnp.where(is_real, ahead, behind)
    sums[...] = jnp.zeros_like(sums)
    copy.wait()

    def some_chunks(step, carry):
        for i in range(UNROLL):
            chunk = live[step * UNROLL + i]
            tile = weights[chunk]
            totals = [None, None]
            for u in range(8):
                row = table_rows(table, place[chunk * 8 + u])
                term = row * tile[u : u + 1]
                totals[u % 2] = term if u < 2 else totals[u % 2] + term
            t = lax.shift_right_logical(chunk, 2)
            sums[t] = sums[t] + (totals[0] + totals[1])
        return carry

    lax.fori_loop(0, lax.div(count[0] + UNROLL - 1, UNROLL), some_chunks, 0)

    lane = lax.broadcasted_iota(jnp.int32, (128, 128), 1)
    is_real = (lane // BINS) % 2 == 0
    for g in range(4):
        for y in range(4):
            first = sums[g * 128 : (g + 1) * 128, y, :]
            second = sums[g * 128 : (g + 1) * 128, 4 + y, :]
            real = first - pltpu.roll(first, 128 - BINS, 1)
            imag = second + pltpu.roll(second, BINS, 1)
            total = turned(unit, jnp.where(is_real, real, imag).astype(BF)).astype(BF)
            parts = [total[16 * i : 16 * (i + 1)] for i in range(8)]
            for i, part in enumerate(swap_blocks(parts, lane[:16])):
                out[(8 * g + i) * 4 + y] = part


def table_rows(table, first):
    rows = table.reshape(8192, 128)
    return rows[pl.ds(pl.multiple_of(first, 8), 8)]


def spread_table():
    lane = np.arange(128)
    one = np.zeros((2, BINS, 128))
    for part in range(2):
        one[part, lane % BINS, lane] = (lane // BINS) % 2 == part
    one = one.reshape(2 * BINS, 128)
    table = np.zeros((4, 8, 2 * BINS, 2, 128))
    for share in range(8):
        table[share // 2, share, :, share % 2] = one
    return table.reshape(4, 128, 256).astype(BF)


def correlate(place, chunks, own, other, bank):
    vmem = pl.BlockSpec(memory_space=pltpu.VMEM)
    smem = pl.BlockSpec(memory_space=pltpu.SMEM)
    unit = jnp.eye(128, dtype=BF)
    weights, live, count = pl.pallas_call(
        weights_kernel,
        out_shape=(
            jax.ShapeDtypeStruct((2049, 8, 128), F32),
            jax.ShapeDtypeStruct((2048 + 2 * UNROLL,), jnp.int32),
            jax.ShapeDtypeStruct((1,), jnp.int32),
        ),
        in_specs=[smem, vmem, vmem, vmem],
        out_specs=(vmem, smem, smem),
        scratch_shapes=[pltpu.VMEM((2048, 128), BF)],
        compiler_params=pltpu.CompilerParams(vmem_limit_bytes=14 * 2**20),
        cost_estimate=pl.CostEstimate(flops=2**29, bytes_accessed=10**7, transcendentals=0),
    )(chunks, bank, jnp.asarray(spread_table()), unit)
    correlated = pl.pallas_call(
        correlate_kernel,
        out_shape=jax.ShapeDtypeStruct((SHARES, 16, 128), BF),
        in_specs=[pl.BlockSpec(memory_space=pl.ANY), smem, smem, vmem, vmem, vmem, vmem],
        out_specs=vmem,
        scratch_shapes=[
            pltpu.VMEM((1024, 8, 128), F32),
            pltpu.VMEM((513, 8, 128), F32),
            pltpu.SMEM(place.shape, jnp.int32),
            pltpu.SemaphoreType.DMA,
        ],
        compiler_params=pltpu.CompilerParams(vmem_limit_bytes=18 * 2**20),
    )(place, live, count, own, other, weights, unit)
    return correlated


def on_device(records, waveforms, slot_channels, slot_counts, slot_lags):
    core = lax.axis_index("c")
    quarter = lax.axis_index("y")
    following = lax.ppermute(records[:, : NFFT - HOP], ("z", "x"), [(i, i - 1) for i in range(1, 32)])

    first = core * 16 + quarter * 4
    lags = lax.dynamic_slice_in_dim(slot_lags, first, 4, 0).reshape(1, 128)
    counts = lax.dynamic_slice_in_dim(slot_counts, first, 4, 0)
    channels = lax.dynamic_slice_in_dim(slot_channels, first, 4, 0).reshape(128)
    live = (jnp.arange(SLOTS, dtype=jnp.int32)[None] < counts[:, None]).reshape(128)
    waves = lax.dynamic_slice_in_dim(waveforms, first, 4, 0)
    bank = bank_spectra(waves, lags, live.astype(F32)[None])
    digits = jnp.stack([channels // 32 + jnp.where(live, 32, 0), channels % 32]).astype(BF)
    digits = jnp.broadcast_to(digits, (SHARES, 1, 2, 128))

    rows = jnp.concatenate([bank.reshape(SHARES, 8, 2, 128), digits], axis=1)
    shares = lax.optimization_barrier(jnp.pad(rows, ((0, 0), (8, 0), (0, 0), (0, 0))))
    spectra = forward_spectra(records, following).reshape(SHARES, 8, 2, 128)
    shares = lax.dynamic_update_slice(shares, spectra, (0, 0, 0, 0))
    shares = lax.all_to_all(shares, ("z", "x", "y"), split_axis=0, concat_axis=0, tiled=True)
    own = shares[:, :8].reshape(SHARES, 2 * BINS, 128)
    bank = shares[:, 8:16].reshape(SHARES, 2 * BINS, 128)
    other = lax.ppermute(own, "c", [(0, 1), (1, 0)])
    digits = shares[:, 16].astype(jnp.int32)
    channels = (digits[:, 0] % 32) * 32 + digits[:, 1]
    home = channels // 128
    place = ((home % 2) ^ core) * 512 + (home // 2) * 128 + channels % 128
    place = jnp.pad(8 * place.reshape(512 * SLOTS), (0, 128))
    counts = jnp.sum((digits[:, 0] // 32).reshape(512, SLOTS), axis=1)
    chunks = (counts + 7) // 8
    correlated = correlate(place, chunks, own, other, bank)
    here = lax.all_to_all(correlated, ("z", "x", "y"), split_axis=0, concat_axis=0, tiled=True)
    there = lax.ppermute(here, "c", [(0, 1), (1, 0)])
    traces, energy = inverse_traces(here, there, core)
    energy = energy + lax.ppermute(energy, "c", [(0, 1), (1, 0)])
    shifts = [[(i, (i + d) % 4) for i in range(4)] for d in range(1, 4)]
    energy = sum((lax.ppermute(energy, "y", shift) for shift in shifts), energy)
    return traces * lax.rsqrt(energy / (32 * HOP) + EPS).reshape(32, 1)


def solution(mesh):
    fine = Mesh(mesh.devices.reshape(8, 4, 4, 2), ("z", "x", "y", "c"))
    tmpl, chan = ("z", "x"), ("y", "c")
    in_specs = (P(chan, tmpl), P(tmpl, None, None), P(tmpl, None), P(tmpl), P(tmpl, None))
    return jax.shard_map(
        on_device, mesh=fine, in_specs=in_specs, out_specs=P(tmpl, chan), check_vma=False
    )
```
